32 devices in a mesh: dp: 2 (over core), seq: 4 (over z), head: 4 (over y, x).
Axes of the slice: x: 2, y: 2, z: 4, core: 2. Of those that a mesh axis runs over, the one named last changes fastest.
Arguments:
- tokens: float32 [2, 2048, 1536], P('dp', 'seq'), may hold values from -6 to 6
- cotangent: float32 [2, 2048, 1536], P('dp', 'seq'), may hold values from -6 to 6
- pre_gain: float32 [2, 1536], replicated, may hold values from 0.5 to 1.5
- gate_weight: float32 [2, 1536, 3072], P(None, None, 'head'), may hold values from -0.15625 to 0.15625
- inner_weight: float32 [2, 1536, 3072], P(None, None, 'head'), may hold values from -0.15625 to 0.15625
- state_weight: float32 [2, 1536, 256], P(None, None, 'head'), may hold values from -0.15625 to 0.15625
- step_weight: float32 [2, 1536, 48], P(None, None, 'head'), may hold values from -0.15625 to 0.15625
- filter_inner: float32 [2, 4, 3072], P(None, None, 'head'), may hold values from -3 to 3
- filter_inner_bias: float32 [2, 3072], P(None, 'head'), may hold values from -3 to 3
- filter_state: float32 [2, 4, 256], P(None, None, 'head'), may hold values from -3 to 3
- filter_state_bias: float32 [2, 256], P(None, 'head'), may hold values from -3 to 3
- step_bias: float32 [2, 48], P(None, 'head'), may hold values from -4.5 to -3.5
- log_rate: float32 [2, 48], P(None, 'head'), may hold values from -9 to 1, as said below
- skip_gain: float32 [2, 48], P(None, 'head'), may hold values from 0.5 to 1.5
- norm_gain: float32 [2, 3072], P(None, 'head'), may hold values from 0.5 to 1.5
- out_weight: float32 [2, 1536, 3072], P(None, None, 'head'), may hold values from -0.109375 to 0.109375
Outputs:
- mixed: float32 [2, 2048, 1536], P('dp', 'seq')
- token_grad: float32 [2, 2048, 1536], P('dp', 'seq')
- grad_pre_gain: float32 [2, 1536], replicated
- grad_gate_weight: float32 [2, 1536, 3072], P(None, 'seq', 'head')
- grad_inner_weight: float32 [2, 1536, 3072], P(None, 'seq', 'head')
- grad_state_weight: float32 [2, 1536, 256], P(None, 'seq', 'head')
- grad_step_weight: float32 [2, 1536, 48], P(None, 'seq', 'head')
- grad_filter_inner: float32 [2, 4, 3072], P(None, None, 'head')
- grad_filter_inner_bias: float32 [2, 3072], P(None, 'head')
- grad_filter_state: float32 [2, 4, 256], P(None, None, 'head')
- grad_filter_state_bias: float32 [2, 256], P(None, 'head')
- grad_step_bias: float32 [2, 48], P(None, 'head')
- grad_log_rate: float32 [2, 48], P(None, 'head')
- grad_skip_gain: float32 [2, 48], P(None, 'head')
- grad_norm_gain: float32 [2, 3072], P(None, 'head')
- grad_out_weight: float32 [2, 1536, 3072], P(None, 'seq', 'head')
The draws below stay inside these ranges and needn't reach their ends.
Inputs may be any that keep to these rules, and one draw needn't show every extreme that they name: log_rate holds logarithms of the heads' decay rates.
All inputs are finite; a program needn't handle non-finite values.
Results may differ from the reference program's by a relative error of at most 0.0003.
Values sent between devices are 32-bit elements; how exact they have to be, the bound alone decides.
No kernel may reach another device: no remote copies, remote signals or barrier semaphores. Data moves between devices by JAX's collectives and lax.ppermute only.
A program may use at most 384 MiB of HBM per device.

```python
import jax
import jax.numpy as jnp
from jax import lax

D = 1536
INNER = 3072
HEADS = 48
HEAD_DIM = 64
STATE = 128
KERNEL = 4
GROUP = 256
LAYERS = 2
SEQS = 2
SEQLEN = 2048


def draw_log_rate(key, part):
    key = jax.random.fold_in(key, 11)
    pick_key, slow_key, fast_key = jax.random.split(key, 3)
    shape = (LAYERS, HEADS)
    share = 0.5
    pick = jax.random.uniform(pick_key, shape, jnp.float32)
    slow = jax.random.uniform(slow_key, shape, jnp.float32, jnp.log(10.0 / SEQLEN), jnp.log(60.0 / SEQLEN))
    fast = jax.random.uniform(fast_key, shape, jnp.float32, jnp.log(0.05), jnp.log(1.25))
    return jnp.where(pick < share, slow, fast).astype(jnp.float32)


def level_of(own_key, extent, shards, least, top_value):
    gain, own = 1.0, jax.random.fold_in(own_key, 6)
    for dim, shards_of in shards:
        heights = jnp.exp(jax.random.uniform(jax.random.fold_in(own, dim), (shards_of,), jnp.float32, least / len(shards), top_value / len(shards)))
        gain = gain * jnp.repeat(heights, extent[dim] // shards_of).reshape([-1 if axis == dim else 1 for axis in range(len(extent))])
    return gain


def centred(key, dims, scale, bound, shards=(), dtype=jnp.bfloat16):
    result = jax.random.normal(key, dims, jnp.float32) * scale
    if len(shards) > 0:
        result = level_of(key, dims, shards, -0.22, 0.18) * result
    return jnp.clip(result, min=-bound, max=bound).astype(dtype)


def setup_inputs(seed: int = 0) -> dict:
    key_of = jax.random.split(jax.random.key(seed), 17)
    tokens = centred(key_of[0], (SEQS, SEQLEN, D), 1.0, 6.0, ((0, 2), (1, 4)), jnp.float32)
    cotangent = centred(key_of[1], (SEQS, SEQLEN, D), 1.0, 6.0, ((0, 2), (1, 4)), jnp.float32)
    pre_gain = jnp.clip(1.0 + 0.1 * jax.random.normal(key_of[2], (LAYERS, D), jnp.float32), 0.5, 1.5)
    gate_weight = centred(key_of[3], (LAYERS, D, INNER), D ** -0.5, 0.15625, ((2, 4),), jnp.float32)
    inner_weight = centred(key_of[4], (LAYERS, D, INNER), D ** -0.5, 0.15625, ((2, 4),), jnp.float32)
    state_weight = centred(key_of[5], (LAYERS, D, 2 * STATE), D ** -0.5, 0.15625, ((2, 4),), jnp.float32)
    step_weight = centred(key_of[6], (LAYERS, D, HEADS), D ** -0.5, 0.15625, ((2, 4),), jnp.float32)
    filter_inner = centred(key_of[7], (LAYERS, KERNEL, INNER), KERNEL ** -0.5, 3.0, ((2, 4),), jnp.float32)
    filter_inner_bias = centred(key_of[8], (LAYERS, INNER), 0.5, 3.0, ((1, 4),), jnp.float32)
    filter_state = centred(key_of[9], (LAYERS, KERNEL, 2 * STATE), KERNEL ** -0.5, 3.0, ((2, 4),), jnp.float32)
    filter_state_bias = centred(key_of[10], (LAYERS, 2 * STATE), 0.5, 3.0, ((1, 4),), jnp.float32)
    step_bias = jnp.clip(-4.5 + 1.0 * jax.random.uniform(key_of[11], (LAYERS, HEADS), jnp.float32) ** level_of(key_of[11], (LAYERS, HEADS), ((1, 4),), -0.2, 0.2), -4.5, -3.5)
    log_rate = draw_log_rate(jax.random.fold_in(key_of[16], 71), 0)
    skip_gain = jnp.clip(0.5 + 1.0 * jax.random.uniform(key_of[13], (LAYERS, HEADS), jnp.float32) ** level_of(key_of[13], (LAYERS, HEADS), ((1, 4),), -0.2, 0.2), 0.5, 1.5)
    norm_gain = jnp.clip(1.0 + 0.1 * jax.random.normal(key_of[14], (LAYERS, INNER), jnp.float32), 0.5, 1.5)
    out_weight = centred(key_of[15], (LAYERS, D, INNER), INNER ** -0.5, 0.109375, ((2, 4),), jnp.float32)
    return {"tokens": tokens, "cotangent": cotangent, "pre_gain": pre_gain, "gate_weight": gate_weight, "inner_weight": inner_weight, "state_weight": state_weight, "step_weight": step_weight, "filter_inner": filter_inner, "filter_inner_bias": filter_inner_bias, "filter_state": filter_state, "filter_state_bias": filter_state_bias, "step_bias": step_bias, "log_rate": log_rate, "skip_gain": skip_gain, "norm_gain": norm_gain, "out_weight": out_weight}


epsilon = 1e-05
highest = lax.Precision.HIGHEST

def matmul(left, right):
    return jnp.dot(left, right, precision=highest)

def block_step(state, block):
    values, steps, rates, inputs_b, outputs_c = block
    within = jnp.cumsum(rates, axis=0)
    across = within.T
    length = rates.shape[0]
    lower = jnp.arange(length)[:, None] >= jnp.arange(length)[None, :]
    spread = jnp.where(lower[None], across[:, :, None] - across[:, None, :], 0.0)
    decay = jnp.where(lower[None], jnp.exp(spread), 0.0)
    intersection = matmul(outputs_c, inputs_b.T)
    mixing = decay * intersection[None] * steps.T[:, None, :]
    local = jnp.einsum('hij,jhp->ihp', mixing, values, precision=highest)
    carried = jnp.exp(within)[:, :, None] * jnp.einsum('in,hpn->ihp', outputs_c, state, precision=highest)
    final = within[-1]
    weights = jnp.exp(final[None, :] - within) * steps
    fresh = jnp.einsum('jhp,jn->hpn', weights[:, :, None] * values, inputs_b, precision=highest)
    new_state = jnp.exp(final)[:, None, None] * state + fresh
    return (new_state, local + carried)

def causal_filter(signal, weight, bias):
    length = signal.shape[0]
    padded = jnp.concatenate([jnp.zeros((weight.shape[0] - 1, signal.shape[1]), jnp.float32), signal], axis=0)
    total = bias[None, :] + weight[0][None, :] * padded[0:length]
    for offset in range(1, weight.shape[0]):
        total = total + weight[offset][None, :] * padded[offset:offset + length]
    return jax.nn.silu(total)

def run_layer(current, pre_gain, gate_weight, inner_weight, state_weight, step_weight, filter_inner, filter_inner_bias, filter_state, filter_state_bias, step_bias, log_rate, skip_gain, norm_gain, out_weight):
    length = current.shape[0]
    normed = current * lax.rsqrt(lax.optimization_barrier(jnp.mean(current * current, axis=-1, keepdims=True)) + epsilon) * pre_gain[None, :]
    gate = matmul(normed, gate_weight)
    inner_pre = matmul(normed, inner_weight)
    state_pre = matmul(normed, state_weight)
    step_raw = matmul(normed, step_weight)
    inner_conv = causal_filter(inner_pre, filter_inner, filter_inner_bias)
    state_conv = causal_filter(state_pre, filter_state, filter_state_bias)
    values = inner_conv.reshape(length, HEADS, HEAD_DIM)
    steps = jax.nn.softplus(step_raw + step_bias[None, :])
    rates = -jnp.exp(log_rate)[None, :] * steps
    blocks = length // GROUP

    def split(array):
        return array.reshape((blocks, GROUP) + array.shape[1:])
    start = jnp.zeros((HEADS, HEAD_DIM, STATE), jnp.float32)
    final_state, output = lax.scan(jax.checkpoint(block_step), start, (split(values), split(steps), split(rates), split(state_conv[:, :STATE]), split(state_conv[:, STATE:])))
    mixer = output.reshape(values.shape) + skip_gain[None, :, None] * values
    gated = mixer.reshape(length, INNER) * jax.nn.silu(gate)
    scaled = gated * lax.rsqrt(lax.optimization_barrier(jnp.mean(gated * gated, axis=-1, keepdims=True)) + epsilon) * norm_gain[None, :]
    return current + jnp.dot(scaled, out_weight.T, precision=highest)

def forward(tokens, *weight_stacks):
    current = tokens
    for layer in range(LAYERS):
        layer_weights = [stack[layer] for stack in weight_stacks]
        current = jax.vmap(run_layer, in_axes=(0,) + (None,) * len(layer_weights))(current, *layer_weights)
    return current

def reference(tokens, cotangent, pre_gain, gate_weight, inner_weight, state_weight, step_weight, filter_inner, filter_inner_bias, filter_state, filter_state_bias, step_bias, log_rate, skip_gain, norm_gain, out_weight):
    mixed, backward = jax.vjp(forward, tokens, pre_gain, gate_weight, inner_weight, state_weight, step_weight, filter_inner, filter_inner_bias, filter_state, filter_state_bias, step_bias, log_rate, skip_gain, norm_gain, out_weight)
    grads = backward(cotangent)
    return (mixed, grads[0], grads[1], grads[2], grads[3], grads[4], grads[5], grads[6], grads[7], grads[8], grads[9], grads[10], grads[11], grads[12], grads[13], grads[14])
```

```python
import functools

import jax
import jax.numpy as jnp
from jax import lax
from jax.experimental import pallas as pl
from jax.experimental.pallas import tpu as pltpu
from jax.sharding import PartitionSpec as P

INNER = 3072
CHUNK = 128
LANES = 128
PAD = 8
epsilon = 1e-05
HIGH = lax.Precision.HIGH
HIGHEST = lax.Precision.HIGHEST
NEG = -1e30
F32 = jnp.float32


def power_of_two(n):
    return n & (n - 1) == 0


def exchanged(value, axis, distance):
    n = lax.axis_size(axis)
    return lax.ppermute(value, axis, [(i, i ^ distance) for i in range(n)])


def shifted(value, axis, step):
    n = lax.axis_size(axis)
    pairs = [(i, i + step) for i in range(n) if 0 <= i + step < n]
    return lax.ppermute(value, axis, pairs)


def distances(axis):
    n = lax.axis_size(axis)
    return [1 << k for k in range(n.bit_length() - 1)]


def bit_of(axis, distance):
    return (lax.axis_index(axis) // distance) % 2


def small_sum(value, axis):
    if not power_of_two(lax.axis_size(axis)):
        return lax.psum(value, axis)
    for distance in distances(axis):
        value = value + exchanged(value, axis, distance)
    return value


def half(value, which, dim=0):
    size = value.shape[dim] // 2
    return lax.dynamic_slice_in_dim(value, which * size, size, dim)


def joined(mine, other, axis, distance, dim=0):
    first = bit_of(axis, distance) == 0
    return jnp.concatenate(
        [jnp.where(first, mine, other), jnp.where(first, other, mine)], axis=dim
    )


def scatter_sum(value, axis, order):
    offset = 0
    for distance in order:
        bit = bit_of(axis, distance)
        size = value.shape[0] // 2
        value = half(value, bit) + exchanged(half(value, 1 - bit), axis, distance)
        offset = offset + bit * size
    return value, offset


def gather_back(value, axis, order, dim=0):
    for distance in order[::-1]:
        value = joined(value, exchanged(value, axis, distance), axis, distance, dim)
    return value


def head_sum(partial, finish):
    order = distances("head")
    rows = partial.shape[0] // 2
    parts = []
    for number, way in enumerate((order, order[::-1])):
        mine, offset = scatter_sum(partial[number * rows : (number + 1) * rows], "head", way)
        parts.append((finish(mine, number * rows + offset), way))
    return jnp.concatenate([gather_back(mine, "head", way) for mine, way in parts], axis=0)


def line_scatter_sum(value, axis):
    n = lax.axis_size(axis)
    if n > 4:
        return lax.psum_scatter(value, axis, scatter_dimension=0, tiled=True)
    rows = value.shape[0] // n
    place = lax.axis_index(axis)

    def shard(number):
        return lax.dynamic_slice_in_dim(value, jnp.clip(number, 0, n - 1) * rows, rows, 0)

    up = shard(n + place - 1)
    down = shard(place + 1 - n)
    for step in range(1, n):
        got_up = lax.ppermute(up, axis, [(z, z + 1) for z in range(step)])
        got_down = lax.ppermute(down, axis, [(n - 1 - z, n - 2 - z) for z in range(step)])
        if step < n - 1:
            up = got_up + shard(n + place - step - 1)
            down = got_down + shard(place + step + 1 - n)
        else:
            return got_up + got_down + shard(place)
    return value


def state_before(local, decay, reverse):
    n = lax.axis_size("seq")
    state = jnp.zeros_like(local)
    for hop in range(n - 1):
        source, target = (n - 1 - hop, n - 2 - hop) if reverse else (hop, hop + 1)
        state = state + lax.ppermute(decay * state + local, "seq", [(source, target)])
    return state


def call(kernel, outs, scratch, flops, *args):
    shapes = [jax.ShapeDtypeStruct(shape, F32) for shape in outs]
    size = 4 * sum(a.size for a in args) + 4 * sum(s.size for s in shapes)
    return pl.pallas_call(
        kernel,
        out_shape=shapes,
        in_specs=[pl.BlockSpec(memory_space=pltpu.VMEM)] * len(args),
        out_specs=[pl.BlockSpec(memory_space=pltpu.VMEM)] * len(outs),
        scratch_shapes=scratch,
        compiler_params=pltpu.CompilerParams(vmem_limit_bytes=40 * 1024 * 1024),
        cost_estimate=pl.CostEstimate(flops=flops, bytes_accessed=size, transcendentals=0),
    )(*args)


def dot(left, right, dims=((1,), (0,)), precision=HIGH):
    return lax.dot_general(
        left, right, (dims, ((), ())), precision=precision, preferred_element_type=F32
    )


NT = ((1,), (1,))


def sigmoid(value):
    return 1.0 / (1.0 + jnp.exp(-value))


def spread_heads(columns, tile, width):
    each = LANES // width
    lane = lax.broadcasted_iota(jnp.int32, (columns.shape[0], LANES), 1)
    result = columns[:, tile * each : tile * each + 1]
    for k in range(1, each):
        result = jnp.where(lane < k * width, result, columns[:, tile * each + k : tile * each + k + 1])
    return jnp.broadcast_to(result, (columns.shape[0], LANES))


def head_rows(row, width, total):
    tiles = [spread_heads(row, tile, width) for tile in range(total // LANES)]
    return jnp.concatenate(tiles, axis=1)


def filter_tile(scratch, taps, start, rows, cols):
    block = scratch[pl.ds(start, rows + PAD), cols]
    total = taps[4:5, cols] + taps[3:4, cols] * block[PAD:]
    for back in range(1, 4):
        total = total + taps[3 - back : 4 - back, cols] * pltpu.roll(block, back, 0)[PAD:]
    return total


def start_kernel(
    width, ip, ib, sp, sb, ti, ts, hp, v_out, bc_out, dsi, dss, dt_out, cum_out, cumt_out, fresh, local, chdec, padi, pads
):
    length, inner = ip.shape
    states = ts.shape[1]
    n = states // 2
    padi[0:PAD, :] = ib[...]
    padi[PAD:, :] = ip[...]
    pads[0:PAD, :] = sb[...]
    pads[PAD:, :] = sp[:, :states]
    rows = 64

    def filtered(step, _):
        start = pl.multiple_of(step * rows, rows)
        for scratch, taps, out, slope, size in (
            (padi, ti, v_out, dsi, inner),
            (pads, ts, bc_out, dss, states),
        ):
            for tile in range(size // LANES):
                cols = slice(tile * LANES, (tile + 1) * LANES)
                total = filter_tile(scratch, taps, start, rows, cols)
                gate = sigmoid(total)
                value = total * gate
                out[pl.ds(start, rows), cols] = value
                slope[pl.ds(start, rows), cols] = gate + value * (1.0 - gate)
        return 0

    lax.fori_loop(0, length // rows, filtered, 0)
    raw = sp[:, states:] + hp[0:1, :]
    dt = jnp.maximum(raw, 0.0) + jnp.log1p(jnp.exp(-jnp.abs(raw)))
    dt_out[...] = dt
    rate = -jnp.exp(hp[1:2, :]) * dt
    ones = (
        lax.broadcasted_iota(jnp.int32, (CHUNK, CHUNK), 0)
        >= lax.broadcasted_iota(jnp.int32, (CHUNK, CHUNK), 1)
    ).astype(F32)
    chunks = length // CHUNK
    for c in range(chunks):
        span = slice(c * CHUNK, (c + 1) * CHUNK)
        cum = dot(ones, rate[span], precision=HIGHEST)
        cum_out[span, :] = cum
        cumt_out[:, span] = cum.T[: cumt_out.shape[0]]
        last = cum[CHUNK - 1 : CHUNK, :]
        weight = jnp.exp(last - cum) * dt[span]
        maps = bc_out[span, :n].T
        chdec[c : c + 1, :] = head_rows(jnp.exp(last), width, inner)
        for tile in range(inner // LANES):
            cols = slice(tile * LANES, (tile + 1) * LANES)
            weighted = v_out[span, cols] * spread_heads(weight, tile, width)
            fresh[c, :, cols] = dot(maps, weighted)
    state = fresh[0]
    decay = chdec[0:1, :]
    for c in range(1, chunks):
        state = chdec[c : c + 1, :] * state + fresh[c]
        decay = decay * chdec[c : c + 1, :]
    local[...] = state
    chdec[chunks : chunks + 1, :] = decay


def inner_kernel(width, v, bc, dt, cum, cumt, hp, out):
    length, inner = v.shape
    n = bc.shape[1] // 2
    each = LANES // width
    lane = lax.broadcasted_iota(jnp.int32, (CHUNK, LANES), 1)
    lower = lax.broadcasted_iota(jnp.int32, (CHUNK, CHUNK), 0) >= lax.broadcasted_iota(
        jnp.int32, (CHUNK, CHUNK), 1
    )
    for c in range(length // CHUNK):
        span = slice(c * CHUNK, (c + 1) * CHUNK)
        meet = dot(bc[span, n:], bc[span, :n], NT)
        for tile in range(inner // LANES):
            cols = slice(tile * LANES, (tile + 1) * LANES)
            values = v[span, cols]
            stepped = values * spread_heads(dt[span, :], tile, width)
            result = None
            for k in range(each):
                head = tile * each + k
                spread = cum[span, head : head + 1] - cumt[head : head + 1, span]
                mixing = jnp.exp(jnp.where(lower, spread, NEG)) * meet
                part = dot(mixing, stepped)
                result = part if k == 0 else jnp.where(lane < k * width, result, part)
            skip = spread_heads(hp[2:3, :], tile, width)
            out[span, cols] = result + skip * values


def gate_kernel(width, yd, bc, cum, fresh, chdec, entering, gate, gain, y_out, gn_out, states, squares):
    length, inner = yd.shape
    n = bc.shape[1] // 2
    ones = jnp.ones((PAD, LANES), F32)
    for c in range(length // CHUNK):
        span = slice(c * CHUNK, (c + 1) * CHUNK)
        if c == 0:
            states[0] = entering[...]
        else:
            states[c] = chdec[c - 1 : c, :] * states[c - 1] + fresh[c - 1]
        carried = jnp.exp(cum[span, :])
        maps = bc[span, n:]
        total = None
        for tile in range(inner // LANES):
            cols = slice(tile * LANES, (tile + 1) * LANES)
            y = yd[span, cols] + spread_heads(carried, tile, width) * dot(maps, states[c, :, cols])
            y_out[span, cols] = y
            g = gate[span, cols]
            gated = y * (g * sigmoid(g))
            gn_out[span, cols] = gated * gain[0:1, cols]
            total = gated * gated if tile == 0 else total + gated * gated
        squares[:, span] = dot(ones, total, NT, HIGHEST)


def open_kernel(
    width, q, y, gate, gain, scale, slope, bc, cum, chdec, dy_out, dgate, u_out, dgain, adjoint, local
):
    length, inner = q.shape
    n = bc.shape[1] // 2
    chunks = length // CHUNK
    for c in range(chunks):
        span = slice(c * CHUNK, (c + 1) * CHUNK)
        carried = jnp.exp(cum[span, :])
        maps = bc[span, n:].T
        s = scale[span, :]
        t = slope[span, :]
        for tile in range(inner // LANES):
            cols = slice(tile * LANES, (tile + 1) * LANES)
            g = gate[span, cols]
            soft = sigmoid(g)
            silu = g * soft
            out = y[span, cols]
            gated = out * silu
            grad = q[span, cols]
            scaled = gated * s
            u_out[span, cols] = scaled * gain[0:1, cols]
            part = (grad * scaled).reshape(CHUNK // PAD, PAD, LANES).sum(axis=0)
            dgain[:, cols] = part if c == 0 else dgain[:, cols] + part
            dgated = s * (grad * gain[0:1, cols]) - t * gated
            dgate[span, cols] = dgated * out * (soft + silu * (1.0 - soft))
            dy = dgated * silu
            dy_out[span, cols] = dy
            adjoint[c, :, cols] = dot(maps, dy * spread_heads(carried, tile, width))
    state = adjoint[chunks - 1]
    for c in range(chunks - 2, -1, -1):
        state = adjoint[c] + chdec[c : c + 1, :] * state
    local[...] = state


def back_kernel(width, dy, v, bc, dt, cum, cumt, states, du, dbc, gram):
    length, inner = v.shape
    n = bc.shape[1] // 2
    each = LANES // width
    lane = lax.broadcasted_iota(jnp.int32, (CHUNK, LANES), 1)
    upper = lax.broadcasted_iota(jnp.int32, (CHUNK, CHUNK), 0) <= lax.broadcasted_iota(
        jnp.int32, (CHUNK, CHUNK), 1
    )
    for c in range(length // CHUNK):
        span = slice(c * CHUNK, (c + 1) * CHUNK)
        inputs, outputs = bc[span, :n], bc[span, n:]
        meet = dot(inputs, outputs, NT)
        carried = jnp.exp(cum[span, :])
        grad_out = None
        for tile in range(inner // LANES):
            cols = slice(tile * LANES, (tile + 1) * LANES)
            grad = dy[span, cols]
            stepped = v[span, cols] * spread_heads(dt[span, :], tile, width)
            result = None
            for k in range(each):
                head = tile * each + k
                spread = cumt[head : head + 1, span] - cum[span, head : head + 1]
                decay = jnp.exp(jnp.where(upper, spread, NEG))
                part = dot(decay * meet, grad)
                result = part if k == 0 else jnp.where(lane < k * width, result, part)
                own = (lane >= k * width) & (lane < (k + 1) * width)
                cross = decay * dot(jnp.where(own, stepped, 0.0), grad, NT)
                first = tile == 0 and k == 0
                gram[...] = cross if first else gram[...] + cross
            du[span, cols] = result
            part = dot(grad * spread_heads(carried, tile, width), states[c, :, cols], NT)
            grad_out = part if tile == 0 else grad_out + part
        total = gram[...]
        dbc[span, :n] = dot(total, outputs)
        dbc[span, n:] = grad_out + dot(total.T, inputs)


def head_totals(product, width):
    each = LANES // width
    lane = lax.broadcasted_iota(jnp.int32, product.shape, 1)
    result = []
    for k in range(each):
        own = (lane >= k * width) & (lane < (k + 1) * width)
        result.append(jnp.sum(jnp.where(own, product, 0.0), axis=1, keepdims=True))
    return result


def place_heads(columns, shape):
    lane = lax.broadcasted_iota(jnp.int32, shape, 1)
    result = jnp.zeros(shape, F32)
    for head, column in enumerate(columns):
        result = jnp.where(lane == head, column, result)
    return result


def close_kernel(
    width, dy, y, v, bc, dt, cum, sp, hp, du, dbc, dsi, dss, adjoint, chdec, fresh, states, later,
    dti, dts, dstep, rows, leaving,
):
    length, inner = v.shape
    n = bc.shape[1] // 2
    chunks = length // CHUNK
    heads_rate = -jnp.exp(hp[1:2, :])
    final = chdec[chunks - 1 : chunks, :] * states[chunks - 1] + fresh[chunks - 1]
    crossing = jnp.sum(final * later[...], axis=0, keepdims=True)
    columns = []
    for tile in range(inner // LANES):
        columns += head_totals(crossing[:, tile * LANES : (tile + 1) * LANES], width)
    running = place_heads(columns, (1, LANES))
    ones = (
        lax.broadcasted_iota(jnp.int32, (CHUNK, CHUNK), 0)
        <= lax.broadcasted_iota(jnp.int32, (CHUNK, CHUNK), 1)
    ).astype(F32)
    leaving[...] = later[...]
    rows[...] = jnp.zeros_like(rows)
    for c in range(chunks - 1, -1, -1):
        span = slice(c * CHUNK, (c + 1) * CHUNK)
        step = dt[span, :]
        cums = cum[span, :]
        fade = jnp.exp(cums[CHUNK - 1 : CHUNK, :] - cums)
        inputs = bc[span, :n]
        grad_in = dbc[span, :n]
        own, direct = [], []
        for tile in range(inner // LANES):
            cols = slice(tile * LANES, (tile + 1) * LANES)
            adj = leaving[:, cols]
            wide_fade = spread_heads(fade, tile, width)
            wide_step = spread_heads(step, tile, width)
            skip = spread_heads(hp[2:3, :], tile, width)
            values = v[span, cols]
            grad = dy[span, cols]
            dstepped = du[span, cols] + wide_fade * dot(inputs, adj)
            grad_in = grad_in + dot(wide_fade * wide_step * values, adj, NT)
            dti[span, cols] = (wide_step * dstepped + skip * grad) * dsi[span, cols]
            own += head_totals(grad * (y[span, cols] - skip * values), width)
            direct += head_totals(values * dstepped, width)
            part = (grad * values).reshape(CHUNK // PAD, PAD, LANES).sum(axis=0)
            rows[0:PAD, cols] = rows[0:PAD, cols] + part
            leaving[:, cols] = adjoint[c, :, cols] + chdec[c : c + 1, cols] * adj
        dts[span, :n] = grad_in * dss[span, :n]
        dts[span, n:] = dbc[span, n:] * dss[span, n:]
        direct = place_heads(direct, (CHUNK, LANES))
        dcum = place_heads(own, (CHUNK, LANES)) - step * direct
        drate = dot(ones, dcum, precision=HIGHEST) + running
        running = drate[0:1, :]
        dstep_value = direct + drate * heads_rate
        raw = sp[span, 2 * n :] + hp[0:1, :]
        grad_raw = dstep_value * sigmoid(raw)
        dstep[span, :] = grad_raw
        lanes = slice(0, LANES)
        rates = drate * heads_rate * step
        rows[PAD : 2 * PAD, lanes] = rows[PAD : 2 * PAD, lanes] + rates.reshape(
            CHUNK // PAD, PAD, LANES
        ).sum(axis=0)
        rows[2 * PAD : 3 * PAD, lanes] = rows[2 * PAD : 3 * PAD, lanes] + grad_raw.reshape(
            CHUNK // PAD, PAD, LANES
        ).sum(axis=0)


def filter_back_kernel(dti, hi, dts, hs, ip, ib, sp, sb, ti, ts, dip, dsp, ri, rs, padi, pads, padgi, padgs):
    length, inner = ip.shape
    states = dts.shape[1]
    padi[0:PAD, :] = ib[...]
    padi[PAD:, :] = ip[...]
    pads[0:PAD, :] = sb[...]
    pads[PAD:, :] = sp[:, :states]
    padgi[0:length, :] = dti[...]
    padgi[length:, :] = hi[...]
    padgs[0:length, :] = dts[...]
    padgs[length:, :] = hs[...]
    ri[...] = jnp.zeros_like(ri)
    rs[...] = jnp.zeros_like(rs)
    rows = 64

    def folded(value):
        return value.reshape(rows // PAD, PAD, LANES).sum(axis=0)

    def step(number, _):
        start = pl.multiple_of(number * rows, rows)
        for signal, grads, taps, out, sums, size in (
            (padi, padgi, ti, dip, ri, inner),
            (pads, padgs, ts, dsp, rs, states),
        ):
            for tile in range(size // LANES):
                cols = slice(tile * LANES, (tile + 1) * LANES)
                ahead = grads[pl.ds(start, rows + PAD), cols]
                grad = ahead[:rows]
                before = signal[pl.ds(start, rows + PAD), cols]
                total = taps[3:4, cols] * grad
                sums[3 * PAD : 4 * PAD, cols] = sums[3 * PAD : 4 * PAD, cols] + folded(grad * before[PAD:])
                sums[4 * PAD : 5 * PAD, cols] = sums[4 * PAD : 5 * PAD, cols] + folded(grad)
                for back in range(1, 4):
                    tap = 3 - back
                    total = total + taps[tap : tap + 1, cols] * pltpu.roll(ahead, rows + PAD - back, 0)[:rows]
                    place = slice(tap * PAD, (tap + 1) * PAD)
                    sums[place, cols] = sums[place, cols] + folded(
                        grad * pltpu.roll(before, back, 0)[PAD:]
                    )
                out[pl.ds(start, rows), cols] = total
        return 0

    lax.fori_loop(0, length // rows, step, 0)


def matmul(left, right, dims=((1,), (0,))):
    return lax.dot_general(left, right, (dims, ((), ())), precision=HIGH)


def padded_rows(rows, lanes):
    rows = jnp.concatenate(rows, axis=0)
    return jnp.pad(rows, ((0, PAD - rows.shape[0]), (0, lanes - rows.shape[1])))


def forward(current, w):
    length = current.shape[0]
    inner = w["inner"].shape[1]
    heads = w["heads"]
    width = inner // heads
    states = w["taps_s"].shape[1]
    n = states // 2
    chunks = length // CHUNK
    root = lax.rsqrt(jnp.mean(current * current, axis=-1, keepdims=True) + epsilon)
    normed = current * root * w["pre_gain"][None, :]
    ip = matmul(normed, w["inner"])
    sp = matmul(normed, w["maps"])
    border = shifted(
        jnp.concatenate([ip[length - PAD :], sp[length - PAD :, :states]], axis=1), "seq", 1
    )
    ib, sb = border[:, :inner], border[:, inner:]
    gate = matmul(normed, w["gate"])
    v, bc, dsi, dss, dt, cum, cumt, fresh, local, chdec = call(
        functools.partial(start_kernel, width),
        [
            (length, inner),
            (length, states),
            (length, inner),
            (length, states),
            (length, LANES),
            (length, LANES),
            (16, length),
            (chunks, n, inner),
            (n, inner),
            (2 * PAD, inner),
        ],
        [pltpu.VMEM((length + PAD, inner), F32), pltpu.VMEM((length + PAD, states), F32)],
        2 * 3 * length * n * inner,
        ip, ib, sp, sb, w["taps_i"], w["taps_s"], w["heads_rows"],
    )
    decay = chdec[chunks : chunks + 1]
    entering = state_before(local, decay, False)
    (yd,) = call(
        functools.partial(inner_kernel, width),
        [(length, inner)],
        [],
        2 * 6 * length * CHUNK * inner,
        v, bc, dt, cum, cumt, w["heads_rows"],
    )
    y, gn, carried, squares = call(
        functools.partial(gate_kernel, width),
        [(length, inner), (length, inner), (chunks, n, inner), (PAD, length)],
        [],
        2 * 3 * length * n * inner,
        yd, bc, cum, fresh, chdec, entering, gate, w["norm_gain"][None, :],
    )
    part = matmul(gn, w["out"], NT)
    saved = dict(
        current=current, root=root, normed=normed, ip=ip, sp=sp, ib=ib, sb=sb, gate=gate, v=v, bc=bc,
        dsi=dsi, dss=dss, dt=dt, cum=cum, cumt=cumt, fresh=fresh, chdec=chdec, decay=decay, y=y,
        gn=gn, states=carried,
    )
    return part, squares[0], saved


def both_cores(left, right):
    place = lax.axis_index("dp")
    n = lax.axis_size("dp")
    if n != 2:
        return lax.psum(matmul(left, right, ((0,), (0,))), "dp")
    sent = exchanged(matmul(left, half(right, 1 - place, 1), ((0,), (0,))), "dp", 1)
    return matmul(left, half(right, place, 1), ((0,), (0,))) + sent


def weight_grad(left, right):
    total = line_scatter_sum(both_cores(left, right), "seq")
    if lax.axis_size("dp") != 2:
        return total
    return joined(total, exchanged(total, "dp", 1), "dp", 1, 1)


def backward(grad, q, scale, slope, w, saved):
    s = saved
    length, inner = q.shape
    width = inner // w["heads"]
    states = w["taps_s"].shape[1]
    n = states // 2
    chunks = length // CHUNK
    dy, dgate, u, dgain, adjoint, local = call(
        functools.partial(open_kernel, width),
        [(length, inner), (length, inner), (length, inner), (PAD, inner), (chunks, n, inner), (n, inner)],
        [],
        2 * 3 * length * n * inner,
        q, s["y"], s["gate"], w["norm_gain"][None, :], scale[:, None], slope[:, None], s["bc"], s["cum"], s["chdec"],
    )
    later = state_before(local, s["decay"], True)
    du, dbc = call(
        functools.partial(back_kernel, width),
        [(length, inner), (length, states)],
        [pltpu.VMEM((CHUNK, CHUNK), F32)],
        2 * 15 * length * CHUNK * inner,
        dy, s["v"], s["bc"], s["dt"], s["cum"], s["cumt"], s["states"],
    )
    grad_out_weight = weight_grad(grad, u)
    grad_gate_weight = weight_grad(s["normed"], dgate)
    dti, dts, dstep, rows = call(
        functools.partial(close_kernel, width),
        [(length, inner), (length, states), (length, LANES), (3 * PAD, inner)],
        [pltpu.VMEM((n, inner), F32)],
        2 * 6 * length * n * inner,
        dy, s["y"], s["v"], s["bc"], s["dt"], s["cum"], s["sp"], w["heads_rows"], du, dbc, s["dsi"], s["dss"],
        adjoint, s["chdec"], s["fresh"], s["states"], later,
    )
    halo = shifted(jnp.concatenate([dti[:PAD], dts[:PAD]], axis=1), "seq", -1)
    dip, dsp, ri, rs = call(
        filter_back_kernel,
        [(length, inner), (length, states), (5 * PAD, inner), (5 * PAD, states)],
        [
            pltpu.VMEM((length + PAD, inner), F32),
            pltpu.VMEM((length + PAD, states), F32),
            pltpu.VMEM((length + PAD, inner), F32),
            pltpu.VMEM((length + PAD, states), F32),
        ],
        16 * length * inner,
        dti, halo[:, :inner], dts, halo[:, inner:], s["ip"], s["ib"], s["sp"], s["sb"], w["taps_i"], w["taps_s"],
    )
    dnormed = (
        matmul(dgate, w["gate"], NT)
        + matmul(dip, w["inner"], NT)
        + matmul(jnp.concatenate([dsp, dstep], axis=1), w["maps"], NT)
    )
    grad_inner_weight = weight_grad(s["normed"], dip)

    dgain_pre = jnp.sum(dnormed * s["current"] * s["root"], axis=0)

    def finish(rows_grad, offset):
        def take(array):
            return lax.dynamic_slice_in_dim(array, offset, rows_grad.shape[0], 0)

        x, root = take(s["current"]), take(s["root"])
        scaled = rows_grad * w["pre_gain"][None, :]
        along = jnp.mean(scaled * x, axis=-1, keepdims=True)
        return root * scaled - x * (root * root * root * along)

    branch = head_sum(dnormed, finish)

    order = distances("head")
    shared = dsp
    heads_count = lax.axis_size("head")
    if power_of_two(heads_count):
        for distance in order[::-1]:
            bit = bit_of("head", distance)
            shared = half(shared, bit, 1) + exchanged(half(shared, 1 - bit, 1), "head", distance)
    else:
        shared = lax.psum_scatter(shared, "head", scatter_dimension=1, tiled=True)
    small = jnp.concatenate([shared, dstep[:, : w["heads"]]], axis=1)
    grad_small = small_sum(matmul(s["normed"], small, ((0,), (0,))), "dp")
    grad_small = line_scatter_sum(grad_small, "seq")
    own = shared.shape[1]

    def folded(array):
        return array.reshape(-1, PAD, array.shape[1]).sum(axis=1)

    ri, rs, rows = folded(ri), folded(rs), folded(rows)
    over_heads = small_sum(jnp.concatenate([dgain_pre, rs.reshape(-1)]), "head")
    flat = jnp.concatenate(
        [over_heads, ri.reshape(-1), dgain.sum(axis=0), rows[0], rows[1, :LANES], rows[2, :LANES]]
    )
    flat = small_sum(small_sum(flat, "dp"), "seq")
    cut = []
    start = 0
    for size in (dgain_pre.size, rs.size, ri.size, inner, inner, LANES, LANES):
        cut.append(flat[start : start + size])
        start += size
    g_pre, g_rs, g_ri, g_norm, g_skip, g_rate, g_bias = cut
    g_rs = lax.dynamic_slice_in_dim(g_rs.reshape(5, states), lax.axis_index("head") * own, own, 1)
    g_ri = g_ri.reshape(5, inner)
    heads = w["heads"]
    grads = (
        g_pre,
        grad_gate_weight,
        grad_inner_weight,
        grad_small[:, :own],
        grad_small[:, own:],
        g_ri[:4],
        g_ri[4],
        g_rs[:4],
        g_rs[4],
        g_bias[:heads],
        g_rate[:heads],
        g_skip.reshape(heads, width).sum(axis=1),
        g_norm,
        grad_out_weight,
    )
    return grad + branch, grads


def gathered_columns(value):
    if not power_of_two(lax.axis_size("head")):
        return lax.all_gather(value, "head", axis=1, tiled=True)
    return gather_back(value, "head", distances("head")[::-1], 1)


def gathered_all(value):
    return gathered_columns(value)


def body(
    tokens,
    cotangent,
    pre_gain,
    gate_weight,
    inner_weight,
    state_weight,
    step_weight,
    filter_inner,
    filter_inner_bias,
    filter_state,
    filter_state_bias,
    step_bias,
    log_rate,
    skip_gain,
    norm_gain,
    out_weight,
):
    layers = pre_gain.shape[0]
    heads = step_bias.shape[1]
    inner = gate_weight.shape[2]
    taps = jnp.concatenate([filter_state, filter_state_bias[:, None, :]], axis=1)
    taps = gathered_columns(taps.reshape(-1, taps.shape[2]))
    taps = taps.reshape(layers, 5, -1)
    weights = []
    for layer in range(layers):
        maps = jnp.concatenate(
            [
                gathered_columns(state_weight[layer]),
                jnp.pad(step_weight[layer], ((0, 0), (0, LANES - heads))),
            ],
            axis=1,
        )
        weights.append(
            dict(
                heads=heads,
                pre_gain=pre_gain[layer],
                gate=gate_weight[layer],
                inner=inner_weight[layer],
                maps=maps,
                out=out_weight[layer],
                norm_gain=norm_gain[layer],
                taps_i=padded_rows([filter_inner[layer], filter_inner_bias[layer][None]], inner),
                taps_s=padded_rows([taps[layer]], taps.shape[2]),
                heads_rows=padded_rows(
                    [step_bias[layer][None], log_rate[layer][None], skip_gain[layer][None]], LANES
                ),
            )
        )
    current = tokens[0]
    grad = cotangent[0]
    kept = []
    for layer in range(layers):
        w = weights[layer]
        part, squares, saved = forward(current, w)
        last = layer == layers - 1
        if last:
            q = matmul(grad, w["out"])
            both = jnp.stack([squares, jnp.sum(q * saved["gn"], axis=1)])
            both = small_sum(both, "head")
            squares, along = both[0], both[1]
        else:
            squares = small_sum(squares, "head")
        scale = lax.rsqrt(squares / INNER + epsilon)

        def finish(rows, offset, scale=scale):
            return rows * lax.dynamic_slice_in_dim(scale, offset, rows.shape[0], 0)[:, None]

        branch = head_sum(part, finish)
        kept.append((saved, scale, branch))
        current = current + branch
    collected = [None] * layers
    for layer in reversed(range(layers)):
        w = weights[layer]
        saved, scale, branch = kept[layer]
        if layer < layers - 1:
            q = matmul(grad, w["out"])
            slope = jnp.sum(grad * branch, axis=1) * scale * scale / INNER
        else:
            slope = along * scale * scale * scale / INNER
        grad, collected[layer] = backward(grad, q, scale, slope, w, saved)
    stacked = [jnp.stack([entry[number] for entry in collected], axis=0) for number in range(14)]
    return (current[None], grad[None], *stacked)


def solution(mesh):
    placed = (
        P("dp", "seq", None),
        P("dp", "seq", None),
        P(),
        P(None, None, "head"),
        P(None, None, "head"),
        P(None, None, "head"),
        P(None, None, "head"),
        P(None, None, "head"),
        P(None, "head"),
        P(None, None, "head"),
        P(None, "head"),
        P(None, "head"),
        P(None, "head"),
        P(None, "head"),
        P(None, "head"),
        P(None, None, "head"),
    )
    return jax.shard_map(
        body,
        mesh=mesh,
        in_specs=placed,
        out_specs=(
            P("dp", "seq", None),
            P("dp", "seq", None),
            P(),
            P(None, "seq", "head"),
            P(None, "seq", "head"),
            P(None, "seq", "head"),
            P(None, "seq", "head"),
            P(None, None, "head"),
            P(None, "head"),
            P(None, None, "head"),
            P(None, "head"),
            P(None, "head"),
            P(None, "head"),
            P(None, "head"),
            P(None, "head"),
            P(None, "seq", "head"),
        ),
        check_vma=False,
    )
```

```python
import functools

import jax
import jax.numpy as jnp
from jax import lax
from jax.experimental import pallas as pl
from jax.experimental.pallas import tpu as pltpu
from jax.sharding import PartitionSpec as P

INNER = 3072
CHUNK = 128
LANES = 128
PAD = 8
VMEM = 20 * 1024 * 1024
epsilon = 1e-05
HIGH = lax.Precision.HIGH
HIGHEST = lax.Precision.HIGHEST
NEG = -1e30
F32 = jnp.float32


def power_of_two(n):
    return n & (n - 1) == 0


def exchanged(value, axis, distance):
    n = lax.axis_size(axis)
    return lax.ppermute(value, axis, [(i, i ^ distance) for i in range(n)])


def shifted(value, axis, step):
    n = lax.axis_size(axis)
    pairs = [(i, i + step) for i in range(n) if 0 <= i + step < n]
    return lax.ppermute(value, axis, pairs)


def distances(axis):
    n = lax.axis_size(axis)
    return [1 << k for k in range(n.bit_length() - 1)]


def bit_of(axis, distance):
    return (lax.axis_index(axis) // distance) % 2


def small_sum(value, axis):
    if not power_of_two(lax.axis_size(axis)):
        return lax.psum(value, axis)
    for distance in distances(axis):
        value = value + exchanged(value, axis, distance)
    return value


def half(value, which, dim=0):
    size = value.shape[dim] // 2
    return lax.dynamic_slice_in_dim(value, which * size, size, dim)


def joined(mine, other, axis, distance, dim=0):
    first = bit_of(axis, distance) == 0
    return jnp.concatenate(
        [jnp.where(first, mine, other), jnp.where(first, other, mine)], axis=dim
    )


def gather_back(value, axis, order, dim=0):
    for distance in order[::-1]:
        value = joined(value, exchanged(value, axis, distance), axis, distance, dim)
    return value


def tied(value, *others):
    return lax.optimization_barrier((value, *others))


def head_sum(lefts, product, finish):
    order = distances("head")
    rows = lefts[0].shape[0] // 2
    ways = (order, order[::-1])

    def chosen(other):
        picked = []
        for array in lefts:
            pieces = []
            for number, way in enumerate(ways):
                bit = bit_of("head", way[0])
                part = array[number * rows : (number + 1) * rows]
                pieces.append(half(part, 1 - bit if other else bit))
            picked.append(jnp.concatenate(pieces, axis=0))
        return product(*picked)

    sent = chosen(True)
    kept = chosen(False)
    sent, kept = yield sent, kept
    size = rows // 2
    got = [
        exchanged(sent[number * size : (number + 1) * size], "head", way[0])
        for number, way in enumerate(ways)
    ]
    kept = [kept[:size], kept[size:]]
    offsets = [bit_of("head", way[0]) * size + number * rows for number, way in enumerate(ways)]
    got, kept = yield got, kept
    for step in range(1, len(order)):
        bits = [bit_of("head", way[step]) for way in ways]
        sends = [half(k, 1 - bit) + half(g, 1 - bit) for k, g, bit in zip(kept, got, bits)]
        arrived = [exchanged(send, "head", way[step]) for send, way in zip(sends, ways)]
        kept = [half(k, bit) + half(g, bit) for k, g, bit in zip(kept, got, bits)]
        offsets = [o + bit * k.shape[0] for o, bit, k in zip(offsets, bits, kept)]
        got, kept = yield arrived, kept
    mine = [finish(k + g, o) for k, g, o in zip(kept, got, offsets)]
    for step in range(len(order) - 1, -1, -1):
        others = [exchanged(m, "head", way[step]) for m, way in zip(mine, ways)]
        others, mine = yield others, mine
        mine = [joined(m, o, "head", way[step]) for m, o, way in zip(mine, others, ways)]
    return jnp.concatenate(mine, axis=0)


class Steps:
    def __init__(self, steps):
        self.steps = steps
        self.now = next(steps)
        self.result = None

    def advance(self, *others):
        if self.result is not None:
            return others
        if len(others) > 0:
            self.now, *others = tied(self.now, *others)
        try:
            self.now = self.steps.send(self.now)
        except StopIteration as end:
            self.result = end.value
        return others

    def finished(self):
        while self.result is None:
            self.advance()
        return self.result


def after(value, *others):
    return tied(value, *others)[0]


def state_before(local, decay, reverse, windows):
    n = lax.axis_size("seq")
    state = jnp.zeros_like(local)
    done = []
    before = local
    for hop in range(n - 1):
        source, target = (n - 1 - hop, n - 2 - hop) if reverse else (hop, hop + 1)
        got = lax.ppermute(decay * state + local, "seq", [(source, target)])
        if hop < len(windows):
            got, *result = tied(got, *windows[hop](before))
            done.append(result)
        before = got
        state = state + got
    for window in windows[n - 1 :]:
        done.append(window(before))
    return state, done


def rows_of(*shape):
    return pl.BlockSpec(shape, lambda c: (c,) + (0,) * (len(shape) - 1))


def columns_of(*shape):
    return pl.BlockSpec(shape, lambda c: (0, c))


def all_of(*shape):
    return pl.BlockSpec(shape, lambda c: (0,) * len(shape))


def reverse(spec, steps):
    index = spec.index_map
    return pl.BlockSpec(spec.block_shape, lambda c: index(steps - 1 - c))


def call(kernel, steps, outs, scratch, flops, *args, backward=False):
    shapes = [jax.ShapeDtypeStruct(shape, F32) for shape, _ in outs]
    size = 4 * sum(a.size for a, _ in args) + 4 * sum(s.size for s in shapes)

    def spec(blocks):
        return reverse(blocks, steps) if backward else blocks

    return pl.pallas_call(
        kernel,
        grid=(steps,),
        out_shape=shapes,
        in_specs=[spec(blocks) for _, blocks in args],
        out_specs=[spec(blocks) for _, blocks in outs],
        scratch_shapes=scratch,
        compiler_params=pltpu.CompilerParams(vmem_limit_bytes=VMEM),
        cost_estimate=pl.CostEstimate(flops=flops, bytes_accessed=size, transcendentals=0),
    )(*[a for a, _ in args])


def dot(left, right, dims=((1,), (0,)), precision=HIGH):
    return lax.dot_general(
        left, right, (dims, ((), ())), precision=precision, preferred_element_type=F32
    )


NT = ((1,), (1,))


def sigmoid(value):
    return 1.0 / (1.0 + jnp.exp(-value))


def spread_heads(columns, tile, width):
    each = LANES // width
    lane = lax.broadcasted_iota(jnp.int32, (columns.shape[0], LANES), 1)
    result = columns[:, tile * each : tile * each + 1]
    for k in range(1, each):
        result = jnp.where(lane < k * width, result, columns[:, tile * each + k : tile * each + k + 1])
    return jnp.broadcast_to(result, (columns.shape[0], LANES))


def head_rows(row, width, total):
    tiles = [spread_heads(row, tile, width) for tile in range(total // LANES)]
    return jnp.concatenate(tiles, axis=1)


def filter_tile(scratch, taps, start, rows, cols):
    block = scratch[pl.ds(start, rows + PAD), cols]
    total = taps[4:5, cols] + taps[3:4, cols] * block[PAD:]
    for back in range(1, 4):
        total = total + taps[3 - back : 4 - back, cols] * pltpu.roll(block, back, 0)[PAD:]
    return total


def start_kernel(
    width, ip, ib, sp, sb, ti, ts, hp, v_out, bc_out, dsi, dss, dt_out, cum_out, cumt_out, fresh, local, chdec, passed, padi, pads
):
    inner = ip.shape[1]
    states = ts.shape[1]
    n = states // 2
    c = pl.program_id(0)

    @pl.when(c == 0)
    def _():
        padi[0:PAD, :] = ib[...]
        pads[0:PAD, :] = sb[...]
        passed[...] = jnp.ones_like(passed)
        local[...] = jnp.zeros_like(local)

    @pl.when(c > 0)
    def _():
        padi[0:PAD, :] = padi[CHUNK:, :]
        pads[0:PAD, :] = pads[CHUNK:, :]

    padi[PAD:, :] = ip[...]
    pads[PAD:, :] = sp[:, :states]
    rows = 64

    def filtered(step, _):
        start = pl.multiple_of(step * rows, rows)
        for scratch, taps, out, slope, size in (
            (padi, ti, v_out, dsi, inner),
            (pads, ts, bc_out, dss, states),
        ):
            for tile in range(size // LANES):
                cols = slice(tile * LANES, (tile + 1) * LANES)
                total = filter_tile(scratch, taps, start, rows, cols)
                gate = sigmoid(total)
                value = total * gate
                out[pl.ds(start, rows), cols] = value
                slope[pl.ds(start, rows), cols] = gate + value * (1.0 - gate)
        return 0

    lax.fori_loop(0, CHUNK // rows, filtered, 0)
    raw = sp[:, states:] + hp[0:1, :]
    dt = jnp.maximum(raw, 0.0) + jnp.log1p(jnp.exp(-jnp.abs(raw)))
    dt_out[...] = dt
    rate = -jnp.exp(hp[1:2, :]) * dt
    ones = (
        lax.broadcasted_iota(jnp.int32, (CHUNK, CHUNK), 0)
        >= lax.broadcasted_iota(jnp.int32, (CHUNK, CHUNK), 1)
    ).astype(F32)
    cum = dot(ones, rate, precision=HIGHEST)
    cum_out[...] = cum
    cumt_out[...] = cum.T[: cumt_out.shape[0]]
    last = cum[CHUNK - 1 : CHUNK, :]
    weight = jnp.exp(last - cum) * dt
    maps = bc_out[:, :n].T
    decay = head_rows(jnp.exp(last), width, inner)
    chdec[0] = jnp.broadcast_to(decay, (PAD, inner))
    passed[...] = passed[...] * decay
    for tile in range(inner // LANES):
        cols = slice(tile * LANES, (tile + 1) * LANES)
        weighted = v_out[:, cols] * spread_heads(weight, tile, width)
        part = dot(maps, weighted)
        fresh[0, :, cols] = part
        local[:, cols] = decay[:, cols] * local[:, cols] + part


def inner_kernel(width, v, bc, dt, cum, cumt, hp, out):
    inner = v.shape[1]
    n = bc.shape[1] // 2
    each = LANES // width
    lane = lax.broadcasted_iota(jnp.int32, (CHUNK, LANES), 1)
    lower = lax.broadcasted_iota(jnp.int32, (CHUNK, CHUNK), 0) >= lax.broadcasted_iota(
        jnp.int32, (CHUNK, CHUNK), 1
    )
    meet = dot(bc[:, n:], bc[:, :n], NT)
    for tile in range(inner // LANES):
        cols = slice(tile * LANES, (tile + 1) * LANES)
        values = v[:, cols]
        stepped = values * spread_heads(dt[...], tile, width)
        result = None
        for k in range(each):
            head = tile * each + k
            spread = cum[:, head : head + 1] - cumt[head : head + 1, :]
            mixing = jnp.exp(jnp.where(lower, spread, NEG)) * meet
            part = dot(mixing, stepped)
            result = part if k == 0 else jnp.where(lane < k * width, result, part)
        out[:, cols] = result + spread_heads(hp[2:3, :], tile, width) * values


def gate_kernel(width, yd, bc, cum, fresh, chdec, entering, gate, gain, y_out, gn_out, states, squares, final):
    inner = yd.shape[1]
    n = bc.shape[1] // 2
    ones = jnp.ones((PAD, LANES), F32)
    c = pl.program_id(0)

    @pl.when(c == 0)
    def _():
        final[...] = entering[...]

    carried = jnp.exp(cum[...])
    maps = bc[:, n:]
    total = None
    for tile in range(inner // LANES):
        cols = slice(tile * LANES, (tile + 1) * LANES)
        state = final[:, cols]
        states[0, :, cols] = state
        final[:, cols] = chdec[0, 0:1, cols] * state + fresh[0, :, cols]
        y = yd[:, cols] + spread_heads(carried, tile, width) * dot(maps, state)
        y_out[:, cols] = y
        g = gate[:, cols]
        gated = y * (g * sigmoid(g))
        gn_out[:, cols] = gated * gain[0:1, cols]
        total = gated * gated if tile == 0 else total + gated * gated
    squares[...] = dot(ones, total, NT, HIGHEST)


def open_kernel(
    width, q, y, gate, gain, factors, bc, cum, chdec, dy_out, dgate, u_out, dgain, adjoint, local, passed
):
    inner = q.shape[1]
    n = bc.shape[1] // 2
    c = pl.program_id(0)

    @pl.when(c == 0)
    def _():
        dgain[...] = jnp.zeros_like(dgain)
        local[...] = jnp.zeros_like(local)
        passed[...] = jnp.ones_like(passed)

    carried = jnp.exp(cum[...])
    maps = bc[:, n:].T
    turned = factors[...].T
    s = turned[:, 0:1]
    t = turned[:, 1:2]
    for tile in range(inner // LANES):
        cols = slice(tile * LANES, (tile + 1) * LANES)
        g = gate[:, cols]
        soft = sigmoid(g)
        silu = g * soft
        out = y[:, cols]
        gated = out * silu
        grad = q[:, cols]
        scaled = gated * s
        u_out[:, cols] = scaled * gain[0:1, cols]
        dgain[:, cols] = dgain[:, cols] + (grad * scaled).reshape(CHUNK // PAD, PAD, LANES).sum(axis=0)
        dgated = s * (grad * gain[0:1, cols]) - t * gated
        dgate[:, cols] = dgated * out * (soft + silu * (1.0 - soft))
        dy = dgated * silu
        dy_out[:, cols] = dy
        part = dot(maps, dy * spread_heads(carried, tile, width))
        adjoint[0, :, cols] = part
        local[:, cols] = local[:, cols] + passed[0:1, cols] * part
    passed[...] = passed[...] * chdec[0]


def back_kernel(width, dy, v, bc, dt, cum, cumt, states, du, dbc, gram):
    inner = v.shape[1]
    n = bc.shape[1] // 2
    each = LANES // width
    lane = lax.broadcasted_iota(jnp.int32, (CHUNK, LANES), 1)
    upper = lax.broadcasted_iota(jnp.int32, (CHUNK, CHUNK), 0) <= lax.broadcasted_iota(
        jnp.int32, (CHUNK, CHUNK), 1
    )
    inputs, outputs = bc[:, :n], bc[:, n:]
    meet = dot(inputs, outputs, NT)
    carried = jnp.exp(cum[...])
    grad_out = None
    for tile in range(inner // LANES):
        cols = slice(tile * LANES, (tile + 1) * LANES)
        grad = dy[:, cols]
        stepped = v[:, cols] * spread_heads(dt[...], tile, width)
        result = None
        for k in range(each):
            head = tile * each + k
            spread = cumt[head : head + 1, :] - cum[:, head : head + 1]
            decay = jnp.exp(jnp.where(upper, spread, NEG))
            part = dot(decay * meet, grad)
            result = part if k == 0 else jnp.where(lane < k * width, result, part)
            own = (lane >= k * width) & (lane < (k + 1) * width)
            cross = decay * dot(jnp.where(own, stepped, 0.0), grad, NT)
            first = tile == 0 and k == 0
            gram[...] = cross if first else gram[...] + cross
        du[:, cols] = result
        part = dot(grad * spread_heads(carried, tile, width), states[0, :, cols], NT)
        grad_out = part if tile == 0 else grad_out + part
    total = gram[...]
    dbc[:, :n] = dot(total, outputs)
    dbc[:, n:] = grad_out + dot(total.T, inputs)


def head_totals(product, width):
    each = LANES // width
    lane = lax.broadcasted_iota(jnp.int32, product.shape, 1)
    result = []
    for k in range(each):
        own = (lane >= k * width) & (lane < (k + 1) * width)
        result.append(jnp.sum(jnp.where(own, product, 0.0), axis=1, keepdims=True))
    return result


def place_heads(columns, shape):
    lane = lax.broadcasted_iota(jnp.int32, shape, 1)
    result = jnp.zeros(shape, F32)
    for head, column in enumerate(columns):
        result = jnp.where(lane == head, column, result)
    return result


def close_kernel(
    width, dy, y, v, du, dsi, adjoint, bc, dt, cum, sp, hp, dbc, dss, chdec, final, later,
    dti, dts, dstep, rows, leaving, running,
):
    inner = v.shape[1]
    n = bc.shape[1] // 2
    heads_rate = -jnp.exp(hp[1:2, :])

    @pl.when(pl.program_id(0) == 0)
    def _():
        crossing = jnp.sum(final[...] * later[...], axis=0, keepdims=True)
        columns = []
        for tile in range(inner // LANES):
            columns += head_totals(crossing[:, tile * LANES : (tile + 1) * LANES], width)
        running[...] = jnp.broadcast_to(place_heads(columns, (1, LANES)), running.shape)
        leaving[...] = later[...]
        rows[...] = jnp.zeros_like(rows)

    ones = (
        lax.broadcasted_iota(jnp.int32, (CHUNK, CHUNK), 0)
        <= lax.broadcasted_iota(jnp.int32, (CHUNK, CHUNK), 1)
    ).astype(F32)
    step = dt[...]
    cums = cum[...]
    fade = jnp.exp(cums[CHUNK - 1 : CHUNK, :] - cums)
    inputs = bc[:, :n]
    grad_in = dbc[:, :n]
    own, direct = [], []
    for tile in range(inner // LANES):
        cols = slice(tile * LANES, (tile + 1) * LANES)
        adj = leaving[:, cols]
        wide_fade = spread_heads(fade, tile, width)
        wide_step = spread_heads(step, tile, width)
        skip = spread_heads(hp[2:3, :], tile, width)
        values = v[:, cols]
        grad = dy[:, cols]
        dstepped = du[:, cols] + wide_fade * dot(inputs, adj)
        grad_in = grad_in + dot(wide_fade * wide_step * values, adj, NT)
        dti[:, cols] = (wide_step * dstepped + skip * grad) * dsi[:, cols]
        own += head_totals(grad * (y[:, cols] - skip * values), width)
        direct += head_totals(values * dstepped, width)
        part = (grad * values).reshape(CHUNK // PAD, PAD, LANES).sum(axis=0)
        rows[0:PAD, cols] = rows[0:PAD, cols] + part
        leaving[:, cols] = adjoint[0, :, cols] + chdec[0, 0:1, cols] * adj
    dts[:, :n] = grad_in * dss[:, :n]
    dts[:, n:] = dbc[:, n:] * dss[:, n:]
    direct = place_heads(direct, (CHUNK, LANES))
    dcum = place_heads(own, (CHUNK, LANES)) - step * direct
    drate = dot(ones, dcum, precision=HIGHEST) + running[0:1, :]
    running[...] = jnp.broadcast_to(drate[0:1, :], running.shape)
    dstep_value = direct + drate * heads_rate
    raw = sp[:, 2 * n :] + hp[0:1, :]
    grad_raw = dstep_value * sigmoid(raw)
    dstep[...] = grad_raw
    lanes = slice(0, LANES)
    rates = drate * heads_rate * step
    rows[PAD : 2 * PAD, lanes] = rows[PAD : 2 * PAD, lanes] + rates.reshape(
        CHUNK // PAD, PAD, LANES
    ).sum(axis=0)
    rows[2 * PAD : 3 * PAD, lanes] = rows[2 * PAD : 3 * PAD, lanes] + grad_raw.reshape(
        CHUNK // PAD, PAD, LANES
    ).sum(axis=0)


def filter_back_kernel(
    dti, hi, dts, hs, ip, pi, ib, sp, ps, sb, ti, ts, dip, dsp, ri, rs, padi, pads, padgi, padgs
):
    inner = ip.shape[1]
    states = dts.shape[1]
    place = pl.program_id(0)

    @pl.when(place == 0)
    def _():
        padgi[CHUNK:, :] = hi[...]
        padgs[CHUNK:, :] = hs[...]
        ri[...] = jnp.zeros_like(ri)
        rs[...] = jnp.zeros_like(rs)

    @pl.when(place > 0)
    def _():
        padgi[CHUNK:, :] = padgi[0:PAD, :]
        padgs[CHUNK:, :] = padgs[0:PAD, :]

    @pl.when(place == pl.num_programs(0) - 1)
    def _():
        padi[0:PAD, :] = ib[...]
        pads[0:PAD, :] = sb[...]

    @pl.when(place < pl.num_programs(0) - 1)
    def _():
        padi[0:PAD, :] = pi[...]
        pads[0:PAD, :] = ps[:, :states]

    padi[PAD:, :] = ip[...]
    pads[PAD:, :] = sp[:, :states]
    padgi[0:CHUNK, :] = dti[...]
    padgs[0:CHUNK, :] = dts[...]
    rows = 64

    def folded(value):
        return value.reshape(rows // PAD, PAD, LANES).sum(axis=0)

    def step(number, _):
        start = pl.multiple_of(number * rows, rows)
        for signal, grads, taps, out, sums, size in (
            (padi, padgi, ti, dip, ri, inner),
            (pads, padgs, ts, dsp, rs, states),
        ):
            for tile in range(size // LANES):
                cols = slice(tile * LANES, (tile + 1) * LANES)
                ahead = grads[pl.ds(start, rows + PAD), cols]
                grad = ahead[:rows]
                before = signal[pl.ds(start, rows + PAD), cols]
                total = taps[3:4, cols] * grad
                sums[3 * PAD : 4 * PAD, cols] = sums[3 * PAD : 4 * PAD, cols] + folded(grad * before[PAD:])
                sums[4 * PAD : 5 * PAD, cols] = sums[4 * PAD : 5 * PAD, cols] + folded(grad)
                for back in range(1, 4):
                    tap = 3 - back
                    total = total + taps[tap : tap + 1, cols] * pltpu.roll(ahead, rows + PAD - back, 0)[:rows]
                    place = slice(tap * PAD, (tap + 1) * PAD)
                    sums[place, cols] = sums[place, cols] + folded(
                        grad * pltpu.roll(before, back, 0)[PAD:]
                    )
                out[pl.ds(start, rows), cols] = total
        return 0

    lax.fori_loop(0, CHUNK // rows, step, 0)


def matmul(left, right, dims=((1,), (0,)), precision=HIGH):
    return lax.dot_general(left, right, (dims, ((), ())), precision=precision)


def padded_rows(rows, lanes):
    rows = jnp.concatenate(rows, axis=0)
    return jnp.pad(rows, ((0, PAD - rows.shape[0]), (0, lanes - rows.shape[1])))


def forward(current, w, first, extra, other_maps, taps):
    length = current.shape[0]
    inner = w["inner"].shape[1]
    heads = w["heads"]
    width = inner // heads
    states = w["states"]
    n = states // 2
    chunks = length // CHUNK
    root = lax.rsqrt(jnp.mean(current * current, axis=-1, keepdims=True) + epsilon)
    normed = current * root * w["pre_gain"][None, :]
    if first:
        whole = matmul(normed, w["state"], precision=HIGHEST)
        whole = jnp.concatenate([whole, taps], axis=0)
        ip = matmul(after(normed, whole), w["inner"])
        if power_of_two(lax.axis_size("head")):
            wait = whole
            for distance in distances("head"):
                other = exchanged(whole, "head", distance)
                if distance == 1:
                    other, ip = tied(other, ip)
                    wait = other
                whole = joined(whole, other, "head", distance, 1)
        else:
            whole = gathered_columns(whole)
            wait = whole
        gate = matmul(after(normed, wait), w["gate"])
        whole, gate = tied(whole, gate)
        taps = whole[length:]
        sp = whole[:length]
    else:
        ip = matmul(normed, w["inner"])
        sp = matmul(normed, w["maps"], NT, HIGHEST)
        gate = None
    border = shifted(
        jnp.concatenate([ip[length - PAD :], sp[length - PAD :, :states]], axis=1), "seq", 1
    )
    if first:
        step = matmul(after(normed, sp), w["step"], precision=HIGHEST)
        border, step = tied(border, step)
        sp = jnp.concatenate([sp, step], axis=1)
    else:
        gate = matmul(after(normed, ip, sp), w["gate"])
        border, gate = tied(border, gate)
    ib, sb = border[:, :inner], border[:, inner:]
    taps_s = taps[w["layer"] * PAD : (w["layer"] + 1) * PAD]
    b_inner, b_states, b_lanes = (rows_of(CHUNK, size) for size in (inner, states, LANES))
    b_heads, b_sp = columns_of(16, CHUNK), rows_of(CHUNK, states + LANES)
    b_block, b_state = rows_of(1, n, inner), all_of(n, inner)
    b_decay = rows_of(1, PAD, inner)
    v, bc, dsi, dss, dt, cum, cumt, fresh, local, chdec, decay = call(
        functools.partial(start_kernel, width),
        chunks,
        [
            ((length, inner), b_inner),
            ((length, states), b_states),
            ((length, inner), b_inner),
            ((length, states), b_states),
            ((length, LANES), b_lanes),
            ((length, LANES), b_lanes),
            ((16, length), b_heads),
            ((chunks, n, inner), b_block),
            ((n, inner), b_state),
            ((chunks, PAD, inner), b_decay),
            ((PAD, inner), all_of(PAD, inner)),
        ],
        [pltpu.VMEM((CHUNK + PAD, inner), F32), pltpu.VMEM((CHUNK + PAD, states), F32)],
        2 * 3 * length * n * inner,
        (ip, b_inner),
        (ib, all_of(PAD, inner)),
        (sp, b_sp),
        (sb, all_of(PAD, states)),
        (w["taps_i"], all_of(PAD, inner)),
        (taps_s, all_of(PAD, states)),
        (w["heads_rows"], all_of(PAD, LANES)),
    )
    decay = decay[0:1]

    def inside(before):
        return call(
            functools.partial(inner_kernel, width),
            chunks,
            [((length, inner), b_inner)],
            [],
            2 * 6 * length * CHUNK * inner,
            (v, b_inner),
            (bc, b_states),
            (dt, b_lanes),
            (cum, b_lanes),
            (cumt, b_heads),
            (w["heads_rows"], all_of(PAD, LANES)),
        )

    other_maps = gathered_rows(after(other_maps, chdec).T)

    def aside(before):
        return [matmul(after(extra, before), w["last_out"])] if first else [extra]

    entering, ((yd,), (extra,), (other_maps,)) = state_before(
        local, decay, False, [inside, aside, lambda before: [other_maps]]
    )
    y, gn, carried, squares, final = call(
        functools.partial(gate_kernel, width),
        chunks,
        [
            ((length, inner), b_inner),
            ((length, inner), b_inner),
            ((chunks, n, inner), b_block),
            ((PAD, length), columns_of(PAD, CHUNK)),
            ((n, inner), b_state),
        ],
        [],
        2 * 3 * length * n * inner,
        (yd, b_inner),
        (bc, b_states),
        (cum, b_lanes),
        (fresh, b_block),
        (chdec, b_decay),
        (entering, b_state),
        (gate, b_inner),
        (w["norm_gain"][None, :], all_of(1, inner)),
    )
    saved = dict(
        current=current, root=root, normed=normed, ip=ip, sp=sp, ib=ib, sb=sb, gate=gate, v=v, bc=bc,
        dsi=dsi, dss=dss, dt=dt, cum=cum, cumt=cumt, fresh=fresh, chdec=chdec, decay=decay, y=y,
        gn=gn, states=carried, taps_s=taps_s, final=final,
    )
    return gn, squares[0:1], saved, extra, other_maps, taps


def core_products(left, right):
    place = lax.axis_index("dp")
    if lax.axis_size("dp") != 2:
        total = matmul(left, right, ((0,), (0,)))
        return total, total
    return (
        matmul(left, half(right, 1 - place, 1), ((0,), (0,))),
        matmul(left, half(right, place, 1), ((0,), (0,))),
    )


def over_cores(sent, kept):
    if lax.axis_size("dp") != 2:
        return lax.psum(kept, "dp")
    return kept + exchanged(sent, "dp", 1)


def over_seq(total):
    return lax.psum_scatter(total, "seq", scatter_dimension=0, tiled=True)


def place_kernel(*refs):
    *parts, out = refs
    first = lax.axis_index("dp") == 0
    width = out.shape[2] // 2
    for layer in range(len(parts) // 2):
        mine, other = parts[2 * layer], parts[2 * layer + 1]

        @pl.when(first)
        def _():
            out[layer, :, :width] = mine[...]
            out[layer, :, width:] = other[...]

        @pl.when(jnp.logical_not(first))
        def _():
            out[layer, :, :width] = other[...]
            out[layer, :, width:] = mine[...]


def cores_joined(pairs, start, width):
    if lax.axis_size("dp") != 2:
        return jnp.stack([mine[:, start : start + width] for mine, _ in pairs], axis=0)
    pieces = [piece for pair in pairs for piece in pair]
    rows = pieces[0].shape[0]
    tile = 96 if rows % 96 == 0 else rows
    return pl.pallas_call(
        place_kernel,
        grid=(rows // tile,),
        out_shape=jax.ShapeDtypeStruct((len(pairs), rows, 2 * width), F32),
        in_specs=[pl.BlockSpec((tile, width), lambda i: (i, start // width))] * len(pieces),
        out_specs=pl.BlockSpec((len(pairs), tile, 2 * width), lambda i: (0, i, 0)),
        compiler_params=pltpu.CompilerParams(vmem_limit_bytes=24 * 1024 * 1024),
    )(*pieces)


def backward(grad, q, scale, slope, w, saved, beside, waiting):
    s = saved
    length, inner = q.shape
    width = inner // w["heads"]
    states = w["states"]
    n = states // 2
    chunks = length // CHUNK
    factors = jnp.pad(jnp.concatenate([scale, slope], axis=0), ((0, PAD - 2), (0, 0)))
    b_inner, b_states, b_lanes = (rows_of(CHUNK, size) for size in (inner, states, LANES))
    b_heads, b_sp = columns_of(16, CHUNK), rows_of(CHUNK, states + LANES)
    b_block, b_state = rows_of(1, n, inner), all_of(n, inner)
    b_decay = rows_of(1, PAD, inner)
    dy, dgate, u, dgain, adjoint, local = call(
        functools.partial(open_kernel, width),
        chunks,
        [
            ((length, inner), b_inner),
            ((length, inner), b_inner),
            ((length, inner), b_inner),
            ((PAD, inner), all_of(PAD, inner)),
            ((chunks, n, inner), b_block),
            ((n, inner), b_state),
        ],
        [pltpu.VMEM((PAD, inner), F32)],
        2 * 3 * length * n * inner,
        (q, b_inner),
        (s["y"], b_inner),
        (s["gate"], b_inner),
        (w["norm_gain"][None, :], all_of(1, inner)),
        (factors, columns_of(PAD, CHUNK)),
        (s["bc"], b_states),
        (s["cum"], b_lanes),
        (s["chdec"], b_decay),
    )

    def cross_out(before):
        return core_products(grad, after(u, before))

    def cross_gate(before):
        result = core_products(s["normed"], after(dgate, before))
        return beside.advance(*result) if beside is not None else result

    def inside(before):
        result = call(
            functools.partial(back_kernel, width),
            chunks,
            [((length, inner), b_inner), ((length, states), b_states)],
            [pltpu.VMEM((CHUNK, CHUNK), F32)],
            2 * 15 * length * CHUNK * inner,
            (after(dy, before), b_inner),
            (s["v"], b_inner),
            (s["bc"], b_states),
            (s["dt"], b_lanes),
            (s["cum"], b_lanes),
            (s["cumt"], b_heads),
            (s["states"], b_block),
        )
        return beside.advance(*result) if beside is not None else result

    later, (halves_out, halves_gate, (du, dbc)) = state_before(
        local, s["decay"], True, [cross_out, cross_gate, inside]
    )
    pair = jnp.concatenate([over_cores(*halves_out), over_cores(*halves_gate)], axis=1)
    if waiting is not None:
        pair = after(pair, waiting)
    pair = over_seq(pair)
    dti, dts, dstep, rows = call(
        functools.partial(close_kernel, width),
        chunks,
        [
            ((length, inner), b_inner),
            ((length, states), b_states),
            ((length, LANES), b_lanes),
            ((3 * PAD, inner), all_of(3 * PAD, inner)),
        ],
        [pltpu.VMEM((n, inner), F32), pltpu.VMEM((PAD, LANES), F32)],
        2 * 6 * length * n * inner,
        (dy, b_inner),
        (s["y"], b_inner),
        (s["v"], b_inner),
        (du, b_inner),
        (s["dsi"], b_inner),
        (adjoint, b_block),
        (s["bc"], b_states),
        (s["dt"], b_lanes),
        (s["cum"], b_lanes),
        (s["sp"], b_sp),
        (w["heads_rows"], all_of(PAD, LANES)),
        (dbc, b_states),
        (s["dss"], b_states),
        (s["chdec"], b_decay),
        (s["final"], b_state),
        (later, b_state),
        backward=True,
    )
    if beside is not None:
        dti, dts = beside.advance(dti, dts)
    halo = shifted(jnp.concatenate([dti[:PAD], dts[:PAD]], axis=1), "seq", -1)
    base = matmul(after(dgate, dti), w["gate"], NT)
    halo, base = tied(halo, base)
    def edge(size):
        return pl.BlockSpec((PAD, size), lambda c: (jnp.maximum(c * (CHUNK // PAD) - 1, 0), 0))

    dip, dsp, ri, rs = call(
        filter_back_kernel,
        chunks,
        [
            ((length, inner), b_inner),
            ((length, states), b_states),
            ((5 * PAD, inner), all_of(5 * PAD, inner)),
            ((5 * PAD, states), all_of(5 * PAD, states)),
        ],
        [pltpu.VMEM((CHUNK + PAD, size), F32) for size in (inner, states, inner, states)],
        16 * length * inner,
        (dti, b_inner),
        (halo[:, :inner], all_of(PAD, inner)),
        (dts, b_states),
        (halo[:, inner:], all_of(PAD, states)),
        (s["ip"], b_inner),
        (s["ip"], edge(inner)),
        (s["ib"], all_of(PAD, inner)),
        (s["sp"], b_sp),
        (s["sp"], edge(states + LANES)),
        (s["sb"], all_of(PAD, states)),
        (w["taps_i"], all_of(PAD, inner)),
        (s["taps_s"], all_of(PAD, states)),
        backward=True,
    )
    if beside is not None:
        (dip,) = beside.advance(dip)

    def product(base, dip, dmaps):
        return base + matmul(dip, w["inner"], NT) + matmul(dmaps, w["maps"])

    gains = []

    def finish(rows_grad, offset):
        def take(array):
            return lax.dynamic_slice_in_dim(array, offset, rows_grad.shape[0], 0)

        x, root = take(s["current"]), take(s["root"])
        scaled = rows_grad * w["pre_gain"][None, :]
        along = jnp.mean(scaled * x, axis=-1, keepdims=True)
        gains.append(jnp.sum(rows_grad * x * root, axis=0))
        return root * scaled - x * (root * root * root * along)

    shared = dsp
    own = states // lax.axis_size("head")
    lefts = [base, dip, jnp.concatenate([dsp, dstep], axis=1)]
    if power_of_two(lax.axis_size("head")):
        way = distances("head")[::-1]
        for number, distance in enumerate(way):
            bit = bit_of("head", distance)
            other = exchanged(half(shared, 1 - bit, 1), "head", distance)
            if number == 0:
                steps = Steps(head_sum(lefts, product, finish))
                (other,) = steps.advance(other)
            shared = half(shared, bit, 1) + other
    else:
        shared = lax.psum_scatter(shared, "head", scatter_dimension=1, tiled=True)
        steps = Steps(head_sum(lefts, product, finish))
        steps.advance()
    halves = core_products(s["normed"], after(dip, shared))
    if waiting is None:
        (pair,) = steps.advance(pair)
    else:
        steps.advance()
    small = jnp.concatenate([shared, dstep[:, : LANES - own]], axis=1)
    total_small = small_sum(matmul(s["normed"], after(small, halves), ((0,), (0,))), "dp")
    last = jnp.concatenate([over_cores(*halves), total_small], axis=1)
    if waiting is None:
        (last,) = steps.advance(last)
    else:
        last, pair = steps.advance(last, pair)
    last = over_seq(after(last, pair))
    branch = steps.finished()
    grad = grad + branch

    def folded(array):
        return array.reshape(-1, PAD, array.shape[1]).sum(axis=1)

    ri, rs, rows = folded(ri), folded(rs), folded(rows)
    over_heads = jnp.concatenate([gains[0] + gains[1], rs.reshape(-1)])
    flat = jnp.concatenate(
        [ri.reshape(-1), dgain.sum(axis=0), rows[0], rows[1, :LANES], rows[2, :LANES]]
    )
    return grad, pair, last, over_heads, flat, own


def small_grads(over_heads, flat, own, w):
    model, inner = w["inner"].shape
    states = w["states"]
    heads = w["heads"]
    g_pre, g_rs = over_heads[:model], over_heads[model:]
    cut = []
    start = 0
    for size in (5 * inner, inner, inner, LANES, LANES):
        cut.append(flat[start : start + size])
        start += size
    g_ri, g_norm, g_skip, g_rate, g_bias = cut
    g_rs = lax.dynamic_slice_in_dim(g_rs.reshape(5, states), lax.axis_index("head") * own, own, 1)
    g_ri = g_ri.reshape(5, inner)
    return (
        g_pre,
        g_ri[:4],
        g_ri[4],
        g_rs[:4],
        g_rs[4],
        g_bias[:heads],
        g_rate[:heads],
        g_skip.reshape(heads, -1).sum(axis=1),
        g_norm,
    )


def gathered_columns(value):
    if not power_of_two(lax.axis_size("head")):
        return lax.all_gather(value, "head", axis=1, tiled=True)
    return gather_back(value, "head", distances("head")[::-1], 1)


def gathered_rows(value):
    if not power_of_two(lax.axis_size("head")):
        return lax.all_gather(value, "head", axis=0, tiled=True)
    return gather_back(value, "head", distances("head")[::-1], 0)


def body(
    tokens,
    cotangent,
    pre_gain,
    gate_weight,
    inner_weight,
    state_weight,
    step_weight,
    filter_inner,
    filter_inner_bias,
    filter_state,
    filter_state_bias,
    step_bias,
    log_rate,
    skip_gain,
    norm_gain,
    out_weight,
):
    layers = pre_gain.shape[0]
    heads = step_bias.shape[1]
    inner = gate_weight.shape[2]
    taps = jnp.concatenate([filter_state, filter_state_bias[:, None, :]], axis=1)
    taps = jnp.pad(taps, ((0, 0), (0, PAD - taps.shape[1]), (0, 0))).reshape(layers * PAD, -1)
    weights = []
    for layer in range(layers):
        steps = jnp.pad(step_weight[layer], ((0, 0), (0, LANES - heads)))
        weights.append(
            dict(
                layer=layer,
                heads=heads,
                states=state_weight.shape[2] * lax.axis_size("head"),
                pre_gain=pre_gain[layer],
                gate=gate_weight[layer],
                inner=inner_weight[layer],
                state=state_weight[layer],
                step=steps,
                out=out_weight[layer],
                norm_gain=norm_gain[layer],
                taps_i=padded_rows([filter_inner[layer], filter_inner_bias[layer][None]], inner),
                heads_rows=padded_rows(
                    [step_bias[layer][None], log_rate[layer][None], skip_gain[layer][None]], LANES
                ),
            )
        )
    current = tokens[0]
    grad = cotangent[0]
    kept = []
    weights[0]["last_out"] = weights[layers - 1]["out"]
    extra = grad
    for layer in range(layers):
        w = weights[layer]
        other = weights[(layer + 1) % layers]
        gn, squares, saved, extra, maps, taps = forward(
            current, w, layer == 0, extra, other["state"], taps
        )
        other["maps"] = jnp.concatenate([maps, after(other["step"], maps).T], axis=0)
        last = layer == layers - 1
        if last:
            both = jnp.concatenate([squares, jnp.sum(extra * gn, axis=1)[None, :]], axis=0)
            both = small_sum(both, "head")
            squares, along = both[0:1], both[1:2]
        else:
            squares = small_sum(squares, "head")
        scale = lax.rsqrt(squares / INNER + epsilon)

        def finish(rows, offset, scale=scale):
            return rows * lax.dynamic_slice_in_dim(scale[0], offset, rows.shape[0], 0)[:, None]

        steps = Steps(head_sum([gn], lambda rows, w=w: matmul(rows, w["out"], NT), finish))
        if last:
            scale = after(scale, steps.now)
            steps.advance(scale)
        branch = None if last else steps.finished()
        kept.append((saved, scale, branch))
        if not last:
            current = current + branch
    collected = [None] * layers
    waiting = None
    for layer in reversed(range(layers)):
        w = weights[layer]
        saved, scale, branch = kept[layer]
        if layer < layers - 1:
            q, waiting = tied(matmul(grad, w["out"]), waiting)
            collected[layer + 1][1] = waiting
            slope = jnp.sum(grad * branch, axis=1)[None, :] * scale * scale / INNER
        else:
            q = extra
            slope = along * scale * scale * scale / INNER
        grad, *collected[layer] = backward(
            grad, q, scale, slope, w, saved, steps if layer == layers - 1 else None, waiting
        )
        waiting = collected[layer][1]
    current = current + steps.finished()
    over_heads = jnp.concatenate([entry[2] for entry in collected])
    flat = jnp.concatenate([small_sum(over_heads, "head")] + [entry[3] for entry in collected])
    flat = small_sum(small_sum(flat, "dp"), "seq")
    size = collected[0][2].size
    rest = collected[0][3].size
    results = []
    for layer in range(layers):
        start = layers * size + layer * rest
        results.append(
            small_grads(
                flat[layer * size : (layer + 1) * size],
                flat[start : start + rest],
                collected[layer][4],
                weights[layer],
            )
        )
    stacked = [jnp.stack([entry[number] for entry in results], axis=0) for number in range(9)]
    two = lax.axis_size("dp") == 2

    def with_other(part):
        return part, exchanged(part, "dp", 1) if two else part

    pairs = [[with_other(entry[0]) for entry in collected]]
    half_width = inner // 2 if two else inner
    large = {
        "out": cores_joined(pairs[0], 0, half_width),
        "gate": cores_joined(pairs[0], half_width, half_width),
    }
    collected[0][1], current, grad, stacked, large = tied(
        collected[0][1], current, grad, stacked, large
    )
    pairs.append([with_other(entry[1]) for entry in collected])
    large["inner"] = cores_joined(pairs[1], 0, half_width)
    small = jnp.stack([entry[1][:, half_width : half_width + LANES] for entry in collected], axis=0)
    own = collected[0][4]
    return (
        current[None],
        grad[None],
        stacked[0],
        large["gate"],
        large["inner"],
        small[:, :, :own],
        small[:, :, own : own + heads],
        *stacked[1:],
        large["out"],
    )


def solution(mesh):
    placed = (
        P("dp", "seq", None),
        P("dp", "seq", None),
        P(),
        P(None, None, "head"),
        P(None, None, "head"),
        P(None, None, "head"),
        P(None, None, "head"),
        P(None, None, "head"),
        P(None, "head"),
        P(None, None, "head"),
        P(None, "head"),
        P(None, "head"),
        P(None, "head"),
        P(None, "head"),
        P(None, "head"),
        P(None, None, "head"),
    )
    return jax.shard_map(
        body,
        mesh=mesh,
        in_specs=placed,
        out_specs=(
            P("dp", "seq", None),
            P("dp", "seq", None),
            P(),
            P(None, "seq", "head"),
            P(None, "seq", "head"),
            P(None, "seq", "head"),
            P(None, "seq", "head"),
            P(None, None, "head"),
            P(None, "head"),
            P(None, None, "head"),
            P(None, "head"),
            P(None, "head"),
            P(None, "head"),
            P(None, "head"),
            P(None, "head"),
            P(None, "seq", "head"),
        ),
        check_vma=False,
    )
```

```python
import functools

import jax
import jax.numpy as jnp
from jax import lax
from jax.experimental import pallas as pl
from jax.experimental.pallas import tpu as pltpu
from jax.sharding import PartitionSpec as P

INNER = 3072
CHUNK = 128
LANES = 128
PAD = 8
SMALL = 96
COST = 4
VMEM = 20 * 1024 * 1024
LARGE = 56 * 1024 * 1024
epsilon = 1e-05
HIGH = lax.Precision.HIGH
HIGHEST = lax.Precision.HIGHEST
NEG = -1e30
F32 = jnp.float32


def power_of_two(n):
    return n & (n - 1) == 0


def exchanged(value, axis, distance):
    n = lax.axis_size(axis)
    return lax.ppermute(value, axis, [(i, i ^ distance) for i in range(n)])


def shifted(value, axis, step):
    n = lax.axis_size(axis)
    pairs = [(i, i + step) for i in range(n) if 0 <= i + step < n]
    return lax.ppermute(value, axis, pairs)


def distances(axis):
    n = lax.axis_size(axis)
    return [1 << k for k in range(n.bit_length() - 1)]


def bit_of(axis, distance):
    return (lax.axis_index(axis) // distance) % 2


def small_sum(value, axis):
    if not power_of_two(lax.axis_size(axis)):
        return lax.psum(value, axis)
    for distance in distances(axis):
        value = value + exchanged(value, axis, distance)
    return value


def half(value, which, dim=0):
    size = value.shape[dim] // 2
    return lax.dynamic_slice_in_dim(value, which * size, size, dim)


def joined(mine, other, axis, distance, dim=0):
    first = bit_of(axis, distance) == 0
    return jnp.concatenate(
        [jnp.where(first, mine, other), jnp.where(first, other, mine)], axis=dim
    )


def gather_back(value, axis, order, dim=0):
    for distance in order[::-1]:
        value = joined(value, exchanged(value, axis, distance), axis, distance, dim)
    return value


def tied(value, *others):
    return lax.optimization_barrier((value, *others))


def head_sum(lefts, product, finish):
    order = distances("head")
    rows = lefts[0].shape[0] // 2
    ways = (order, order[::-1])

    def chosen(other):
        picked = []
        for array in lefts:
            pieces = []
            for number, way in enumerate(ways):
                bit = bit_of("head", way[0])
                part = array[number * rows : (number + 1) * rows]
                pieces.append(half(part, 1 - bit if other else bit))
            picked.append(jnp.concatenate(pieces, axis=0))
        return product(*picked)

    sent = chosen(True)
    kept = chosen(False)
    sent, kept = yield sent, kept
    size = rows // 2
    got = [
        exchanged(sent[number * size : (number + 1) * size], "head", way[0])
        for number, way in enumerate(ways)
    ]
    kept = [kept[:size], kept[size:]]
    offsets = [bit_of("head", way[0]) * size + number * rows for number, way in enumerate(ways)]
    got, kept = yield got, kept
    for step in range(1, len(order)):
        bits = [bit_of("head", way[step]) for way in ways]
        sends = [half(k, 1 - bit) + half(g, 1 - bit) for k, g, bit in zip(kept, got, bits)]
        arrived = [exchanged(send, "head", way[step]) for send, way in zip(sends, ways)]
        kept = [half(k, bit) + half(g, bit) for k, g, bit in zip(kept, got, bits)]
        offsets = [o + bit * k.shape[0] for o, bit, k in zip(offsets, bits, kept)]
        got, kept = yield arrived, kept
    mine = [finish(k + g, o) for k, g, o in zip(kept, got, offsets)]
    for step in range(len(order) - 1, -1, -1):
        others = [exchanged(m, "head", way[step]) for m, way in zip(mine, ways)]
        others, mine = yield others, mine
        mine = [joined(m, o, "head", way[step]) for m, o, way in zip(mine, others, ways)]
    return jnp.concatenate(mine, axis=0)


class Steps:
    def __init__(self, steps):
        self.steps = steps
        self.now = next(steps)
        self.result = None

    def advance(self, *others):
        if self.result is not None:
            return others
        if len(others) > 0:
            self.now, *others = tied(self.now, *others)
        try:
            self.now = self.steps.send(self.now)
        except StopIteration as end:
            self.result = end.value
        return others

    def finished(self):
        while self.result is None:
            self.advance()
        return self.result


def after(value, *others):
    return tied(value, *others)[0]


def state_before(local, decay, reverse, windows):
    n = lax.axis_size("seq")
    done = []
    arrived = []
    before = local
    for hop in range(n - 1):
        source, target = (n - 1 - hop, n - 2 - hop) if reverse else (hop, hop + 1)
        leaving = local if hop == 0 else decay * before + local
        got = lax.ppermute(leaving, "seq", [(source, target)])
        if hop < len(windows):
            got, *result = tied(got, *windows[hop](before, done))
            done.append(result)
        before = got
        arrived.append(got)
    for window in windows[n - 1 :]:
        done.append(window(before, done))
    return sum(arrived) if len(arrived) > 0 else jnp.zeros_like(local), done


def rows_of(*shape):
    return pl.BlockSpec(shape, lambda c: (c,) + (0,) * (len(shape) - 1))


def columns_of(*shape):
    return pl.BlockSpec(shape, lambda c: (0, c))


def all_of(*shape):
    return pl.BlockSpec(shape, lambda c: (0,) * len(shape))


def reverse(spec, steps):
    index = spec.index_map
    return pl.BlockSpec(spec.block_shape, lambda c: index(steps - 1 - c))


def call(kernel, steps, outs, scratch, flops, *args, backward=False, vmem=VMEM):
    shapes = [jax.ShapeDtypeStruct(shape, F32) for shape, _ in outs]
    size = 4 * sum(a.size for a, _ in args) + 4 * sum(s.size for s in shapes)

    def spec(blocks):
        return reverse(blocks, steps) if backward else blocks

    return pl.pallas_call(
        kernel,
        grid=(steps,),
        out_shape=shapes,
        in_specs=[spec(blocks) for _, blocks in args],
        out_specs=[spec(blocks) for _, blocks in outs],
        scratch_shapes=scratch,
        compiler_params=pltpu.CompilerParams(vmem_limit_bytes=vmem),
        cost_estimate=pl.CostEstimate(flops=flops // COST, bytes_accessed=size // COST, transcendentals=0),
    )(*[a for a, _ in args])


def dot(left, right, dims=((1,), (0,)), precision=HIGH):
    return lax.dot_general(
        left, right, (dims, ((), ())), precision=precision, preferred_element_type=F32
    )


NT = ((1,), (1,))


def sigmoid(value):
    return 1.0 / (1.0 + jnp.exp(-value))


def spread_heads(columns, tile, width):
    each = LANES // width
    lane = lax.broadcasted_iota(jnp.int32, (columns.shape[0], LANES), 1)
    result = columns[:, tile * each : tile * each + 1]
    for k in range(1, each):
        result = jnp.where(lane < k * width, result, columns[:, tile * each + k : tile * each + k + 1])
    return jnp.broadcast_to(result, (columns.shape[0], LANES))


def head_rows(row, width, total):
    tiles = [spread_heads(row, tile, width) for tile in range(total // LANES)]
    return jnp.concatenate(tiles, axis=1)


def filter_tile(scratch, taps, start, rows, cols):
    block = scratch[pl.ds(start, rows + PAD), cols]
    total = taps[4:5, cols] + taps[3:4, cols] * block[PAD:]
    for back in range(1, 4):
        total = total + taps[3 - back : 4 - back, cols] * pltpu.roll(block, back, 0)[PAD:]
    return total


def start_kernel(
    width, ip, ib, sp, sb, ti, ts, hp, v_out, bc_out, dsi, dss, dt_out, cum_out, cumt_out, fresh, local, chdec, passed, padi, pads
):
    inner = ip.shape[1]
    states = ts.shape[1]
    n = states // 2
    c = pl.program_id(0)

    @pl.when(c == 0)
    def _():
        padi[0:PAD, :] = ib[...]
        pads[0:PAD, :] = sb[...]
        passed[...] = jnp.ones_like(passed)
        local[...] = jnp.zeros_like(local)

    @pl.when(c > 0)
    def _():
        padi[0:PAD, :] = padi[CHUNK:, :]
        pads[0:PAD, :] = pads[CHUNK:, :]

    padi[PAD:, :] = ip[...]
    pads[PAD:, :] = sp[:, :states]
    rows = 64

    def filtered(step, _):
        start = pl.multiple_of(step * rows, rows)
        for scratch, taps, out, slope, size in (
            (padi, ti, v_out, dsi, inner),
            (pads, ts, bc_out, dss, states),
        ):
            for tile in range(size // LANES):
                cols = slice(tile * LANES, (tile + 1) * LANES)
                total = filter_tile(scratch, taps, start, rows, cols)
                gate = sigmoid(total)
                value = total * gate
                out[pl.ds(start, rows), cols] = value
                slope[pl.ds(start, rows), cols] = gate + value * (1.0 - gate)
        return 0

    lax.fori_loop(0, CHUNK // rows, filtered, 0)
    raw = sp[:, states:] + hp[0:1, :]
    dt = jnp.maximum(raw, 0.0) + jnp.log1p(jnp.exp(-jnp.abs(raw)))
    dt_out[...] = dt
    rate = -jnp.exp(hp[1:2, :]) * dt
    ones = (
        lax.broadcasted_iota(jnp.int32, (CHUNK, CHUNK), 0)
        >= lax.broadcasted_iota(jnp.int32, (CHUNK, CHUNK), 1)
    ).astype(F32)
    cum = dot(ones, rate, precision=HIGHEST)
    cum_out[...] = cum
    cumt_out[...] = cum.T[: cumt_out.shape[0]]
    last = cum[CHUNK - 1 : CHUNK, :]
    weight = jnp.exp(last - cum) * dt
    maps = bc_out[:, :n].T
    decay = head_rows(jnp.exp(last), width, inner)
    chdec[0] = jnp.broadcast_to(decay, (PAD, inner))
    passed[...] = passed[...] * decay
    for tile in range(inner // LANES):
        cols = slice(tile * LANES, (tile + 1) * LANES)
        weighted = v_out[:, cols] * spread_heads(weight, tile, width)
        part = dot(maps, weighted, precision=HIGHEST)
        fresh[0, :, cols] = part
        local[:, cols] = decay[:, cols] * local[:, cols] + part


def inner_kernel(width, v, bc, dt, cum, cumt, hp, out):
    inner = v.shape[1]
    n = bc.shape[1] // 2
    each = LANES // width
    lane = lax.broadcasted_iota(jnp.int32, (CHUNK, LANES), 1)
    lower = lax.broadcasted_iota(jnp.int32, (CHUNK, CHUNK), 0) >= lax.broadcasted_iota(
        jnp.int32, (CHUNK, CHUNK), 1
    )
    meet = dot(bc[:, n:], bc[:, :n], NT, HIGHEST)
    for tile in range(inner // LANES):
        cols = slice(tile * LANES, (tile + 1) * LANES)
        values = v[:, cols]
        stepped = values * spread_heads(dt[...], tile, width)
        result = None
        for k in range(each):
            head = tile * each + k
            spread = cum[:, head : head + 1] - cumt[head : head + 1, :]
            mixing = jnp.exp(jnp.where(lower, spread, NEG)) * meet
            part = dot(mixing, stepped, precision=HIGHEST)
            result = part if k == 0 else jnp.where(lane < k * width, result, part)
        out[:, cols] = result + spread_heads(hp[2:3, :], tile, width) * values


def gate_kernel(width, yd, bc, cum, fresh, chdec, entering, gate, gain, y_out, gn_out, states, squares, final):
    inner = yd.shape[1]
    n = bc.shape[1] // 2
    ones = jnp.ones((PAD, LANES), F32)
    c = pl.program_id(0)

    @pl.when(c == 0)
    def _():
        final[...] = entering[...]

    carried = jnp.exp(cum[...])
    maps = bc[:, n:]
    total = None
    for tile in range(inner // LANES):
        cols = slice(tile * LANES, (tile + 1) * LANES)
        state = final[:, cols]
        states[0, :, cols] = state
        final[:, cols] = chdec[0, 0:1, cols] * state + fresh[0, :, cols]
        y = yd[:, cols] + spread_heads(carried, tile, width) * dot(maps, state, precision=HIGHEST)
        y_out[:, cols] = y
        g = gate[:, cols]
        gated = y * (g * sigmoid(g))
        gn_out[:, cols] = gated * gain[0:1, cols]
        total = gated * gated if tile == 0 else total + gated * gated
    squares[...] = dot(ones, total, NT, HIGHEST)


def open_kernel(
    width, q, y, gate, gain, factors, bc, cum, chdec, dy_out, dgate, u_out, dgain, adjoint, local, passed
):
    inner = q.shape[1]
    n = bc.shape[1] // 2
    c = pl.program_id(0)

    @pl.when(c == 0)
    def _():
        dgain[...] = jnp.zeros_like(dgain)
        local[...] = jnp.zeros_like(local)
        passed[...] = jnp.ones_like(passed)

    carried = jnp.exp(cum[...])
    maps = bc[:, n:].T
    turned = factors[...].T
    s = turned[:, 0:1]
    t = turned[:, 1:2]
    for tile in range(inner // LANES):
        cols = slice(tile * LANES, (tile + 1) * LANES)
        g = gate[:, cols]
        soft = sigmoid(g)
        silu = g * soft
        out = y[:, cols]
        gated = out * silu
        grad = q[:, cols]
        scaled = gated * s
        u_out[:, cols] = scaled * gain[0:1, cols]
        dgain[:, cols] = dgain[:, cols] + (grad * scaled).reshape(CHUNK // PAD, PAD, LANES).sum(axis=0)
        dgated = s * (grad * gain[0:1, cols]) - t * gated
        dgate[:, cols] = dgated * out * (soft + silu * (1.0 - soft))
        dy = dgated * silu
        dy_out[:, cols] = dy
        part = dot(maps, dy * spread_heads(carried, tile, width))
        adjoint[0, :, cols] = part
        local[:, cols] = local[:, cols] + passed[0:1, cols] * part
    passed[...] = passed[...] * chdec[0]


def back_kernel(width, dy, v, bc, dt, cum, cumt, states, du, dbc, gram):
    inner = v.shape[1]
    n = bc.shape[1] // 2
    each = LANES // width
    lane = lax.broadcasted_iota(jnp.int32, (CHUNK, LANES), 1)
    upper = lax.broadcasted_iota(jnp.int32, (CHUNK, CHUNK), 0) <= lax.broadcasted_iota(
        jnp.int32, (CHUNK, CHUNK), 1
    )
    inputs, outputs = bc[:, :n], bc[:, n:]
    meet = dot(inputs, outputs, NT)
    carried = jnp.exp(cum[...])
    grad_out = None
    for tile in range(inner // LANES):
        cols = slice(tile * LANES, (tile + 1) * LANES)
        grad = dy[:, cols]
        stepped = v[:, cols] * spread_heads(dt[...], tile, width)
        result = None
        for k in range(each):
            head = tile * each + k
            spread = cumt[head : head + 1, :] - cum[:, head : head + 1]
            decay = jnp.exp(jnp.where(upper, spread, NEG))
            part = dot(decay * meet, grad)
            result = part if k == 0 else jnp.where(lane < k * width, result, part)
            own = (lane >= k * width) & (lane < (k + 1) * width)
            cross = decay * dot(jnp.where(own, stepped, 0.0), grad, NT)
            first = tile == 0 and k == 0
            gram[...] = cross if first else gram[...] + cross
        du[:, cols] = result
        part = dot(grad * spread_heads(carried, tile, width), states[0, :, cols], NT)
        grad_out = part if tile == 0 else grad_out + part
    total = gram[...]
    dbc[:, :n] = dot(total, outputs)
    dbc[:, n:] = grad_out + dot(total.T, inputs)


def head_totals(product, width):
    each = LANES // width
    lane = lax.broadcasted_iota(jnp.int32, product.shape, 1)
    result = []
    for k in range(each):
        own = (lane >= k * width) & (lane < (k + 1) * width)
        result.append(jnp.sum(jnp.where(own, product, 0.0), axis=1, keepdims=True))
    return result


def place_heads(columns, shape):
    lane = lax.broadcasted_iota(jnp.int32, shape, 1)
    result = jnp.zeros(shape, F32)
    for head, column in enumerate(columns):
        result = jnp.where(lane == head, column, result)
    return result


def close_kernel(
    width, dy, y, v, du, dsi, adjoint, bc, dt, cum, sp, hp, dbc, dss, chdec, final, later,
    dti, dts, dstep, rows, leaving, running,
):
    inner = v.shape[1]
    n = bc.shape[1] // 2
    heads_rate = -jnp.exp(hp[1:2, :])

    @pl.when(pl.program_id(0) == 0)
    def _():
        crossing = jnp.sum(final[...] * later[...], axis=0, keepdims=True)
        columns = []
        for tile in range(inner // LANES):
            columns += head_totals(crossing[:, tile * LANES : (tile + 1) * LANES], width)
        running[...] = jnp.broadcast_to(place_heads(columns, (1, LANES)), running.shape)
        leaving[...] = later[...]
        rows[...] = jnp.zeros_like(rows)

    ones = (
        lax.broadcasted_iota(jnp.int32, (CHUNK, CHUNK), 0)
        <= lax.broadcasted_iota(jnp.int32, (CHUNK, CHUNK), 1)
    ).astype(F32)
    step = dt[...]
    cums = cum[...]
    fade = jnp.exp(cums[CHUNK - 1 : CHUNK, :] - cums)
    inputs = bc[:, :n]
    grad_in = dbc[:, :n]
    own, direct = [], []
    for tile in range(inner // LANES):
        cols = slice(tile * LANES, (tile + 1) * LANES)
        adj = leaving[:, cols]
        wide_fade = spread_heads(fade, tile, width)
        wide_step = spread_heads(step, tile, width)
        skip = spread_heads(hp[2:3, :], tile, width)
        values = v[:, cols]
        grad = dy[:, cols]
        dstepped = du[:, cols] + wide_fade * dot(inputs, adj)
        grad_in = grad_in + dot(wide_fade * wide_step * values, adj, NT)
        dti[:, cols] = (wide_step * dstepped + skip * grad) * dsi[:, cols]
        own += head_totals(grad * (y[:, cols] - skip * values), width)
        direct += head_totals(values * dstepped, width)
        part = (grad * values).reshape(CHUNK // PAD, PAD, LANES).sum(axis=0)
        rows[0:PAD, cols] = rows[0:PAD, cols] + part
        leaving[:, cols] = adjoint[0, :, cols] + chdec[0, 0:1, cols] * adj
    dts[:, :n] = grad_in * dss[:, :n]
    dts[:, n:] = dbc[:, n:] * dss[:, n:]
    direct = place_heads(direct, (CHUNK, LANES))
    dcum = place_heads(own, (CHUNK, LANES)) - step * direct
    drate = dot(ones, dcum, precision=HIGHEST) + running[0:1, :]
    running[...] = jnp.broadcast_to(drate[0:1, :], running.shape)
    dstep_value = direct + drate * heads_rate
    raw = sp[:, 2 * n :] + hp[0:1, :]
    grad_raw = dstep_value * sigmoid(raw)
    dstep[...] = grad_raw
    lanes = slice(0, LANES)
    rates = drate * heads_rate * step
    rows[PAD : 2 * PAD, lanes] = rows[PAD : 2 * PAD, lanes] + rates.reshape(
        CHUNK // PAD, PAD, LANES
    ).sum(axis=0)
    rows[2 * PAD : 3 * PAD, lanes] = rows[2 * PAD : 3 * PAD, lanes] + grad_raw.reshape(
        CHUNK // PAD, PAD, LANES
    ).sum(axis=0)


def filter_back_kernel(
    dti, hi, dts, hs, ip, pi, ib, sp, ps, sb, ti, ts, dip, dsp, ri, rs, padi, pads, padgi, padgs
):
    inner = ip.shape[1]
    states = dts.shape[1]
    place = pl.program_id(0)

    @pl.when(place == 0)
    def _():
        padgi[CHUNK:, :] = hi[...]
        padgs[CHUNK:, :] = hs[...]
        ri[...] = jnp.zeros_like(ri)
        rs[...] = jnp.zeros_like(rs)

    @pl.when(place > 0)
    def _():
        padgi[CHUNK:, :] = padgi[0:PAD, :]
        padgs[CHUNK:, :] = padgs[0:PAD, :]

    @pl.when(place == pl.num_programs(0) - 1)
    def _():
        padi[0:PAD, :] = ib[...]
        pads[0:PAD, :] = sb[...]

    @pl.when(place < pl.num_programs(0) - 1)
    def _():
        padi[0:PAD, :] = pi[...]
        pads[0:PAD, :] = ps[:, :states]

    padi[PAD:, :] = ip[...]
    pads[PAD:, :] = sp[:, :states]
    padgi[0:CHUNK, :] = dti[...]
    padgs[0:CHUNK, :] = dts[...]
    rows = 64

    def folded(value):
        return value.reshape(rows // PAD, PAD, LANES).sum(axis=0)

    def step(number, _):
        start = pl.multiple_of(number * rows, rows)
        for signal, grads, taps, out, sums, size in (
            (padi, padgi, ti, dip, ri, inner),
            (pads, padgs, ts, dsp, rs, states),
        ):
            for tile in range(size // LANES):
                cols = slice(tile * LANES, (tile + 1) * LANES)
                ahead = grads[pl.ds(start, rows + PAD), cols]
                grad = ahead[:rows]
                before = signal[pl.ds(start, rows + PAD), cols]
                total = taps[3:4, cols] * grad
                sums[3 * PAD : 4 * PAD, cols] = sums[3 * PAD : 4 * PAD, cols] + folded(grad * before[PAD:])
                sums[4 * PAD : 5 * PAD, cols] = sums[4 * PAD : 5 * PAD, cols] + folded(grad)
                for back in range(1, 4):
                    tap = 3 - back
                    total = total + taps[tap : tap + 1, cols] * pltpu.roll(ahead, rows + PAD - back, 0)[:rows]
                    place = slice(tap * PAD, (tap + 1) * PAD)
                    sums[place, cols] = sums[place, cols] + folded(
                        grad * pltpu.roll(before, back, 0)[PAD:]
                    )
                out[pl.ds(start, rows), cols] = total
        return 0

    lax.fori_loop(0, CHUNK // rows, step, 0)


def matmul(left, right, dims=((1,), (0,)), precision=HIGH):
    return lax.dot_general(left, right, (dims, ((), ())), precision=precision)


def padded_rows(rows, lanes):
    rows = jnp.concatenate(rows, axis=0)
    return jnp.pad(rows, ((0, PAD - rows.shape[0]), (0, lanes - rows.shape[1])))


def forward(current, w, first, taps, beside):
    length = current.shape[0]
    inner = w["inner"].shape[1]
    heads = w["heads"]
    width = inner // heads
    states = w["states"]
    n = states // 2
    chunks = length // CHUNK
    root = lax.rsqrt(jnp.mean(current * current, axis=-1, keepdims=True) + epsilon)
    normed = current * root * w["pre_gain"][None, :]
    if first:
        whole = matmul(normed, w["state"], precision=HIGHEST)
        whole = jnp.concatenate([whole, taps], axis=0)
        ip = matmul(after(normed, whole), w["inner"], precision=HIGHEST)
        if power_of_two(lax.axis_size("head")):
            wait = whole
            for distance in distances("head"):
                other = exchanged(whole, "head", distance)
                if distance == 1:
                    other, ip = tied(other, ip)
                    wait = other
                whole = joined(whole, other, "head", distance, 1)
        else:
            whole = gathered_columns(whole)
            wait = whole
        gate = matmul(after(normed, wait), w["gate"], precision=HIGHEST)
        whole, gate = tied(whole, gate)
        taps = whole[length:]
        sp = whole[:length]
    else:
        ip = matmul(normed, w["inner"])
        sp = matmul(normed, w["maps"], NT, HIGHEST)
        gate = None
    border = shifted(
        jnp.concatenate([ip[length - PAD :], sp[length - PAD :, :states]], axis=1), "seq", 1
    )
    if first:
        step = matmul(after(normed, sp), w["step"], precision=HIGHEST)
        border, step = tied(border, step)
        sp = jnp.concatenate([sp, step], axis=1)
    else:
        gate = matmul(after(normed, ip, sp), w["gate"])
        border, gate = tied(border, gate)
    ib, sb = border[:, :inner], border[:, inner:]
    taps_s = taps[w["layer"] * PAD : (w["layer"] + 1) * PAD]
    b_inner, b_states, b_lanes = (rows_of(CHUNK, size) for size in (inner, states, LANES))
    b_heads, b_sp = columns_of(16, CHUNK), rows_of(CHUNK, states + LANES)
    b_block, b_state = rows_of(1, n, inner), all_of(n, inner)
    b_decay = rows_of(1, PAD, inner)
    v, bc, dsi, dss, dt, cum, cumt, fresh, local, chdec, decay = call(
        functools.partial(start_kernel, width),
        chunks,
        [
            ((length, inner), b_inner),
            ((length, states), b_states),
            ((length, inner), b_inner),
            ((length, states), b_states),
            ((length, LANES), b_lanes),
            ((length, LANES), b_lanes),
            ((16, length), b_heads),
            ((chunks, n, inner), b_block),
            ((n, inner), b_state),
            ((chunks, PAD, inner), b_decay),
            ((PAD, inner), all_of(PAD, inner)),
        ],
        [pltpu.VMEM((CHUNK + PAD, inner), F32), pltpu.VMEM((CHUNK + PAD, states), F32)],
        2 * 3 * length * n * inner,
        (ip, b_inner),
        (ib, all_of(PAD, inner)),
        (sp, b_sp),
        (sb, all_of(PAD, states)),
        (w["taps_i"], all_of(PAD, inner)),
        (taps_s, all_of(PAD, states)),
        (w["heads_rows"], all_of(PAD, LANES)),
        vmem=LARGE,
    )
    decay = decay[0:1]

    def inside(before, done):
        return call(
            functools.partial(inner_kernel, width),
            chunks,
            [((length, inner), b_inner)],
            [],
            2 * 6 * length * CHUNK * inner,
            (v, b_inner),
            (bc, b_states),
            (dt, b_lanes),
            (cum, b_lanes),
            (cumt, b_heads),
            (w["heads_rows"], all_of(PAD, LANES)),
            vmem=LARGE,
        )

    def aside(before, done):
        return [beside]

    entering, ((yd,), (beside,)) = state_before(local, decay, False, [inside, aside])
    y, gn, carried, squares, final = call(
        functools.partial(gate_kernel, width),
        chunks,
        [
            ((length, inner), b_inner),
            ((length, inner), b_inner),
            ((chunks, n, inner), b_block),
            ((PAD, length), columns_of(PAD, CHUNK)),
            ((n, inner), b_state),
        ],
        [],
        2 * 3 * length * n * inner,
        (yd, b_inner),
        (bc, b_states),
        (cum, b_lanes),
        (fresh, b_block),
        (chdec, b_decay),
        (entering, b_state),
        (gate, b_inner),
        (w["norm_gain"][None, :], all_of(1, inner)),
    )
    saved = dict(
        current=current, root=root, normed=normed, ip=ip, sp=sp, ib=ib, sb=sb, gate=gate, v=v, bc=bc,
        dsi=dsi, dss=dss, dt=dt, cum=cum, cumt=cumt, fresh=fresh, chdec=chdec, decay=decay, y=y,
        gn=gn, states=carried, taps_s=taps_s, final=final,
    )
    return gn, squares[0:1], saved, taps, beside


def core_products(left, right):
    place = lax.axis_index("dp")
    if lax.axis_size("dp") != 2:
        total = matmul(left, right, ((0,), (0,)))
        return total, total
    return (
        matmul(left, half(right, 1 - place, 1), ((0,), (0,))),
        matmul(left, half(right, place, 1), ((0,), (0,))),
    )


def over_cores(sent, kept):
    if lax.axis_size("dp") != 2:
        return lax.psum(kept, "dp")
    return kept + exchanged(sent, "dp", 1)


def pair_kernel(one, a, two, b, sent, kept):
    width = a.shape[1] // 2
    first = lax.axis_index("dp") == 0
    for number, (left, right) in enumerate(((one, a), (two, b))):
        product = dot(left[...].T, right[...])
        cols = slice(number * width, (number + 1) * width)
        sent[:, cols] = jnp.where(first, product[:, width:], product[:, :width])
        kept[:, cols] = jnp.where(first, product[:, :width], product[:, width:])


def pair_products(one, a, two, b):
    length, model = one.shape
    inner = a.shape[1]
    tile = 256
    out = ((model, inner), rows_of(tile, inner))
    return call(
        pair_kernel,
        model // tile,
        [out, out],
        [],
        4 * length * model * inner,
        (one, columns_of(length, tile)),
        (a, all_of(length, inner)),
        (two, columns_of(length, tile)),
        (b, all_of(length, inner)),
        vmem=LARGE,
    )


def last_kernel(left, right, small, sent, kept):
    width = right.shape[1] // 2
    rows = left.shape[1]
    first = lax.axis_index("dp") == 0
    turned = left[...].T
    product = dot(turned, right[...])
    sent[0, :rows, :] = jnp.where(first, product[:, width:], product[:, :width])
    kept[0, :rows, :] = jnp.where(first, product[:, :width], product[:, width:])
    below = dot(small[...].T, left[...])
    size = SMALL // 2
    sent[0, rows:, :] = jnp.where(first, below[size : 2 * size], below[:size])
    kept[0, rows:, :] = jnp.where(first, below[:size], below[size : 2 * size])


def last_products(left, right, small):
    length, model = left.shape
    inner = right.shape[1]
    shards = lax.axis_size("seq")
    rows = model // shards
    out = ((shards, rows + SMALL // 2, inner // 2), rows_of(1, rows + SMALL // 2, inner // 2))
    return call(
        last_kernel,
        shards,
        [out, out],
        [],
        2 * length * model * (inner + LANES),
        (left, columns_of(length, rows)),
        (right, all_of(length, inner)),
        (small, all_of(length, LANES)),
    )


def over_seq(total):
    return lax.psum_scatter(total, "seq", scatter_dimension=0, tiled=True)


def place_kernel(*refs):
    *parts, out = refs
    first = lax.axis_index("dp") == 0
    width = out.shape[2] // 2
    for layer in range(len(parts) // 2):
        mine, other = parts[2 * layer], parts[2 * layer + 1]

        @pl.when(first)
        def _():
            out[layer, :, :width] = mine[...]
            out[layer, :, width:] = other[...]

        @pl.when(jnp.logical_not(first))
        def _():
            out[layer, :, :width] = other[...]
            out[layer, :, width:] = mine[...]


def cores_joined(pairs, start, width, rows):
    if lax.axis_size("dp") != 2:
        return jnp.stack([mine[:rows, start : start + width] for mine, _ in pairs], axis=0)
    pieces = [piece for pair in pairs for piece in pair]
    tile = 96 if rows % 96 == 0 else rows
    return pl.pallas_call(
        place_kernel,
        grid=(rows // tile,),
        out_shape=jax.ShapeDtypeStruct((len(pairs), rows, 2 * width), F32),
        in_specs=[pl.BlockSpec((tile, width), lambda i: (i, start // width))] * len(pieces),
        out_specs=pl.BlockSpec((len(pairs), tile, 2 * width), lambda i: (0, i, 0)),
        compiler_params=pltpu.CompilerParams(vmem_limit_bytes=24 * 1024 * 1024),
    )(*pieces)


def backward(grad, q, scale, slope, w, saved, beside, waiting, earlier, final):
    s = saved
    length, inner = q.shape
    width = inner // w["heads"]
    states = w["states"]
    n = states // 2
    chunks = length // CHUNK
    factors = jnp.pad(jnp.concatenate([scale, slope], axis=0), ((0, PAD - 2), (0, 0)))
    b_inner, b_states, b_lanes = (rows_of(CHUNK, size) for size in (inner, states, LANES))
    b_heads, b_sp = columns_of(16, CHUNK), rows_of(CHUNK, states + LANES)
    b_block, b_state = rows_of(1, n, inner), all_of(n, inner)
    b_decay = rows_of(1, PAD, inner)
    dy, dgate, u, dgain, adjoint, local = call(
        functools.partial(open_kernel, width),
        chunks,
        [
            ((length, inner), b_inner),
            ((length, inner), b_inner),
            ((length, inner), b_inner),
            ((PAD, inner), all_of(PAD, inner)),
            ((chunks, n, inner), b_block),
            ((n, inner), b_state),
        ],
        [pltpu.VMEM((PAD, inner), F32)],
        2 * 3 * length * n * inner,
        (q, b_inner),
        (s["y"], b_inner),
        (s["gate"], b_inner),
        (w["norm_gain"][None, :], all_of(1, inner)),
        (factors, columns_of(PAD, CHUNK)),
        (s["bc"], b_states),
        (s["cum"], b_lanes),
        (s["chdec"], b_decay),
    )

    def cross(before, done):
        if lax.axis_size("dp") == 2:
            result = pair_products(grad, after(u, before), s["normed"], dgate)
        else:
            result = [
                jnp.concatenate(both, axis=1)
                for both in zip(core_products(grad, u), core_products(s["normed"], dgate))
            ]
        if waiting is not None:
            result = (*result, waiting)
        return beside.advance(*result) if beside is not None else result

    def inside(before, done):
        result = call(
            functools.partial(back_kernel, width),
            chunks,
            [((length, inner), b_inner), ((length, states), b_states)],
            [pltpu.VMEM((CHUNK, CHUNK), F32)],
            2 * 15 * length * CHUNK * inner,
            (after(dy, before), b_inner),
            (s["v"], b_inner),
            (s["bc"], b_states),
            (s["dt"], b_lanes),
            (s["cum"], b_lanes),
            (s["cumt"], b_heads),
            (s["states"], b_block),
        )
        return beside.advance(*result) if beside is not None else result

    def summed(before, done):
        result = [over_cores(*done[0][:2])]
        return beside.advance(*result) if beside is not None else result


    later, (_, (du, dbc), (pair, *_)) = state_before(local, s["decay"], True, [cross, inside, summed])
    pair = over_seq(pair)
    dti, dts, dstep, rows = call(
        functools.partial(close_kernel, width),
        chunks,
        [
            ((length, inner), b_inner),
            ((length, states), b_states),
            ((length, LANES), b_lanes),
            ((3 * PAD, inner), all_of(3 * PAD, inner)),
        ],
        [pltpu.VMEM((n, inner), F32), pltpu.VMEM((PAD, LANES), F32)],
        2 * 6 * length * n * inner,
        (dy, b_inner),
        (s["y"], b_inner),
        (s["v"], b_inner),
        (du, b_inner),
        (s["dsi"], b_inner),
        (adjoint, b_block),
        (s["bc"], b_states),
        (s["dt"], b_lanes),
        (s["cum"], b_lanes),
        (s["sp"], b_sp),
        (w["heads_rows"], all_of(PAD, LANES)),
        (dbc, b_states),
        (s["dss"], b_states),
        (s["chdec"], b_decay),
        (s["final"], b_state),
        (later, b_state),
        backward=True,
        vmem=LARGE,
    )
    if beside is not None:
        dti, dts = beside.advance(dti, dts)
    halo = shifted(jnp.concatenate([dti[:PAD], dts[:PAD]], axis=1), "seq", -1)
    base = matmul(after(dgate, dti), w["gate"], NT)
    halo, base = tied(halo, base)
    def edge(size):
        return pl.BlockSpec((PAD, size), lambda c: (jnp.maximum(c * (CHUNK // PAD) - 1, 0), 0))

    dip, dsp, ri, rs = call(
        filter_back_kernel,
        chunks,
        [
            ((length, inner), b_inner),
            ((length, states), b_states),
            ((5 * PAD, inner), all_of(5 * PAD, inner)),
            ((5 * PAD, states), all_of(5 * PAD, states)),
        ],
        [pltpu.VMEM((CHUNK + PAD, size), F32) for size in (inner, states, inner, states)],
        16 * length * inner,
        (dti, b_inner),
        (halo[:, :inner], all_of(PAD, inner)),
        (dts, b_states),
        (halo[:, inner:], all_of(PAD, states)),
        (s["ip"], b_inner),
        (s["ip"], edge(inner)),
        (s["ib"], all_of(PAD, inner)),
        (s["sp"], b_sp),
        (s["sp"], edge(states + LANES)),
        (s["sb"], all_of(PAD, states)),
        (w["taps_i"], all_of(PAD, inner)),
        (s["taps_s"], all_of(PAD, states)),
        backward=True,
    )
    gains = []

    def product(base, dip, dmaps, scaled):
        total = base + matmul(dip, w["inner"], NT) + matmul(dmaps, w["maps"])
        gains.append(jnp.sum(total * scaled, axis=0))
        return total

    def finish(rows_grad, offset):
        def take(array):
            return lax.dynamic_slice_in_dim(array, offset, rows_grad.shape[0], 0)

        x, root = take(s["current"]), take(s["root"])
        scaled = rows_grad * w["pre_gain"][None, :]
        along = jnp.mean(scaled * x, axis=-1, keepdims=True)
        return root * scaled - x * (root * root * root * along)

    shared = dsp
    own = states // lax.axis_size("head")
    lefts = [base, dip, jnp.concatenate([dsp, dstep], axis=1), s["current"] * s["root"]]
    if power_of_two(lax.axis_size("head")):
        way = distances("head")[::-1]
        for number, distance in enumerate(way):
            bit = bit_of("head", distance)
            other = exchanged(half(shared, 1 - bit, 1), "head", distance)
            if number == 0:
                steps = Steps(head_sum(lefts, product, finish))
                (other,) = steps.advance(other)
            shared = half(shared, bit, 1) + other
    else:
        shared = lax.psum_scatter(shared, "head", scatter_dimension=1, tiled=True)
        steps = Steps(head_sum(lefts, product, finish))
        steps.advance()
    def folded(array):
        return array.reshape(-1, PAD, array.shape[1]).sum(axis=1)

    ri, rs, rows = folded(ri), folded(rs), folded(rows)
    over_heads = jnp.concatenate([gains[0] + gains[1], rs.reshape(-1)])
    flat = jnp.concatenate(
        [ri.reshape(-1), dgain.sum(axis=0), rows[0], rows[1, :LANES], rows[2, :LANES]]
    )
    small_parts = [*earlier, (over_heads, flat)]
    (dip,) = steps.advance(dip)
    if final:
        over_heads = jnp.concatenate([part[0] for part in small_parts])
        over_heads = small_sum(after(over_heads, dip), "head")
    shards = lax.axis_size("seq")
    model = s["normed"].shape[1]
    small = jnp.concatenate([shared, dstep[:, : LANES - own]], axis=1)
    if lax.axis_size("dp") == 2 and model // shards % LANES == 0:
        sent, kept = last_products(s["normed"], dip, small)
        if final:
            sent, pair = tied(sent, pair)
        last = over_cores(sent, kept)
    else:
        last = over_cores(*core_products(s["normed"], dip)).reshape(shards, -1, inner // lax.axis_size("dp"))
        small = matmul(small[:, :SMALL], s["normed"], ((0,), (0,)))
        small = jnp.transpose(small.reshape(SMALL, shards, -1), (1, 0, 2))
        if lax.axis_size("dp") == 2:
            place = lax.axis_index("dp")
            small = over_cores(half(small, 1 - place, 1), half(small, place, 1))
        else:
            small = lax.psum(small, "dp")
        small = jnp.pad(small, ((0, 0), (0, 0), (0, last.shape[2] - small.shape[2])))
        last = jnp.concatenate([last, small], axis=1)
    last = last.reshape(-1, last.shape[2])
    if final:
        (last,) = steps.advance(last)
    else:
        last, pair = steps.advance(last, pair)
    last = over_seq(after(last, pair))
    if not final:
        branch = steps.finished()
        return grad + branch, pair, last, small_parts, own
    (over_heads,) = steps.advance(over_heads)
    flat = jnp.concatenate([over_heads] + [part[1] for part in small_parts])
    flat = small_sum(small_sum(flat, "dp"), "seq")
    flat, last = steps.advance(flat, last)
    branch = steps.finished()
    sizes = (small_parts[0][0].size, small_parts[0][1].size)
    return grad + branch, pair, last, (flat, sizes), own


def small_grads(over_heads, flat, own, w):
    model, inner = w["inner"].shape
    states = w["states"]
    heads = w["heads"]
    g_pre, g_rs = over_heads[:model], over_heads[model:]
    cut = []
    start = 0
    for size in (5 * inner, inner, inner, LANES, LANES):
        cut.append(flat[start : start + size])
        start += size
    g_ri, g_norm, g_skip, g_rate, g_bias = cut
    g_rs = lax.dynamic_slice_in_dim(g_rs.reshape(5, states), lax.axis_index("head") * own, own, 1)
    g_ri = g_ri.reshape(5, inner)
    return (
        g_pre,
        g_ri[:4],
        g_ri[4],
        g_rs[:4],
        g_rs[4],
        g_bias[:heads],
        g_rate[:heads],
        g_skip.reshape(heads, -1).sum(axis=1),
        g_norm,
    )


def gathered_columns(value):
    if not power_of_two(lax.axis_size("head")):
        return lax.all_gather(value, "head", axis=1, tiled=True)
    return gather_back(value, "head", distances("head")[::-1], 1)


def body(
    tokens,
    cotangent,
    pre_gain,
    gate_weight,
    inner_weight,
    state_weight,
    step_weight,
    filter_inner,
    filter_inner_bias,
    filter_state,
    filter_state_bias,
    step_bias,
    log_rate,
    skip_gain,
    norm_gain,
    out_weight,
):
    layers = pre_gain.shape[0]
    heads = step_bias.shape[1]
    inner = gate_weight.shape[2]
    taps = jnp.concatenate([filter_state, filter_state_bias[:, None, :]], axis=1)
    taps = jnp.pad(taps, ((0, 0), (0, PAD - taps.shape[1]), (0, 0))).reshape(layers * PAD, -1)
    weights = []
    for layer in range(layers):
        steps = jnp.pad(step_weight[layer], ((0, 0), (0, LANES - heads)))
        weights.append(
            dict(
                layer=layer,
                heads=heads,
                states=state_weight.shape[2] * lax.axis_size("head"),
                pre_gain=pre_gain[layer],
                gate=gate_weight[layer],
                inner=inner_weight[layer],
                state=state_weight[layer],
                step=steps,
                out=out_weight[layer],
                norm_gain=norm_gain[layer],
                taps_i=padded_rows([filter_inner[layer], filter_inner_bias[layer][None]], inner),
                heads_rows=padded_rows(
                    [step_bias[layer][None], log_rate[layer][None], skip_gain[layer][None]], LANES
                ),
            )
        )
    maps = jnp.concatenate([state_weight[layer].T for layer in range(layers)], axis=1)
    maps = lax.all_gather(maps, "head", axis=0, tiled=True)
    current = tokens[0]
    grad = cotangent[0]
    kept = []
    extra = None
    for layer in range(layers):
        w = weights[layer]
        gn, squares, saved, taps, maps = forward(current, w, layer == 0, taps, maps)
        if layer == 0:
            for number, other in enumerate(weights):
                size = other["inner"].shape[0]
                cut = maps[:, number * size : (number + 1) * size]
                other["maps"] = jnp.concatenate([cut, other["step"].T], axis=0)
        last = layer == layers - 1
        if last:
            both = jnp.concatenate([squares, jnp.sum(extra * gn, axis=1)[None, :]], axis=0)
            both = small_sum(both, "head")
            squares, along = both[0:1], both[1:2]
        else:
            squares = small_sum(squares, "head")
        scale = lax.rsqrt(squares / INNER + epsilon)

        def finish(rows, offset, scale=scale):
            return rows * lax.dynamic_slice_in_dim(scale[0], offset, rows.shape[0], 0)[:, None]

        steps = Steps(head_sum([gn], lambda rows, w=w, p=HIGH if last else HIGHEST: matmul(rows, w["out"], NT, p), finish))
        if last:
            scale = after(scale, steps.now)
        if layer == 0:
            product = matmul(after(grad, steps.now), weights[layers - 1]["out"])
            if not last:
                steps.advance()
                (product,) = steps.advance(product)
            extra = product
        branch = None if last else steps.finished()
        kept.append((saved, scale, branch))
        if not last:
            current = current + branch
    collected = [None] * layers
    waiting = None
    earlier = []
    for layer in reversed(range(layers)):
        w = weights[layer]
        saved, scale, branch = kept[layer]
        if layer < layers - 1:
            if layer == layers - 2:
                (grad,) = steps.advance(grad)
            q = matmul(grad, w["out"])
            slope = jnp.sum(grad * branch, axis=1)[None, :] * scale * scale / INNER
        else:
            q = extra
            slope = along * scale * scale * scale / INNER
        grad, *collected[layer] = backward(
            grad, q, scale, slope, w, saved, steps if layer == layers - 2 else None, waiting, earlier, layer == 0
        )
        waiting = collected[layer][1]
        earlier = collected[layer][2]
    current = current + steps.finished()
    flat, (size, rest) = earlier
    results = []
    for layer in range(layers):
        number = layers - 1 - layer
        start = layers * size + number * rest
        results.append(
            small_grads(
                flat[number * size : (number + 1) * size],
                flat[start : start + rest],
                collected[layer][3],
                weights[layer],
            )
        )
    stacked = [jnp.stack([entry[number] for entry in results], axis=0) for number in range(9)]
    two = lax.axis_size("dp") == 2

    def with_other(part):
        return part, exchanged(part, "dp", 1) if two else part

    pairs = [[with_other(entry[0]) for entry in collected]]
    half_width = inner // 2 if two else inner
    rows = gate_weight.shape[1] // lax.axis_size("seq")
    large = {
        "out": cores_joined(pairs[0], 0, half_width, rows),
        "gate": cores_joined(pairs[0], half_width, half_width, rows),
    }
    collected[0][1], current, grad, stacked, large = tied(
        collected[0][1], current, grad, stacked, large
    )
    pairs.append([with_other(entry[1]) for entry in collected])
    large["inner"] = cores_joined(pairs[1], 0, half_width, rows)
    small = []
    for mine, other in pairs[1]:
        mine, other = mine[rows:, :rows], other[rows:, :rows]
        if two:
            mine = jnp.concatenate(
                [jnp.where(lax.axis_index("dp") == 0, a, b) for a, b in ((mine, other), (other, mine))],
                axis=0,
            )
        small.append(mine.T)
    small = jnp.stack(small, axis=0)
    own = collected[0][3]
    return (
        current[None],
        grad[None],
        stacked[0],
        large["gate"],
        large["inner"],
        small[:, :, :own],
        small[:, :, own : own + heads],
        *stacked[1:],
        large["out"],
    )


def solution(mesh):
    placed = (
        P("dp", "seq", None),
        P("dp", "seq", None),
        P(),
        P(None, None, "head"),
        P(None, None, "head"),
        P(None, None, "head"),
        P(None, None, "head"),
        P(None, None, "head"),
        P(None, "head"),
        P(None, None, "head"),
        P(None, "head"),
        P(None, "head"),
        P(None, "head"),
        P(None, "head"),
        P(None, "head"),
        P(None, None, "head"),
    )
    return jax.shard_map(
        body,
        mesh=mesh,
        in_specs=placed,
        out_specs=(
            P("dp", "seq", None),
            P("dp", "seq", None),
            P(),
            P(None, "seq", "head"),
            P(None, "seq", "head"),
            P(None, "seq", "head"),
            P(None, "seq", "head"),
            P(None, None, "head"),
            P(None, "head"),
            P(None, None, "head"),
            P(None, "head"),
            P(None, "head"),
            P(None, "head"),
            P(None, "head"),
            P(None, "head"),
            P(None, "seq", "head"),
        ),
        check_vma=False,
    )
```

```python
import functools

import jax
import jax.numpy as jnp
from jax import lax
from jax.experimental import pallas as pl
from jax.experimental.pallas import tpu as pltpu
from jax.sharding import PartitionSpec as P

INNER = 3072
CHUNK = 128
LANES = 128
PAD = 8
SMALL = 96
COST = 4
VMEM = 20 * 1024 * 1024
LARGE = 56 * 1024 * 1024
epsilon = 1e-05
HIGH = lax.Precision.HIGH
HIGHEST = lax.Precision.HIGHEST
NEG = -1e30
F32 = jnp.float32


def power_of_two(n):
    return n & (n - 1) == 0


def exchanged(value, axis, distance):
    n = lax.axis_size(axis)
    return lax.ppermute(value, axis, [(i, i ^ distance) for i in range(n)])


def shifted(value, axis, step):
    n = lax.axis_size(axis)
    pairs = [(i, i + step) for i in range(n) if 0 <= i + step < n]
    return lax.ppermute(value, axis, pairs)


def distances(axis):
    n = lax.axis_size(axis)
    return [1 << k for k in range(n.bit_length() - 1)]


def bit_of(axis, distance):
    return (lax.axis_index(axis) // distance) % 2


def small_sum(value, axis):
    if not power_of_two(lax.axis_size(axis)):
        return lax.psum(value, axis)
    for distance in distances(axis):
        value = value + exchanged(value, axis, distance)
    return value


def half(value, which, dim=0):
    size = value.shape[dim] // 2
    return lax.dynamic_slice_in_dim(value, which * size, size, dim)


def joined(mine, other, axis, distance, dim=0):
    first = bit_of(axis, distance) == 0
    return jnp.concatenate(
        [jnp.where(first, mine, other), jnp.where(first, other, mine)], axis=dim
    )


def gather_back(value, axis, order, dim=0):
    for distance in order[::-1]:
        value = joined(value, exchanged(value, axis, distance), axis, distance, dim)
    return value


def tied(value, *others):
    return lax.optimization_barrier((value, *others))


def head_sum(lefts, product, finish):
    order = distances("head")
    rows = lefts[0].shape[0] // 2
    ways = (order, order[::-1])

    def chosen(other):
        picked = []
        for array in lefts:
            pieces = []
            for number, way in enumerate(ways):
                bit = bit_of("head", way[0])
                part = array[number * rows : (number + 1) * rows]
                pieces.append(half(part, 1 - bit if other else bit))
            picked.append(jnp.concatenate(pieces, axis=0))
        return product(*picked)

    sent = chosen(True)
    kept = chosen(False)
    sent, kept = yield sent, kept
    size = rows // 2
    got = [
        exchanged(sent[number * size : (number + 1) * size], "head", way[0])
        for number, way in enumerate(ways)
    ]
    kept = [kept[:size], kept[size:]]
    offsets = [bit_of("head", way[0]) * size + number * rows for number, way in enumerate(ways)]
    got, kept = yield got, kept
    for step in range(1, len(order)):
        bits = [bit_of("head", way[step]) for way in ways]
        sends = [half(k, 1 - bit) + half(g, 1 - bit) for k, g, bit in zip(kept, got, bits)]
        arrived = [exchanged(send, "head", way[step]) for send, way in zip(sends, ways)]
        kept = [half(k, bit) + half(g, bit) for k, g, bit in zip(kept, got, bits)]
        offsets = [o + bit * k.shape[0] for o, bit, k in zip(offsets, bits, kept)]
        got, kept = yield arrived, kept
    mine = [finish(k + g, o) for k, g, o in zip(kept, got, offsets)]
    for step in range(len(order) - 1, -1, -1):
        others = [exchanged(m, "head", way[step]) for m, way in zip(mine, ways)]
        others, mine = yield others, mine
        mine = [joined(m, o, "head", way[step]) for m, o, way in zip(mine, others, ways)]
    return jnp.concatenate(mine, axis=0)


class Steps:
    def __init__(self, steps):
        self.steps = steps
        self.now = next(steps)
        self.result = None

    def advance(self, *others):
        if self.result is not None:
            return others
        if len(others) > 0:
            self.now, *others = tied(self.now, *others)
        try:
            self.now = self.steps.send(self.now)
        except StopIteration as end:
            self.result = end.value
        return others

    def finished(self):
        while self.result is None:
            self.advance()
        return self.result


def after(value, *others):
    return tied(value, *others)[0]


def state_before(local, decay, reverse, windows):
    n = lax.axis_size("seq")
    done = []
    arrived = []
    before = local
    for hop in range(n - 1):
        source, target = (n - 1 - hop, n - 2 - hop) if reverse else (hop, hop + 1)
        leaving = local if hop == 0 else decay * before + local
        got = lax.ppermute(leaving, "seq", [(source, target)])
        if hop < len(windows):
            got, *result = tied(got, *windows[hop](before, done))
            done.append(result)
        before = got
        arrived.append(got)
    for window in windows[n - 1 :]:
        done.append(window(before, done))
    return sum(arrived) if len(arrived) > 0 else jnp.zeros_like(local), done


def rows_of(*shape):
    return pl.BlockSpec(shape, lambda c: (c,) + (0,) * (len(shape) - 1))


def columns_of(*shape):
    return pl.BlockSpec(shape, lambda c: (0, c))


def all_of(*shape):
    return pl.BlockSpec(shape, lambda c: (0,) * len(shape))


def reverse(spec, steps):
    index = spec.index_map
    return pl.BlockSpec(spec.block_shape, lambda c: index(steps - 1 - c))


def call(kernel, steps, outs, scratch, flops, *args, backward=False, vmem=VMEM):
    shapes = [jax.ShapeDtypeStruct(shape, F32) for shape, _ in outs]
    size = 4 * sum(a.size for a, _ in args) + 4 * sum(s.size for s in shapes)

    def spec(blocks):
        return reverse(blocks, steps) if backward else blocks

    return pl.pallas_call(
        kernel,
        grid=(steps,),
        out_shape=shapes,
        in_specs=[spec(blocks) for _, blocks in args],
        out_specs=[spec(blocks) for _, blocks in outs],
        scratch_shapes=scratch,
        compiler_params=pltpu.CompilerParams(vmem_limit_bytes=vmem),
        cost_estimate=pl.CostEstimate(flops=flops // COST, bytes_accessed=size // COST, transcendentals=0),
    )(*[a for a, _ in args])


def dot(left, right, dims=((1,), (0,)), precision=HIGH):
    return lax.dot_general(
        left, right, (dims, ((), ())), precision=precision, preferred_element_type=F32
    )


NT = ((1,), (1,))


def sigmoid(value):
    return 1.0 / (1.0 + jnp.exp(-value))


def spread_heads(columns, tile, width):
    each = LANES // width
    lane = lax.broadcasted_iota(jnp.int32, (columns.shape[0], LANES), 1)
    result = columns[:, tile * each : tile * each + 1]
    for k in range(1, each):
        result = jnp.where(lane < k * width, result, columns[:, tile * each + k : tile * each + k + 1])
    return jnp.broadcast_to(result, (columns.shape[0], LANES))


def head_rows(row, width, total):
    tiles = [spread_heads(row, tile, width) for tile in range(total // LANES)]
    return jnp.concatenate(tiles, axis=1)


def filter_tile(scratch, taps, start, rows, cols):
    block = scratch[pl.ds(start, rows + PAD), cols]
    total = taps[4:5, cols] + taps[3:4, cols] * block[PAD:]
    for back in range(1, 4):
        total = total + taps[3 - back : 4 - back, cols] * pltpu.roll(block, back, 0)[PAD:]
    return total


def start_kernel(
    width, ip, ib, sp, sb, ti, ts, hp, v_out, bc_out, dsi, dss, dt_out, cum_out, cumt_out, fresh, local, chdec, passed, padi, pads
):
    inner = ip.shape[1]
    states = ts.shape[1]
    n = states // 2
    c = pl.program_id(0)

    @pl.when(c == 0)
    def _():
        padi[0:PAD, :] = ib[...]
        pads[0:PAD, :] = sb[...]
        passed[...] = jnp.ones_like(passed)
        local[...] = jnp.zeros_like(local)

    @pl.when(c > 0)
    def _():
        padi[0:PAD, :] = padi[CHUNK:, :]
        pads[0:PAD, :] = pads[CHUNK:, :]

    padi[PAD:, :] = ip[...]
    pads[PAD:, :] = sp[:, :states]
    rows = 64

    def filtered(step, _):
        start = pl.multiple_of(step * rows, rows)
        for scratch, taps, out, slope, size in (
            (padi, ti, v_out, dsi, inner),
            (pads, ts, bc_out, dss, states),
        ):
            for tile in range(size // LANES):
                cols = slice(tile * LANES, (tile + 1) * LANES)
                total = filter_tile(scratch, taps, start, rows, cols)
                gate = sigmoid(total)
                value = total * gate
                out[pl.ds(start, rows), cols] = value
                slope[pl.ds(start, rows), cols] = gate + value * (1.0 - gate)
        return 0

    lax.fori_loop(0, CHUNK // rows, filtered, 0)
    raw = sp[:, states:] + hp[0:1, :]
    dt = jnp.maximum(raw, 0.0) + jnp.log1p(jnp.exp(-jnp.abs(raw)))
    dt_out[...] = dt
    rate = -jnp.exp(hp[1:2, :]) * dt
    ones = (
        lax.broadcasted_iota(jnp.int32, (CHUNK, CHUNK), 0)
        >= lax.broadcasted_iota(jnp.int32, (CHUNK, CHUNK), 1)
    ).astype(F32)
    cum = dot(ones, rate, precision=HIGHEST)
    cum_out[...] = cum
    cumt_out[...] = cum.T[: cumt_out.shape[0]]
    last = cum[CHUNK - 1 : CHUNK, :]
    weight = jnp.exp(last - cum) * dt
    maps = bc_out[:, :n].T
    decay = head_rows(jnp.exp(last), width, inner)
    chdec[0] = jnp.broadcast_to(decay, (PAD, inner))
    passed[...] = passed[...] * decay
    for tile in range(inner // LANES):
        cols = slice(tile * LANES, (tile + 1) * LANES)
        weighted = v_out[:, cols] * spread_heads(weight, tile, width)
        part = dot(maps, weighted, precision=HIGHEST)
        fresh[0, :, cols] = part
        local[:, cols] = decay[:, cols] * local[:, cols] + part


def inner_kernel(width, v, bc, dt, cum, cumt, hp, out):
    inner = v.shape[1]
    n = bc.shape[1] // 2
    each = LANES // width
    lane = lax.broadcasted_iota(jnp.int32, (CHUNK, LANES), 1)
    lower = lax.broadcasted_iota(jnp.int32, (CHUNK, CHUNK), 0) >= lax.broadcasted_iota(
        jnp.int32, (CHUNK, CHUNK), 1
    )
    meet = dot(bc[:, n:], bc[:, :n], NT, HIGHEST)
    for tile in range(inner // LANES):
        cols = slice(tile * LANES, (tile + 1) * LANES)
        values = v[:, cols]
        stepped = values * spread_heads(dt[...], tile, width)
        result = None
        for k in range(each):
            head = tile * each + k
            spread = cum[:, head : head + 1] - cumt[head : head + 1, :]
            mixing = jnp.exp(jnp.where(lower, spread, NEG)) * meet
            part = dot(mixing, stepped, precision=HIGHEST)
            result = part if k == 0 else jnp.where(lane < k * width, result, part)
        out[:, cols] = result + spread_heads(hp[2:3, :], tile, width) * values


def gate_kernel(width, yd, bc, cum, fresh, chdec, entering, gate, gain, y_out, gn_out, states, squares, final):
    inner = yd.shape[1]
    n = bc.shape[1] // 2
    ones = jnp.ones((PAD, LANES), F32)
    c = pl.program_id(0)

    @pl.when(c == 0)
    def _():
        final[...] = entering[...]

    carried = jnp.exp(cum[...])
    maps = bc[:, n:]
    total = None
    for tile in range(inner // LANES):
        cols = slice(tile * LANES, (tile + 1) * LANES)
        state = final[:, cols]
        states[0, :, cols] = state
        final[:, cols] = chdec[0, 0:1, cols] * state + fresh[0, :, cols]
        y = yd[:, cols] + spread_heads(carried, tile, width) * dot(maps, state, precision=HIGHEST)
        y_out[:, cols] = y
        g = gate[:, cols]
        gated = y * (g * sigmoid(g))
        gn_out[:, cols] = gated * gain[0:1, cols]
        total = gated * gated if tile == 0 else total + gated * gated
    squares[...] = dot(ones, total, NT, HIGHEST)


def open_kernel(
    width, q, y, gate, gain, factors, bc, cum, chdec, dy_out, dgate, u_out, dgain, adjoint, local, passed
):
    inner = q.shape[1]
    n = bc.shape[1] // 2
    c = pl.program_id(0)

    @pl.when(c == 0)
    def _():
        dgain[...] = jnp.zeros_like(dgain)
        local[...] = jnp.zeros_like(local)
        passed[...] = jnp.ones_like(passed)

    carried = jnp.exp(cum[...])
    maps = bc[:, n:].T
    turned = factors[...].T
    s = turned[:, 0:1]
    t = turned[:, 1:2]
    for tile in range(inner // LANES):
        cols = slice(tile * LANES, (tile + 1) * LANES)
        g = gate[:, cols]
        soft = sigmoid(g)
        silu = g * soft
        out = y[:, cols]
        gated = out * silu
        grad = q[:, cols]
        scaled = gated * s
        u_out[:, cols] = scaled * gain[0:1, cols]
        dgain[:, cols] = dgain[:, cols] + (grad * scaled).reshape(CHUNK // PAD, PAD, LANES).sum(axis=0)
        dgated = s * (grad * gain[0:1, cols]) - t * gated
        dgate[:, cols] = dgated * out * (soft + silu * (1.0 - soft))
        dy = dgated * silu
        dy_out[:, cols] = dy
        part = dot(maps, dy * spread_heads(carried, tile, width))
        adjoint[0, :, cols] = part
        local[:, cols] = local[:, cols] + passed[0:1, cols] * part
    passed[...] = passed[...] * chdec[0]


def back_kernel(width, dy, v, bc, dt, cum, cumt, states, du, dbc, gram):
    inner = v.shape[1]
    n = bc.shape[1] // 2
    each = LANES // width
    lane = lax.broadcasted_iota(jnp.int32, (CHUNK, LANES), 1)
    upper = lax.broadcasted_iota(jnp.int32, (CHUNK, CHUNK), 0) <= lax.broadcasted_iota(
        jnp.int32, (CHUNK, CHUNK), 1
    )
    inputs, outputs = bc[:, :n], bc[:, n:]
    meet = dot(inputs, outputs, NT)
    carried = jnp.exp(cum[...])
    grad_out = None
    for tile in range(inner // LANES):
        cols = slice(tile * LANES, (tile + 1) * LANES)
        grad = dy[:, cols]
        stepped = v[:, cols] * spread_heads(dt[...], tile, width)
        result = None
        for k in range(each):
            head = tile * each + k
            spread = cumt[head : head + 1, :] - cum[:, head : head + 1]
            decay = jnp.exp(jnp.where(upper, spread, NEG))
            part = dot(decay * meet, grad)
            result = part if k == 0 else jnp.where(lane < k * width, result, part)
            own = (lane >= k * width) & (lane < (k + 1) * width)
            cross = decay * dot(jnp.where(own, stepped, 0.0), grad, NT)
            first = tile == 0 and k == 0
            gram[...] = cross if first else gram[...] + cross
        du[:, cols] = result
        part = dot(grad * spread_heads(carried, tile, width), states[0, :, cols], NT)
        grad_out = part if tile == 0 else grad_out + part
    total = gram[...]
    dbc[:, :n] = dot(total, outputs)
    dbc[:, n:] = grad_out + dot(total.T, inputs)


def head_totals(product, width):
    each = LANES // width
    lane = lax.broadcasted_iota(jnp.int32, product.shape, 1)
    result = []
    for k in range(each):
        own = (lane >= k * width) & (lane < (k + 1) * width)
        result.append(jnp.sum(jnp.where(own, product, 0.0), axis=1, keepdims=True))
    return result


def place_heads(columns, shape):
    lane = lax.broadcasted_iota(jnp.int32, shape, 1)
    result = jnp.zeros(shape, F32)
    for head, column in enumerate(columns):
        result = jnp.where(lane == head, column, result)
    return result


def close_kernel(
    width, dy, y, v, du, dsi, adjoint, bc, dt, cum, sp, hp, dbc, dss, chdec, final, later,
    dti, dts, dstep, rows, leaving, running,
):
    inner = v.shape[1]
    n = bc.shape[1] // 2
    heads_rate = -jnp.exp(hp[1:2, :])

    @pl.when(pl.program_id(0) == 0)
    def _():
        crossing = jnp.sum(final[...] * later[...], axis=0, keepdims=True)
        columns = []
        for tile in range(inner // LANES):
            columns += head_totals(crossing[:, tile * LANES : (tile + 1) * LANES], width)
        running[...] = jnp.broadcast_to(place_heads(columns, (1, LANES)), running.shape)
        leaving[...] = later[...]
        rows[...] = jnp.zeros_like(rows)

    ones = (
        lax.broadcasted_iota(jnp.int32, (CHUNK, CHUNK), 0)
        <= lax.broadcasted_iota(jnp.int32, (CHUNK, CHUNK), 1)
    ).astype(F32)
    step = dt[...]
    cums = cum[...]
    fade = jnp.exp(cums[CHUNK - 1 : CHUNK, :] - cums)
    inputs = bc[:, :n]
    grad_in = dbc[:, :n]
    own, direct = [], []
    for tile in range(inner // LANES):
        cols = slice(tile * LANES, (tile + 1) * LANES)
        adj = leaving[:, cols]
        wide_fade = spread_heads(fade, tile, width)
        wide_step = spread_heads(step, tile, width)
        skip = spread_heads(hp[2:3, :], tile, width)
        values = v[:, cols]
        grad = dy[:, cols]
        dstepped = du[:, cols] + wide_fade * dot(inputs, adj)
        grad_in = grad_in + dot(wide_fade * wide_step * values, adj, NT)
        dti[:, cols] = (wide_step * dstepped + skip * grad) * dsi[:, cols]
        own += head_totals(grad * (y[:, cols] - skip * values), width)
        direct += head_totals(values * dstepped, width)
        part = (grad * values).reshape(CHUNK // PAD, PAD, LANES).sum(axis=0)
        rows[0:PAD, cols] = rows[0:PAD, cols] + part
        leaving[:, cols] = adjoint[0, :, cols] + chdec[0, 0:1, cols] * adj
    dts[:, :n] = grad_in * dss[:, :n]
    dts[:, n:] = dbc[:, n:] * dss[:, n:]
    direct = place_heads(direct, (CHUNK, LANES))
    dcum = place_heads(own, (CHUNK, LANES)) - step * direct
    drate = dot(ones, dcum, precision=HIGHEST) + running[0:1, :]
    running[...] = jnp.broadcast_to(drate[0:1, :], running.shape)
    dstep_value = direct + drate * heads_rate
    raw = sp[:, 2 * n :] + hp[0:1, :]
    grad_raw = dstep_value * sigmoid(raw)
    dstep[...] = grad_raw
    lanes = slice(0, LANES)
    rates = drate * heads_rate * step
    rows[PAD : 2 * PAD, lanes] = rows[PAD : 2 * PAD, lanes] + rates.reshape(
        CHUNK // PAD, PAD, LANES
    ).sum(axis=0)
    rows[2 * PAD : 3 * PAD, lanes] = rows[2 * PAD : 3 * PAD, lanes] + grad_raw.reshape(
        CHUNK // PAD, PAD, LANES
    ).sum(axis=0)


def filter_back_kernel(
    dti, hi, dts, hs, ip, pi, ib, sp, ps, sb, ti, ts, dip, dsp, ri, rs, padi, pads, padgi, padgs
):
    inner = ip.shape[1]
    states = dts.shape[1]
    place = pl.program_id(0)

    @pl.when(place == 0)
    def _():
        padgi[CHUNK:, :] = hi[...]
        padgs[CHUNK:, :] = hs[...]
        ri[...] = jnp.zeros_like(ri)
        rs[...] = jnp.zeros_like(rs)

    @pl.when(place > 0)
    def _():
        padgi[CHUNK:, :] = padgi[0:PAD, :]
        padgs[CHUNK:, :] = padgs[0:PAD, :]

    @pl.when(place == pl.num_programs(0) - 1)
    def _():
        padi[0:PAD, :] = ib[...]
        pads[0:PAD, :] = sb[...]

    @pl.when(place < pl.num_programs(0) - 1)
    def _():
        padi[0:PAD, :] = pi[...]
        pads[0:PAD, :] = ps[:, :states]

    padi[PAD:, :] = ip[...]
    pads[PAD:, :] = sp[:, :states]
    padgi[0:CHUNK, :] = dti[...]
    padgs[0:CHUNK, :] = dts[...]
    rows = 64

    def folded(value):
        return value.reshape(rows // PAD, PAD, LANES).sum(axis=0)

    def step(number, _):
        start = pl.multiple_of(number * rows, rows)
        for signal, grads, taps, out, sums, size in (
            (padi, padgi, ti, dip, ri, inner),
            (pads, padgs, ts, dsp, rs, states),
        ):
            for tile in range(size // LANES):
                cols = slice(tile * LANES, (tile + 1) * LANES)
                ahead = grads[pl.ds(start, rows + PAD), cols]
                grad = ahead[:rows]
                before = signal[pl.ds(start, rows + PAD), cols]
                total = taps[3:4, cols] * grad
                sums[3 * PAD : 4 * PAD, cols] = sums[3 * PAD : 4 * PAD, cols] + folded(grad * before[PAD:])
                sums[4 * PAD : 5 * PAD, cols] = sums[4 * PAD : 5 * PAD, cols] + folded(grad)
                for back in range(1, 4):
                    tap = 3 - back
                    total = total + taps[tap : tap + 1, cols] * pltpu.roll(ahead, rows + PAD - back, 0)[:rows]
                    place = slice(tap * PAD, (tap + 1) * PAD)
                    sums[place, cols] = sums[place, cols] + folded(
                        grad * pltpu.roll(before, back, 0)[PAD:]
                    )
                out[pl.ds(start, rows), cols] = total
        return 0

    lax.fori_loop(0, CHUNK // rows, step, 0)


def matmul(left, right, dims=((1,), (0,)), precision=HIGH):
    return lax.dot_general(left, right, (dims, ((), ())), precision=precision)


def padded_rows(rows, lanes):
    rows = jnp.concatenate(rows, axis=0)
    return jnp.pad(rows, ((0, PAD - rows.shape[0]), (0, lanes - rows.shape[1])))


def forward(current, w, first, taps, beside):
    length = current.shape[0]
    inner = w["inner"].shape[1]
    heads = w["heads"]
    width = inner // heads
    states = w["states"]
    n = states // 2
    chunks = length // CHUNK
    root = lax.rsqrt(jnp.mean(current * current, axis=-1, keepdims=True) + epsilon)
    normed = current * root * w["pre_gain"][None, :]
    if first:
        whole = matmul(normed, w["state"], precision=HIGHEST)
        whole = jnp.concatenate([whole, taps], axis=0)
        ip = matmul(after(normed, whole), w["inner"], precision=HIGHEST)
        if power_of_two(lax.axis_size("head")):
            step = None
            for distance in distances("head"):
                other = exchanged(whole, "head", distance)
                if distance == 1:
                    other, ip = tied(other, ip)
                elif step is None:
                    step = matmul(after(normed, whole), w["step"], precision=HIGHEST)
                    other, step = tied(other, step)
                whole = joined(whole, other, "head", distance, 1)
        else:
            whole = gathered_columns(whole)
        if not power_of_two(lax.axis_size("head")) or step is None:
            step = matmul(normed, w["step"], precision=HIGHEST)
        taps = whole[length:]
        sp = whole[:length]
    else:
        ip = matmul(normed, w["inner"])
        sp = matmul(normed, w["maps"], NT, HIGHEST)
    border = shifted(
        jnp.concatenate([ip[length - PAD :], sp[length - PAD :, :states]], axis=1), "seq", 1
    )
    if first:
        sp = jnp.concatenate([sp, step], axis=1)
    ib, sb = border[:, :inner], border[:, inner:]
    taps_s = taps[w["layer"] * PAD : (w["layer"] + 1) * PAD]
    b_inner, b_states, b_lanes = (rows_of(CHUNK, size) for size in (inner, states, LANES))
    b_heads, b_sp = columns_of(16, CHUNK), rows_of(CHUNK, states + LANES)
    b_block, b_state = rows_of(1, n, inner), all_of(n, inner)
    b_decay = rows_of(1, PAD, inner)
    v, bc, dsi, dss, dt, cum, cumt, fresh, local, chdec, decay = call(
        functools.partial(start_kernel, width),
        chunks,
        [
            ((length, inner), b_inner),
            ((length, states), b_states),
            ((length, inner), b_inner),
            ((length, states), b_states),
            ((length, LANES), b_lanes),
            ((length, LANES), b_lanes),
            ((16, length), b_heads),
            ((chunks, n, inner), b_block),
            ((n, inner), b_state),
            ((chunks, PAD, inner), b_decay),
            ((PAD, inner), all_of(PAD, inner)),
        ],
        [pltpu.VMEM((CHUNK + PAD, inner), F32), pltpu.VMEM((CHUNK + PAD, states), F32)],
        2 * 3 * length * n * inner,
        (ip, b_inner),
        (ib, all_of(PAD, inner)),
        (sp, b_sp),
        (sb, all_of(PAD, states)),
        (w["taps_i"], all_of(PAD, inner)),
        (taps_s, all_of(PAD, states)),
        (w["heads_rows"], all_of(PAD, LANES)),
        vmem=LARGE,
    )
    decay = decay[0:1]

    def inside(before, done):
        return call(
            functools.partial(inner_kernel, width),
            chunks,
            [((length, inner), b_inner)],
            [],
            2 * 6 * length * CHUNK * inner,
            (v, b_inner),
            (bc, b_states),
            (dt, b_lanes),
            (cum, b_lanes),
            (cumt, b_heads),
            (w["heads_rows"], all_of(PAD, LANES)),
            vmem=LARGE,
        )

    def aside(before, done):
        gate = matmul(after(normed, before), w["gate"], precision=HIGHEST if first else HIGH)
        return [gate, beside]

    entering, ((yd,), (gate, beside)) = state_before(local, decay, False, [inside, aside])
    y, gn, carried, squares, final = call(
        functools.partial(gate_kernel, width),
        chunks,
        [
            ((length, inner), b_inner),
            ((length, inner), b_inner),
            ((chunks, n, inner), b_block),
            ((PAD, length), columns_of(PAD, CHUNK)),
            ((n, inner), b_state),
        ],
        [],
        2 * 3 * length * n * inner,
        (yd, b_inner),
        (bc, b_states),
        (cum, b_lanes),
        (fresh, b_block),
        (chdec, b_decay),
        (entering, b_state),
        (gate, b_inner),
        (w["norm_gain"][None, :], all_of(1, inner)),
    )
    saved = dict(
        current=current, root=root, normed=normed, ip=ip, sp=sp, ib=ib, sb=sb, gate=gate, v=v, bc=bc,
        dsi=dsi, dss=dss, dt=dt, cum=cum, cumt=cumt, fresh=fresh, chdec=chdec, decay=decay, y=y,
        gn=gn, states=carried, taps_s=taps_s, final=final,
    )
    return gn, squares[0:1], saved, taps, beside


def core_products(left, right):
    place = lax.axis_index("dp")
    if lax.axis_size("dp") != 2:
        total = matmul(left, right, ((0,), (0,)))
        return total, total
    return (
        matmul(left, half(right, 1 - place, 1), ((0,), (0,))),
        matmul(left, half(right, place, 1), ((0,), (0,))),
    )


def over_cores(sent, kept):
    if lax.axis_size("dp") != 2:
        return lax.psum(kept, "dp")
    return kept + exchanged(sent, "dp", 1)


def pair_kernel(one, a, two, b, sent, kept):
    width = a.shape[1] // 2
    first = lax.axis_index("dp") == 0
    for number, (left, right) in enumerate(((one, a), (two, b))):
        product = dot(left[...].T, right[...])
        cols = slice(number * width, (number + 1) * width)
        sent[:, cols] = jnp.where(first, product[:, width:], product[:, :width])
        kept[:, cols] = jnp.where(first, product[:, :width], product[:, width:])


def pair_products(one, a, two, b):
    length, model = one.shape
    inner = a.shape[1]
    tile = 256
    out = ((model, inner), rows_of(tile, inner))
    return call(
        pair_kernel,
        model // tile,
        [out, out],
        [],
        4 * length * model * inner,
        (one, columns_of(length, tile)),
        (a, all_of(length, inner)),
        (two, columns_of(length, tile)),
        (b, all_of(length, inner)),
    )


def last_kernel(left, right, small, sent, kept):
    width = right.shape[1] // 2
    rows = left.shape[1]
    first = lax.axis_index("dp") == 0
    turned = left[...].T
    product = dot(turned, right[...])
    sent[0, :rows, :] = jnp.where(first, product[:, width:], product[:, :width])
    kept[0, :rows, :] = jnp.where(first, product[:, :width], product[:, width:])
    below = dot(small[...].T, left[...])
    size = SMALL // 2
    sent[0, rows:, :] = jnp.where(first, below[size : 2 * size], below[:size])
    kept[0, rows:, :] = jnp.where(first, below[:size], below[size : 2 * size])


def last_products(left, right, small):
    length, model = left.shape
    inner = right.shape[1]
    shards = lax.axis_size("seq")
    rows = model // shards
    out = ((shards, rows + SMALL // 2, inner // 2), rows_of(1, rows + SMALL // 2, inner // 2))
    return call(
        last_kernel,
        shards,
        [out, out],
        [],
        2 * length * model * (inner + LANES),
        (left, columns_of(length, rows)),
        (right, all_of(length, inner)),
        (small, all_of(length, LANES)),
    )


def over_seq(total):
    return lax.psum_scatter(total, "seq", scatter_dimension=0, tiled=True)


def place_kernel(*refs):
    *parts, out = refs
    first = lax.axis_index("dp") == 0
    width = out.shape[2] // 2
    for layer in range(len(parts) // 2):
        mine, other = parts[2 * layer], parts[2 * layer + 1]

        @pl.when(first)
        def _():
            out[layer, :, :width] = mine[...]
            out[layer, :, width:] = other[...]

        @pl.when(jnp.logical_not(first))
        def _():
            out[layer, :, :width] = other[...]
            out[layer, :, width:] = mine[...]


def cores_joined(pairs, start, width, rows):
    if lax.axis_size("dp") != 2:
        return jnp.stack([mine[:rows, start : start + width] for mine, _ in pairs], axis=0)
    pieces = [piece for pair in pairs for piece in pair]
    tile = 96 if rows % 96 == 0 else rows
    return pl.pallas_call(
        place_kernel,
        grid=(rows // tile,),
        out_shape=jax.ShapeDtypeStruct((len(pairs), rows, 2 * width), F32),
        in_specs=[pl.BlockSpec((tile, width), lambda i: (i, start // width))] * len(pieces),
        out_specs=pl.BlockSpec((len(pairs), tile, 2 * width), lambda i: (0, i, 0)),
        compiler_params=pltpu.CompilerParams(vmem_limit_bytes=24 * 1024 * 1024),
        cost_estimate=pl.CostEstimate(flops=0, bytes_accessed=0, transcendentals=0),
    )(*pieces)


def backward(grad, q, scale, slope, w, saved, beside, waiting, earlier, final):
    s = saved
    length, inner = q.shape
    width = inner // w["heads"]
    states = w["states"]
    n = states // 2
    chunks = length // CHUNK
    factors = jnp.pad(jnp.concatenate([scale, slope], axis=0), ((0, PAD - 2), (0, 0)))
    b_inner, b_states, b_lanes = (rows_of(CHUNK, size) for size in (inner, states, LANES))
    b_heads, b_sp = columns_of(16, CHUNK), rows_of(CHUNK, states + LANES)
    b_block, b_state = rows_of(1, n, inner), all_of(n, inner)
    b_decay = rows_of(1, PAD, inner)
    dy, dgate, u, dgain, adjoint, local = call(
        functools.partial(open_kernel, width),
        chunks,
        [
            ((length, inner), b_inner),
            ((length, inner), b_inner),
            ((length, inner), b_inner),
            ((PAD, inner), all_of(PAD, inner)),
            ((chunks, n, inner), b_block),
            ((n, inner), b_state),
        ],
        [pltpu.VMEM((PAD, inner), F32)],
        2 * 3 * length * n * inner,
        (q, b_inner),
        (s["y"], b_inner),
        (s["gate"], b_inner),
        (w["norm_gain"][None, :], all_of(1, inner)),
        (factors, columns_of(PAD, CHUNK)),
        (s["bc"], b_states),
        (s["cum"], b_lanes),
        (s["chdec"], b_decay),
    )

    def cross(before, done):
        if lax.axis_size("dp") == 2:
            result = pair_products(grad, after(u, before), s["normed"], dgate)
        else:
            result = [
                jnp.concatenate(both, axis=1)
                for both in zip(core_products(grad, u), core_products(s["normed"], dgate))
            ]
        if waiting is not None:
            result = (*result, waiting)
        return beside.advance(*result) if beside is not None else result

    def inside(before, done):
        result = call(
            functools.partial(back_kernel, width),
            chunks,
            [((length, inner), b_inner), ((length, states), b_states)],
            [pltpu.VMEM((CHUNK, CHUNK), F32)],
            2 * 15 * length * CHUNK * inner,
            (after(dy, before), b_inner),
            (s["v"], b_inner),
            (s["bc"], b_states),
            (s["dt"], b_lanes),
            (s["cum"], b_lanes),
            (s["cumt"], b_heads),
            (s["states"], b_block),
        )
        return beside.advance(*result) if beside is not None else result

    def summed(before, done):
        result = [over_cores(*done[0][:2])]
        return beside.advance(*result) if beside is not None else result


    later, (_, (du, dbc), (pair, *_)) = state_before(local, s["decay"], True, [cross, inside, summed])
    pair = over_seq(pair)
    dti, dts, dstep, rows = call(
        functools.partial(close_kernel, width),
        chunks,
        [
            ((length, inner), b_inner),
            ((length, states), b_states),
            ((length, LANES), b_lanes),
            ((3 * PAD, inner), all_of(3 * PAD, inner)),
        ],
        [pltpu.VMEM((n, inner), F32), pltpu.VMEM((PAD, LANES), F32)],
        2 * 6 * length * n * inner,
        (dy, b_inner),
        (s["y"], b_inner),
        (s["v"], b_inner),
        (du, b_inner),
        (s["dsi"], b_inner),
        (adjoint, b_block),
        (s["bc"], b_states),
        (s["dt"], b_lanes),
        (s["cum"], b_lanes),
        (s["sp"], b_sp),
        (w["heads_rows"], all_of(PAD, LANES)),
        (dbc, b_states),
        (s["dss"], b_states),
        (s["chdec"], b_decay),
        (s["final"], b_state),
        (later, b_state),
        backward=True,
        vmem=LARGE,
    )
    if beside is not None:
        dti, dts = beside.advance(dti, dts)
    halo = shifted(jnp.concatenate([dti[:PAD], dts[:PAD]], axis=1), "seq", -1)
    base = matmul(after(dgate, dti), w["gate"], NT)
    halo, base = tied(halo, base)
    def edge(size):
        return pl.BlockSpec((PAD, size), lambda c: (jnp.maximum(c * (CHUNK // PAD) - 1, 0), 0))

    dip, dsp, ri, rs = call(
        filter_back_kernel,
        chunks,
        [
            ((length, inner), b_inner),
            ((length, states), b_states),
            ((5 * PAD, inner), all_of(5 * PAD, inner)),
            ((5 * PAD, states), all_of(5 * PAD, states)),
        ],
        [pltpu.VMEM((CHUNK + PAD, size), F32) for size in (inner, states, inner, states)],
        16 * length * inner,
        (dti, b_inner),
        (halo[:, :inner], all_of(PAD, inner)),
        (dts, b_states),
        (halo[:, inner:], all_of(PAD, states)),
        (s["ip"], b_inner),
        (s["ip"], edge(inner)),
        (s["ib"], all_of(PAD, inner)),
        (s["sp"], b_sp),
        (s["sp"], edge(states + LANES)),
        (s["sb"], all_of(PAD, states)),
        (w["taps_i"], all_of(PAD, inner)),
        (s["taps_s"], all_of(PAD, states)),
        backward=True,
    )
    gains = []

    def product(base, dip, dmaps, scaled):
        total = base + matmul(dip, w["inner"], NT) + matmul(dmaps, w["maps"])
        gains.append(jnp.sum(total * scaled, axis=0))
        return total

    def finish(rows_grad, offset):
        def take(array):
            return lax.dynamic_slice_in_dim(array, offset, rows_grad.shape[0], 0)

        x, root = take(s["current"]), take(s["root"])
        scaled = rows_grad * w["pre_gain"][None, :]
        along = jnp.mean(scaled * x, axis=-1, keepdims=True)
        return root * scaled - x * (root * root * root * along)

    shared = dsp
    own = states // lax.axis_size("head")
    lefts = [base, dip, jnp.concatenate([dsp, dstep], axis=1), s["current"] * s["root"]]
    if power_of_two(lax.axis_size("head")):
        way = distances("head")[::-1]
        for number, distance in enumerate(way):
            bit = bit_of("head", distance)
            other = exchanged(half(shared, 1 - bit, 1), "head", distance)
            if number == 0:
                steps = Steps(head_sum(lefts, product, finish))
                (other,) = steps.advance(other)
            shared = half(shared, bit, 1) + other
    else:
        shared = lax.psum_scatter(shared, "head", scatter_dimension=1, tiled=True)
        steps = Steps(head_sum(lefts, product, finish))
        steps.advance()
    def folded(array):
        return array.reshape(-1, PAD, array.shape[1]).sum(axis=1)

    ri, rs, rows = folded(ri), folded(rs), folded(rows)
    over_heads = jnp.concatenate([gains[0] + gains[1], rs.reshape(-1)])
    flat = jnp.concatenate(
        [ri.reshape(-1), dgain.sum(axis=0), rows[0], rows[1, :LANES], rows[2, :LANES]]
    )
    small_parts = [*earlier, (over_heads, flat)]
    (dip,) = steps.advance(dip)
    if final:
        over_heads = jnp.concatenate([part[0] for part in small_parts])
        over_heads = small_sum(after(over_heads, dip), "head")
    shards = lax.axis_size("seq")
    model = s["normed"].shape[1]
    small = jnp.concatenate([shared, dstep[:, : LANES - own]], axis=1)
    if lax.axis_size("dp") == 2 and model // shards % LANES == 0:
        sent, kept = last_products(s["normed"], dip, small)
        if final:
            kept, pair = tied(kept, pair)
        last = over_cores(sent, kept)
    else:
        last = over_cores(*core_products(s["normed"], dip)).reshape(shards, -1, inner // lax.axis_size("dp"))
        small = matmul(small[:, :SMALL], s["normed"], ((0,), (0,)))
        small = jnp.transpose(small.reshape(SMALL, shards, -1), (1, 0, 2))
        if lax.axis_size("dp") == 2:
            place = lax.axis_index("dp")
            small = over_cores(half(small, 1 - place, 1), half(small, place, 1))
        else:
            small = lax.psum(small, "dp")
        small = jnp.pad(small, ((0, 0), (0, 0), (0, last.shape[2] - small.shape[2])))
        last = jnp.concatenate([last, small], axis=1)
    last = last.reshape(-1, last.shape[2])
    if final:
        (last,) = steps.advance(last)
    else:
        last, pair = steps.advance(last, pair)
    last = over_seq(after(last, pair))
    if not final:
        branch = steps.finished()
        return grad + branch, pair, last, small_parts, own
    (over_heads,) = steps.advance(over_heads)
    flat = jnp.concatenate([over_heads] + [part[1] for part in small_parts])
    flat = small_sum(small_sum(flat, "dp"), "seq")
    flat, last = tied(flat, last)
    branch = steps.finished()
    sizes = (small_parts[0][0].size, small_parts[0][1].size)
    return grad + branch, pair, last, (flat, sizes), own


def unpack_kernel(width, size, flat, pre, fi, fib, fs, fsb, bias, rate, skip, norm):
    layers, model = pre.shape
    inner = norm.shape[1]
    own = fs.shape[2]
    heads = bias.shape[1]
    place = lax.axis_index("head")
    shares = size // LANES - model // LANES
    shares = shares * LANES // 5 // own
    rest = 7 * inner // LANES + 2

    def row(number):
        return flat[number : number + 1, :]

    for layer in range(layers):
        number = layers - 1 - layer
        base = number * size // LANES
        for k in range(model // LANES):
            pre[layer : layer + 1, k * LANES : (k + 1) * LANES] = row(base + k)
        base += model // LANES
        for tap in range(5):
            chosen = None
            for share in range(shares):
                start = (tap * shares + share) * own
                line, lane = divmod(start, LANES)
                piece = row(base + line)[:, lane : lane + own]
                chosen = piece if share == 0 else jnp.where(place == share, piece, chosen)
            if tap < 4:
                fs[layer, tap : tap + 1, :] = chosen
            else:
                fsb[layer : layer + 1, :] = chosen
        base = layers * size // LANES + number * rest
        sums = []
        for k in range(inner // LANES):
            cols = slice(k * LANES, (k + 1) * LANES)
            for tap in range(4):
                fi[layer, tap : tap + 1, cols] = row(base + tap * (inner // LANES) + k)
            fib[layer : layer + 1, cols] = row(base + 4 * (inner // LANES) + k)
            norm[layer : layer + 1, cols] = row(base + 5 * (inner // LANES) + k)
            sums += head_totals(row(base + 6 * (inner // LANES) + k), width)
        skip[layer : layer + 1, :] = place_heads(sums, (1, LANES))[:, :heads]
        rate[layer : layer + 1, :] = row(base + rest - 2)[:, :heads]
        bias[layer : layer + 1, :] = row(base + rest - 1)[:, :heads]


def unpacked(flat, size, layers, model, inner, own, heads):
    shapes = [
        (layers, model),
        (layers, 4, inner),
        (layers, inner),
        (layers, 4, own),
        (layers, own),
        (layers, heads),
        (layers, heads),
        (layers, heads),
        (layers, inner),
    ]
    return pl.pallas_call(
        functools.partial(unpack_kernel, inner // heads, size),
        out_shape=[jax.ShapeDtypeStruct(shape, F32) for shape in shapes],
        compiler_params=pltpu.CompilerParams(vmem_limit_bytes=VMEM),
        cost_estimate=pl.CostEstimate(flops=0, bytes_accessed=0, transcendentals=0),
    )(flat.reshape(-1, LANES))


def gathered_columns(value):
    if not power_of_two(lax.axis_size("head")):
        return lax.all_gather(value, "head", axis=1, tiled=True)
    return gather_back(value, "head", distances("head")[::-1], 1)


def body(
    tokens,
    cotangent,
    pre_gain,
    gate_weight,
    inner_weight,
    state_weight,
    step_weight,
    filter_inner,
    filter_inner_bias,
    filter_state,
    filter_state_bias,
    step_bias,
    log_rate,
    skip_gain,
    norm_gain,
    out_weight,
):
    layers = pre_gain.shape[0]
    heads = step_bias.shape[1]
    inner = gate_weight.shape[2]
    taps = jnp.concatenate([filter_state, filter_state_bias[:, None, :]], axis=1)
    taps = jnp.pad(taps, ((0, 0), (0, PAD - taps.shape[1]), (0, 0))).reshape(layers * PAD, -1)
    weights = []
    for layer in range(layers):
        steps = jnp.pad(step_weight[layer], ((0, 0), (0, LANES - heads)))
        weights.append(
            dict(
                layer=layer,
                heads=heads,
                states=state_weight.shape[2] * lax.axis_size("head"),
                pre_gain=pre_gain[layer],
                gate=gate_weight[layer],
                inner=inner_weight[layer],
                state=state_weight[layer],
                step=steps,
                out=out_weight[layer],
                norm_gain=norm_gain[layer],
                taps_i=padded_rows([filter_inner[layer], filter_inner_bias[layer][None]], inner),
                heads_rows=padded_rows(
                    [step_bias[layer][None], log_rate[layer][None], skip_gain[layer][None]], LANES
                ),
            )
        )
    maps = jnp.concatenate([state_weight[layer].T for layer in range(layers)], axis=1)
    maps = lax.all_gather(maps, "head", axis=0, tiled=True)
    current = tokens[0]
    grad = cotangent[0]
    kept = []
    extra = None
    for layer in range(layers):
        w = weights[layer]
        gn, squares, saved, taps, maps = forward(current, w, layer == 0, taps, maps)
        if layer == 0:
            for number, other in enumerate(weights):
                size = other["inner"].shape[0]
                cut = maps[:, number * size : (number + 1) * size]
                other["maps"] = jnp.concatenate([cut, other["step"].T], axis=0)
        last = layer == layers - 1
        if last:
            both = jnp.concatenate([squares, jnp.sum(extra * gn, axis=1)[None, :]], axis=0)
            both = small_sum(both, "head")
            squares, along = both[0:1], both[1:2]
        else:
            squares = small_sum(squares, "head")
        scale = lax.rsqrt(squares / INNER + epsilon)

        def finish(rows, offset, scale=scale):
            return rows * lax.dynamic_slice_in_dim(scale[0], offset, rows.shape[0], 0)[:, None]

        steps = Steps(head_sum([gn], lambda rows, w=w, p=HIGH if last else HIGHEST: matmul(rows, w["out"], NT, p), finish))
        if last:
            scale = after(scale, steps.now)
        if layer == 0:
            product = matmul(after(grad, steps.now), weights[layers - 1]["out"])
            if not last:
                steps.advance()
                (product,) = steps.advance(product)
            extra = product
        branch = None if last else steps.finished()
        kept.append((saved, scale, branch))
        if not last:
            current = current + branch
    collected = [None] * layers
    waiting = None
    earlier = []
    for layer in reversed(range(layers)):
        w = weights[layer]
        saved, scale, branch = kept[layer]
        if layer < layers - 1:
            if layer == layers - 2:
                (grad,) = steps.advance(grad)
            q = matmul(grad, w["out"])
            slope = jnp.sum(grad * branch, axis=1)[None, :] * scale * scale / INNER
        else:
            q = extra
            slope = along * scale * scale * scale / INNER
        grad, *collected[layer] = backward(
            grad, q, scale, slope, w, saved, steps if layer == layers - 2 else None, waiting, earlier, layer == 0
        )
        waiting = collected[layer][1]
        earlier = collected[layer][2]
    current = current + steps.finished()
    flat, (size, _) = earlier
    own = collected[0][3]
    stacked = unpacked(flat, size, layers, gate_weight.shape[1], inner, own, heads)
    two = lax.axis_size("dp") == 2

    def with_other(part):
        return part, exchanged(part, "dp", 1) if two else part

    pairs = [[with_other(entry[0]) for entry in collected]]
    half_width = inner // 2 if two else inner
    rows = gate_weight.shape[1] // lax.axis_size("seq")
    large = {
        "out": cores_joined(pairs[0], 0, half_width, rows),
        "gate": cores_joined(pairs[0], half_width, half_width, rows),
    }
    collected[0][1], current, large = tied(collected[0][1], current, large)
    pairs.append([with_other(entry[1]) for entry in collected])
    large["inner"] = cores_joined(pairs[1], 0, half_width, rows)
    small = []
    for mine, other in pairs[1]:
        mine, other = mine[rows:, :rows], other[rows:, :rows]
        if two:
            mine = jnp.concatenate(
                [jnp.where(lax.axis_index("dp") == 0, a, b) for a, b in ((mine, other), (other, mine))],
                axis=0,
            )
        small.append(mine.T)
    small = jnp.stack(small, axis=0)
    return (
        current[None],
        grad[None],
        stacked[0],
        large["gate"],
        large["inner"],
        small[:, :, :own],
        small[:, :, own : own + heads],
        *stacked[1:],
        large["out"],
    )


def solution(mesh):
    placed = (
        P("dp", "seq", None),
        P("dp", "seq", None),
        P(),
        P(None, None, "head"),
        P(None, None, "head"),
        P(None, None, "head"),
        P(None, None, "head"),
        P(None, None, "head"),
        P(None, "head"),
        P(None, None, "head"),
        P(None, "head"),
        P(None, "head"),
        P(None, "head"),
        P(None, "head"),
        P(None, "head"),
        P(None, None, "head"),
    )
    return jax.shard_map(
        body,
        mesh=mesh,
        in_specs=placed,
        out_specs=(
            P("dp", "seq", None),
            P("dp", "seq", None),
            P(),
            P(None, "seq", "head"),
            P(None, "seq", "head"),
            P(None, "seq", "head"),
            P(None, "seq", "head"),
            P(None, None, "head"),
            P(None, "head"),
            P(None, None, "head"),
            P(None, "head"),
            P(None, "head"),
            P(None, "head"),
            P(None, "head"),
            P(None, "head"),
            P(None, "seq", "head"),
        ),
        check_vma=False,
    )
```

```python
import functools

import jax
import jax.numpy as jnp
from jax import lax
from jax.experimental import pallas as pl
from jax.experimental.pallas import tpu as pltpu
from jax.sharding import PartitionSpec as P

INNER = 3072
CHUNK = 128
LANES = 128
PAD = 8
SMALL = 96
COST = 4
VMEM = 20 * 1024 * 1024
LARGE = 56 * 1024 * 1024
epsilon = 1e-05
HIGH = lax.Precision.HIGH
HIGHEST = lax.Precision.HIGHEST
NEG = -1e30
F32 = jnp.float32


def power_of_two(n):
    return n & (n - 1) == 0


def exchanged(value, axis, distance):
    n = lax.axis_size(axis)
    return lax.ppermute(value, axis, [(i, i ^ distance) for i in range(n)])


def shifted(value, axis, step):
    n = lax.axis_size(axis)
    pairs = [(i, i + step) for i in range(n) if 0 <= i + step < n]
    return lax.ppermute(value, axis, pairs)


def distances(axis):
    n = lax.axis_size(axis)
    return [1 << k for k in range(n.bit_length() - 1)]


def bit_of(axis, distance):
    return (lax.axis_index(axis) // distance) % 2


def small_sum(value, axis):
    if not power_of_two(lax.axis_size(axis)):
        return lax.psum(value, axis)
    for distance in distances(axis):
        value = value + exchanged(value, axis, distance)
    return value


def half(value, which, dim=0):
    size = value.shape[dim] // 2
    return lax.dynamic_slice_in_dim(value, which * size, size, dim)


def joined(mine, other, axis, distance, dim=0):
    first = bit_of(axis, distance) == 0
    return jnp.concatenate(
        [jnp.where(first, mine, other), jnp.where(first, other, mine)], axis=dim
    )


def gather_back(value, axis, order, dim=0):
    for distance in order[::-1]:
        value = joined(value, exchanged(value, axis, distance), axis, distance, dim)
    return value


def tied(value, *others):
    return lax.optimization_barrier((value, *others))


def head_sum(lefts, product, finish):
    order = distances("head")
    rows = lefts[0].shape[0] // 2
    ways = (order, order[::-1])

    def chosen(other):
        picked = []
        for array in lefts:
            pieces = []
            for number, way in enumerate(ways):
                bit = bit_of("head", way[0])
                part = array[number * rows : (number + 1) * rows]
                pieces.append(half(part, 1 - bit if other else bit))
            picked.append(jnp.concatenate(pieces, axis=0))
        return product(*picked)

    sent = chosen(True)
    kept = chosen(False)
    sent, kept = yield sent, kept
    size = rows // 2
    got = [
        exchanged(sent[number * size : (number + 1) * size], "head", way[0])
        for number, way in enumerate(ways)
    ]
    kept = [kept[:size], kept[size:]]
    offsets = [bit_of("head", way[0]) * size + number * rows for number, way in enumerate(ways)]
    got, kept = yield got, kept
    for step in range(1, len(order)):
        bits = [bit_of("head", way[step]) for way in ways]
        sends = [half(k, 1 - bit) + half(g, 1 - bit) for k, g, bit in zip(kept, got, bits)]
        arrived = [exchanged(send, "head", way[step]) for send, way in zip(sends, ways)]
        kept = [half(k, bit) + half(g, bit) for k, g, bit in zip(kept, got, bits)]
        offsets = [o + bit * k.shape[0] for o, bit, k in zip(offsets, bits, kept)]
        got, kept = yield arrived, kept
    mine = [finish(k + g, o) for k, g, o in zip(kept, got, offsets)]
    for step in range(len(order) - 1, -1, -1):
        others = [exchanged(m, "head", way[step]) for m, way in zip(mine, ways)]
        others, mine = yield others, mine
        mine = [joined(m, o, "head", way[step]) for m, o, way in zip(mine, others, ways)]
    return jnp.concatenate(mine, axis=0)


class Steps:
    def __init__(self, steps):
        self.steps = steps
        self.now = next(steps)
        self.result = None

    def advance(self, *others):
        if self.result is not None:
            return others
        if len(others) > 0:
            self.now, *others = tied(self.now, *others)
        try:
            self.now = self.steps.send(self.now)
        except StopIteration as end:
            self.result = end.value
        return others

    def finished(self):
        while self.result is None:
            self.advance()
        return self.result


def after(value, *others):
    return tied(value, *others)[0]


def state_before(local, decay, reverse, windows):
    n = lax.axis_size("seq")
    done = []
    arrived = []
    before = local
    for hop in range(n - 1):
        source, target = (n - 1 - hop, n - 2 - hop) if reverse else (hop, hop + 1)
        leaving = local if hop == 0 else decay * before + local
        got = lax.ppermute(leaving, "seq", [(source, target)])
        if hop < len(windows):
            got, *result = tied(got, *windows[hop](before, done))
            done.append(result)
        before = got
        arrived.append(got)
    for window in windows[n - 1 :]:
        done.append(window(before, done))
    return sum(arrived) if len(arrived) > 0 else jnp.zeros_like(local), done


def rows_of(*shape):
    return pl.BlockSpec(shape, lambda c: (c,) + (0,) * (len(shape) - 1))


def columns_of(*shape):
    return pl.BlockSpec(shape, lambda c: (0, c))


def all_of(*shape):
    return pl.BlockSpec(shape, lambda c: (0,) * len(shape))


def reverse(spec, steps):
    index = spec.index_map
    return pl.BlockSpec(spec.block_shape, lambda c: index(steps - 1 - c))


def call(kernel, steps, outs, scratch, flops, *args, backward=False, vmem=VMEM):
    shapes = [jax.ShapeDtypeStruct(shape, F32) for shape, _ in outs]
    size = 4 * sum(a.size for a, _ in args) + 4 * sum(s.size for s in shapes)

    def spec(blocks):
        return reverse(blocks, steps) if backward else blocks

    return pl.pallas_call(
        kernel,
        grid=(steps,),
        out_shape=shapes,
        in_specs=[spec(blocks) for _, blocks in args],
        out_specs=[spec(blocks) for _, blocks in outs],
        scratch_shapes=scratch,
        compiler_params=pltpu.CompilerParams(vmem_limit_bytes=vmem),
        cost_estimate=pl.CostEstimate(flops=flops // COST, bytes_accessed=size // COST, transcendentals=0),
    )(*[a for a, _ in args])


def dot(left, right, dims=((1,), (0,)), precision=HIGH):
    return lax.dot_general(
        left, right, (dims, ((), ())), precision=precision, preferred_element_type=F32
    )


NT = ((1,), (1,))


def sigmoid(value):
    return 1.0 / (1.0 + jnp.exp(-value))


def spread_heads(columns, tile, width):
    each = LANES // width
    lane = lax.broadcasted_iota(jnp.int32, (columns.shape[0], LANES), 1)
    result = columns[:, tile * each : tile * each + 1]
    for k in range(1, each):
        result = jnp.where(lane < k * width, result, columns[:, tile * each + k : tile * each + k + 1])
    return jnp.broadcast_to(result, (columns.shape[0], LANES))


def head_rows(row, width, total):
    tiles = [spread_heads(row, tile, width) for tile in range(total // LANES)]
    return jnp.concatenate(tiles, axis=1)


def filter_tile(scratch, taps, start, rows, cols):
    block = scratch[pl.ds(start, rows + PAD), cols]
    total = taps[4:5, cols] + taps[3:4, cols] * block[PAD:]
    for back in range(1, 4):
        total = total + taps[3 - back : 4 - back, cols] * pltpu.roll(block, back, 0)[PAD:]
    return total


def start_kernel(
    width, ip, ib, sp, sb, ti, ts, hp, v_out, bc_out, dsi, dss, dt_out, cum_out, cumt_out, fresh, local, chdec, passed, padi, pads
):
    inner = ip.shape[1]
    states = ts.shape[1]
    n = states // 2
    c = pl.program_id(0)

    @pl.when(c == 0)
    def _():
        padi[0:PAD, :] = ib[...]
        pads[0:PAD, :] = sb[...]
        passed[...] = jnp.ones_like(passed)
        local[...] = jnp.zeros_like(local)

    @pl.when(c > 0)
    def _():
        padi[0:PAD, :] = padi[CHUNK:, :]
        pads[0:PAD, :] = pads[CHUNK:, :]

    padi[PAD:, :] = ip[...]
    pads[PAD:, :] = sp[:, :states]
    rows = 64

    def filtered(step, _):
        start = pl.multiple_of(step * rows, rows)
        for scratch, taps, out, slope, size in (
            (padi, ti, v_out, dsi, inner),
            (pads, ts, bc_out, dss, states),
        ):
            for tile in range(size // LANES):
                cols = slice(tile * LANES, (tile + 1) * LANES)
                total = filter_tile(scratch, taps, start, rows, cols)
                gate = sigmoid(total)
                value = total * gate
                out[pl.ds(start, rows), cols] = value
                slope[pl.ds(start, rows), cols] = gate + value * (1.0 - gate)
        return 0

    lax.fori_loop(0, CHUNK // rows, filtered, 0)
    raw = sp[:, states:] + hp[0:1, :]
    dt = jnp.maximum(raw, 0.0) + jnp.log1p(jnp.exp(-jnp.abs(raw)))
    dt_out[...] = dt
    rate = -jnp.exp(hp[1:2, :]) * dt
    ones = (
        lax.broadcasted_iota(jnp.int32, (CHUNK, CHUNK), 0)
        >= lax.broadcasted_iota(jnp.int32, (CHUNK, CHUNK), 1)
    ).astype(F32)
    cum = dot(ones, rate, precision=HIGHEST)
    cum_out[...] = cum
    cumt_out[...] = cum.T[: cumt_out.shape[0]]
    last = cum[CHUNK - 1 : CHUNK, :]
    weight = jnp.exp(last - cum) * dt
    maps = bc_out[:, :n].T
    decay = head_rows(jnp.exp(last), width, inner)
    chdec[0] = jnp.broadcast_to(decay, (PAD, inner))
    passed[...] = passed[...] * decay
    for tile in range(inner // LANES):
        cols = slice(tile * LANES, (tile + 1) * LANES)
        weighted = v_out[:, cols] * spread_heads(weight, tile, width)
        part = dot(maps, weighted, precision=HIGHEST)
        fresh[0, :, cols] = part
        local[:, cols] = decay[:, cols] * local[:, cols] + part


def inner_kernel(width, v, bc, dt, cum, cumt, hp, out):
    inner = v.shape[1]
    n = bc.shape[1] // 2
    each = LANES // width
    lane = lax.broadcasted_iota(jnp.int32, (CHUNK, LANES), 1)
    lower = lax.broadcasted_iota(jnp.int32, (CHUNK, CHUNK), 0) >= lax.broadcasted_iota(
        jnp.int32, (CHUNK, CHUNK), 1
    )
    meet = dot(bc[:, n:], bc[:, :n], NT, HIGHEST)
    for tile in range(inner // LANES):
        cols = slice(tile * LANES, (tile + 1) * LANES)
        values = v[:, cols]
        stepped = values * spread_heads(dt[...], tile, width)
        result = None
        for k in range(each):
            head = tile * each + k
            spread = cum[:, head : head + 1] - cumt[head : head + 1, :]
            mixing = jnp.exp(jnp.where(lower, spread, NEG)) * meet
            part = dot(mixing, stepped, precision=HIGHEST)
            result = part if k == 0 else jnp.where(lane < k * width, result, part)
        out[:, cols] = result + spread_heads(hp[2:3, :], tile, width) * values


def gate_kernel(width, yd, bc, cum, fresh, chdec, entering, gate, gain, y_out, gn_out, states, squares, final):
    inner = yd.shape[1]
    n = bc.shape[1] // 2
    ones = jnp.ones((PAD, LANES), F32)
    c = pl.program_id(0)

    @pl.when(c == 0)
    def _():
        final[...] = entering[...]

    carried = jnp.exp(cum[...])
    maps = bc[:, n:]
    total = None
    for tile in range(inner // LANES):
        cols = slice(tile * LANES, (tile + 1) * LANES)
        state = final[:, cols]
        states[0, :, cols] = state
        final[:, cols] = chdec[0, 0:1, cols] * state + fresh[0, :, cols]
        y = yd[:, cols] + spread_heads(carried, tile, width) * dot(maps, state, precision=HIGHEST)
        y_out[:, cols] = y
        g = gate[:, cols]
        gated = y * (g * sigmoid(g))
        gn_out[:, cols] = gated * gain[0:1, cols]
        total = gated * gated if tile == 0 else total + gated * gated
    squares[...] = dot(ones, total, NT, HIGHEST)


def open_kernel(
    width, q, y, gate, gain, factors, bc, cum, chdec, dy_out, dgate, u_out, dgain, adjoint, local, passed
):
    inner = q.shape[1]
    n = bc.shape[1] // 2
    c = pl.program_id(0)

    @pl.when(c == 0)
    def _():
        dgain[...] = jnp.zeros_like(dgain)
        local[...] = jnp.zeros_like(local)
        passed[...] = jnp.ones_like(passed)

    carried = jnp.exp(cum[...])
    maps = bc[:, n:].T
    turned = factors[...].T
    s = turned[:, 0:1]
    t = turned[:, 1:2]
    for tile in range(inner // LANES):
        cols = slice(tile * LANES, (tile + 1) * LANES)
        g = gate[:, cols]
        soft = sigmoid(g)
        silu = g * soft
        out = y[:, cols]
        gated = out * silu
        grad = q[:, cols]
        scaled = gated * s
        u_out[:, cols] = scaled * gain[0:1, cols]
        dgain[:, cols] = dgain[:, cols] + (grad * scaled).reshape(CHUNK // PAD, PAD, LANES).sum(axis=0)
        dgated = s * (grad * gain[0:1, cols]) - t * gated
        dgate[:, cols] = dgated * out * (soft + silu * (1.0 - soft))
        dy = dgated * silu
        dy_out[:, cols] = dy
        part = dot(maps, dy * spread_heads(carried, tile, width))
        adjoint[0, :, cols] = part
        local[:, cols] = local[:, cols] + passed[0:1, cols] * part
    passed[...] = passed[...] * chdec[0]


def back_kernel(width, dy, v, bc, dt, cum, cumt, states, du, dbc, gram):
    inner = v.shape[1]
    n = bc.shape[1] // 2
    each = LANES // width
    lane = lax.broadcasted_iota(jnp.int32, (CHUNK, LANES), 1)
    upper = lax.broadcasted_iota(jnp.int32, (CHUNK, CHUNK), 0) <= lax.broadcasted_iota(
        jnp.int32, (CHUNK, CHUNK), 1
    )
    inputs, outputs = bc[:, :n], bc[:, n:]
    meet = dot(inputs, outputs, NT)
    carried = jnp.exp(cum[...])
    grad_out = None
    for tile in range(inner // LANES):
        cols = slice(tile * LANES, (tile + 1) * LANES)
        grad = dy[:, cols]
        stepped = v[:, cols] * spread_heads(dt[...], tile, width)
        result = None
        for k in range(each):
            head = tile * each + k
            spread = cumt[head : head + 1, :] - cum[:, head : head + 1]
            decay = jnp.exp(jnp.where(upper, spread, NEG))
            part = dot(decay * meet, grad)
            result = part if k == 0 else jnp.where(lane < k * width, result, part)
            own = (lane >= k * width) & (lane < (k + 1) * width)
            cross = decay * dot(jnp.where(own, stepped, 0.0), grad, NT)
            first = tile == 0 and k == 0
            gram[...] = cross if first else gram[...] + cross
        du[:, cols] = result
        part = dot(grad * spread_heads(carried, tile, width), states[0, :, cols], NT)
        grad_out = part if tile == 0 else grad_out + part
    total = gram[...]
    dbc[:, :n] = dot(total, outputs)
    dbc[:, n:] = grad_out + dot(total.T, inputs)


def head_totals(product, width):
    each = LANES // width
    lane = lax.broadcasted_iota(jnp.int32, product.shape, 1)
    result = []
    for k in range(each):
        own = (lane >= k * width) & (lane < (k + 1) * width)
        result.append(jnp.sum(jnp.where(own, product, 0.0), axis=1, keepdims=True))
    return result


def place_heads(columns, shape):
    lane = lax.broadcasted_iota(jnp.int32, shape, 1)
    result = jnp.zeros(shape, F32)
    for head, column in enumerate(columns):
        result = jnp.where(lane == head, column, result)
    return result


def close_kernel(
    width, dy, y, v, du, dsi, adjoint, bc, dt, cum, sp, hp, dbc, dss, chdec, final, later,
    dti, dts, dstep, rows, leaving, running,
):
    inner = v.shape[1]
    n = bc.shape[1] // 2
    heads_rate = -jnp.exp(hp[1:2, :])

    @pl.when(pl.program_id(0) == 0)
    def _():
        crossing = jnp.sum(final[...] * later[...], axis=0, keepdims=True)
        columns = []
        for tile in range(inner // LANES):
            columns += head_totals(crossing[:, tile * LANES : (tile + 1) * LANES], width)
        running[...] = jnp.broadcast_to(place_heads(columns, (1, LANES)), running.shape)
        leaving[...] = later[...]
        rows[...] = jnp.zeros_like(rows)

    ones = (
        lax.broadcasted_iota(jnp.int32, (CHUNK, CHUNK), 0)
        <= lax.broadcasted_iota(jnp.int32, (CHUNK, CHUNK), 1)
    ).astype(F32)
    step = dt[...]
    cums = cum[...]
    fade = jnp.exp(cums[CHUNK - 1 : CHUNK, :] - cums)
    inputs = bc[:, :n]
    grad_in = dbc[:, :n]
    own, direct = [], []
    for tile in range(inner // LANES):
        cols = slice(tile * LANES, (tile + 1) * LANES)
        adj = leaving[:, cols]
        wide_fade = spread_heads(fade, tile, width)
        wide_step = spread_heads(step, tile, width)
        skip = spread_heads(hp[2:3, :], tile, width)
        values = v[:, cols]
        grad = dy[:, cols]
        dstepped = du[:, cols] + wide_fade * dot(inputs, adj)
        grad_in = grad_in + dot(wide_fade * wide_step * values, adj, NT)
        dti[:, cols] = (wide_step * dstepped + skip * grad) * dsi[:, cols]
        own += head_totals(grad * (y[:, cols] - skip * values), width)
        direct += head_totals(values * dstepped, width)
        part = (grad * values).reshape(CHUNK // PAD, PAD, LANES).sum(axis=0)
        rows[0:PAD, cols] = rows[0:PAD, cols] + part
        leaving[:, cols] = adjoint[0, :, cols] + chdec[0, 0:1, cols] * adj
    dts[:, :n] = grad_in * dss[:, :n]
    dts[:, n:] = dbc[:, n:] * dss[:, n:]
    direct = place_heads(direct, (CHUNK, LANES))
    dcum = place_heads(own, (CHUNK, LANES)) - step * direct
    drate = dot(ones, dcum, precision=HIGHEST) + running[0:1, :]
    running[...] = jnp.broadcast_to(drate[0:1, :], running.shape)
    dstep_value = direct + drate * heads_rate
    raw = sp[:, 2 * n :] + hp[0:1, :]
    grad_raw = dstep_value * sigmoid(raw)
    dstep[...] = grad_raw
    lanes = slice(0, LANES)
    rates = drate * heads_rate * step
    rows[PAD : 2 * PAD, lanes] = rows[PAD : 2 * PAD, lanes] + rates.reshape(
        CHUNK // PAD, PAD, LANES
    ).sum(axis=0)
    rows[2 * PAD : 3 * PAD, lanes] = rows[2 * PAD : 3 * PAD, lanes] + grad_raw.reshape(
        CHUNK // PAD, PAD, LANES
    ).sum(axis=0)


def filter_back_kernel(
    dti, hi, dts, hs, ip, pi, ib, sp, ps, sb, ti, ts, dip, dsp, ri, rs, padi, pads, padgi, padgs
):
    inner = ip.shape[1]
    states = dts.shape[1]
    place = pl.program_id(0)

    @pl.when(place == 0)
    def _():
        padgi[CHUNK:, :] = hi[...]
        padgs[CHUNK:, :] = hs[...]
        ri[...] = jnp.zeros_like(ri)
        rs[...] = jnp.zeros_like(rs)

    @pl.when(place > 0)
    def _():
        padgi[CHUNK:, :] = padgi[0:PAD, :]
        padgs[CHUNK:, :] = padgs[0:PAD, :]

    @pl.when(place == pl.num_programs(0) - 1)
    def _():
        padi[0:PAD, :] = ib[...]
        pads[0:PAD, :] = sb[...]

    @pl.when(place < pl.num_programs(0) - 1)
    def _():
        padi[0:PAD, :] = pi[...]
        pads[0:PAD, :] = ps[:, :states]

    padi[PAD:, :] = ip[...]
    pads[PAD:, :] = sp[:, :states]
    padgi[0:CHUNK, :] = dti[...]
    padgs[0:CHUNK, :] = dts[...]
    rows = 64

    def folded(value):
        return value.reshape(rows // PAD, PAD, LANES).sum(axis=0)

    def step(number, _):
        start = pl.multiple_of(number * rows, rows)
        for signal, grads, taps, out, sums, size in (
            (padi, padgi, ti, dip, ri, inner),
            (pads, padgs, ts, dsp, rs, states),
        ):
            for tile in range(size // LANES):
                cols = slice(tile * LANES, (tile + 1) * LANES)
                ahead = grads[pl.ds(start, rows + PAD), cols]
                grad = ahead[:rows]
                before = signal[pl.ds(start, rows + PAD), cols]
                total = taps[3:4, cols] * grad
                sums[3 * PAD : 4 * PAD, cols] = sums[3 * PAD : 4 * PAD, cols] + folded(grad * before[PAD:])
                sums[4 * PAD : 5 * PAD, cols] = sums[4 * PAD : 5 * PAD, cols] + folded(grad)
                for back in range(1, 4):
                    tap = 3 - back
                    total = total + taps[tap : tap + 1, cols] * pltpu.roll(ahead, rows + PAD - back, 0)[:rows]
                    place = slice(tap * PAD, (tap + 1) * PAD)
                    sums[place, cols] = sums[place, cols] + folded(
                        grad * pltpu.roll(before, back, 0)[PAD:]
                    )
                out[pl.ds(start, rows), cols] = total
        return 0

    lax.fori_loop(0, CHUNK // rows, step, 0)


def matmul(left, right, dims=((1,), (0,)), precision=HIGH):
    return lax.dot_general(left, right, (dims, ((), ())), precision=precision)


def padded_rows(rows, lanes):
    rows = jnp.concatenate(rows, axis=0)
    return jnp.pad(rows, ((0, PAD - rows.shape[0]), (0, lanes - rows.shape[1])))


def forward(current, w, first, taps, beside):
    length = current.shape[0]
    inner = w["inner"].shape[1]
    heads = w["heads"]
    width = inner // heads
    states = w["states"]
    n = states // 2
    chunks = length // CHUNK
    root = lax.rsqrt(jnp.mean(current * current, axis=-1, keepdims=True) + epsilon)
    normed = current * root * w["pre_gain"][None, :]
    if first:
        whole = matmul(normed, w["state"], precision=HIGHEST)
        whole = jnp.concatenate([whole, taps], axis=0)
        ip = matmul(after(normed, whole), w["inner"], precision=HIGHEST)
        if power_of_two(lax.axis_size("head")):
            step = None
            for distance in distances("head"):
                other = exchanged(whole, "head", distance)
                if distance == 1:
                    other, ip = tied(other, ip)
                elif step is None:
                    step = matmul(after(normed, whole), w["own_step"], precision=HIGHEST)
                    other, step = tied(other, step)
                whole = joined(whole, other, "head", distance, 1)
        else:
            whole = gathered_columns(whole)
        if not power_of_two(lax.axis_size("head")) or step is None:
            step = matmul(normed, w["own_step"], precision=HIGHEST)
        step = jnp.pad(step, ((0, 0), (0, LANES - heads)))
        taps = whole[length:]
        sp = whole[:length]
    else:
        ip = matmul(normed, w["inner"])
        sp = matmul(normed, w["maps"], NT, HIGHEST)
    border = shifted(
        jnp.concatenate([ip[length - PAD :], sp[length - PAD :, :states]], axis=1), "seq", 1
    )
    if first:
        sp = jnp.concatenate([sp, step], axis=1)
    ib, sb = border[:, :inner], border[:, inner:]
    taps_s = taps[w["layer"] * PAD : (w["layer"] + 1) * PAD]
    b_inner, b_states, b_lanes = (rows_of(CHUNK, size) for size in (inner, states, LANES))
    b_heads, b_sp = columns_of(16, CHUNK), rows_of(CHUNK, states + LANES)
    b_block, b_state = rows_of(1, n, inner), all_of(n, inner)
    b_decay = rows_of(1, PAD, inner)
    v, bc, dsi, dss, dt, cum, cumt, fresh, local, chdec, decay = call(
        functools.partial(start_kernel, width),
        chunks,
        [
            ((length, inner), b_inner),
            ((length, states), b_states),
            ((length, inner), b_inner),
            ((length, states), b_states),
            ((length, LANES), b_lanes),
            ((length, LANES), b_lanes),
            ((16, length), b_heads),
            ((chunks, n, inner), b_block),
            ((n, inner), b_state),
            ((chunks, PAD, inner), b_decay),
            ((PAD, inner), all_of(PAD, inner)),
        ],
        [pltpu.VMEM((CHUNK + PAD, inner), F32), pltpu.VMEM((CHUNK + PAD, states), F32)],
        2 * 3 * length * n * inner,
        (ip, b_inner),
        (ib, all_of(PAD, inner)),
        (sp, b_sp),
        (sb, all_of(PAD, states)),
        (w["taps_i"], all_of(PAD, inner)),
        (taps_s, all_of(PAD, states)),
        (w["heads_rows"], all_of(PAD, LANES)),
        vmem=LARGE,
    )
    decay = decay[0:1]

    def inside(before, done):
        return call(
            functools.partial(inner_kernel, width),
            chunks,
            [((length, inner), b_inner)],
            [],
            2 * 6 * length * CHUNK * inner,
            (v, b_inner),
            (bc, b_states),
            (dt, b_lanes),
            (cum, b_lanes),
            (cumt, b_heads),
            (w["heads_rows"], all_of(PAD, LANES)),
            vmem=LARGE,
        )

    def aside(before, done):
        gate = matmul(after(normed, before), w["gate"], precision=HIGHEST if first else HIGH)
        return [gate, beside]

    entering, ((yd,), (gate, beside)) = state_before(local, decay, False, [inside, aside])
    y, gn, carried, squares, final = call(
        functools.partial(gate_kernel, width),
        chunks,
        [
            ((length, inner), b_inner),
            ((length, inner), b_inner),
            ((chunks, n, inner), b_block),
            ((PAD, length), columns_of(PAD, CHUNK)),
            ((n, inner), b_state),
        ],
        [],
        2 * 3 * length * n * inner,
        (yd, b_inner),
        (bc, b_states),
        (cum, b_lanes),
        (fresh, b_block),
        (chdec, b_decay),
        (entering, b_state),
        (gate, b_inner),
        (w["norm_gain"][None, :], all_of(1, inner)),
    )
    saved = dict(
        current=current, root=root, normed=normed, ip=ip, sp=sp, ib=ib, sb=sb, gate=gate, v=v, bc=bc,
        dsi=dsi, dss=dss, dt=dt, cum=cum, cumt=cumt, fresh=fresh, chdec=chdec, decay=decay, y=y,
        gn=gn, states=carried, taps_s=taps_s, final=final,
    )
    return gn, squares[0:1], saved, taps, beside


def core_products(left, right):
    place = lax.axis_index("dp")
    if lax.axis_size("dp") != 2:
        total = matmul(left, right, ((0,), (0,)))
        return total, total
    return (
        matmul(left, half(right, 1 - place, 1), ((0,), (0,))),
        matmul(left, half(right, place, 1), ((0,), (0,))),
    )


def over_cores(sent, kept):
    if lax.axis_size("dp") != 2:
        return lax.psum(kept, "dp")
    return kept + exchanged(sent, "dp", 1)


def pair_kernel(one, a, two, b, sent, kept):
    width = a.shape[1] // 2
    first = lax.axis_index("dp") == 0
    for number, (left, right) in enumerate(((one, a), (two, b))):
        product = dot(left[...].T, right[...])
        cols = slice(number * width, (number + 1) * width)
        sent[:, cols] = jnp.where(first, product[:, width:], product[:, :width])
        kept[:, cols] = jnp.where(first, product[:, :width], product[:, width:])


def pair_products(one, a, two, b):
    length, model = one.shape
    inner = a.shape[1]
    tile = 256
    out = ((model, inner), rows_of(tile, inner))
    return call(
        pair_kernel,
        model // tile,
        [out, out],
        [],
        4 * length * model * inner,
        (one, columns_of(length, tile)),
        (a, all_of(length, inner)),
        (two, columns_of(length, tile)),
        (b, all_of(length, inner)),
    )


def last_kernel(left, right, small, sent, kept):
    width = right.shape[1] // 2
    rows = left.shape[1]
    first = lax.axis_index("dp") == 0
    turned = left[...].T
    product = dot(turned, right[...])
    sent[0, :rows, :] = jnp.where(first, product[:, width:], product[:, :width])
    kept[0, :rows, :] = jnp.where(first, product[:, :width], product[:, width:])
    below = dot(small[...].T, left[...])
    size = SMALL // 2
    sent[0, rows:, :] = jnp.where(first, below[size : 2 * size], below[:size])
    kept[0, rows:, :] = jnp.where(first, below[:size], below[size : 2 * size])


def last_products(left, right, small):
    length, model = left.shape
    inner = right.shape[1]
    shards = lax.axis_size("seq")
    rows = model // shards
    out = ((shards, rows + SMALL // 2, inner // 2), rows_of(1, rows + SMALL // 2, inner // 2))
    return call(
        last_kernel,
        shards,
        [out, out],
        [],
        2 * length * model * (inner + LANES),
        (left, columns_of(length, rows)),
        (right, all_of(length, inner)),
        (small, all_of(length, LANES)),
    )


def over_seq(total):
    return lax.psum_scatter(total, "seq", scatter_dimension=0, tiled=True)


def place_kernel(*refs):
    *parts, out = refs
    first = lax.axis_index("dp") == 0
    width = out.shape[2] // 2
    for layer in range(len(parts) // 2):
        mine, other = parts[2 * layer], parts[2 * layer + 1]

        @pl.when(first)
        def _():
            out[layer, :, :width] = mine[...]
            out[layer, :, width:] = other[...]

        @pl.when(jnp.logical_not(first))
        def _():
            out[layer, :, :width] = other[...]
            out[layer, :, width:] = mine[...]


def cores_joined(pairs, start, width, rows):
    if lax.axis_size("dp") != 2:
        return jnp.stack([mine[:rows, start : start + width] for mine, _ in pairs], axis=0)
    pieces = [piece for pair in pairs for piece in pair]
    tile = 96 if rows % 96 == 0 else rows
    return pl.pallas_call(
        place_kernel,
        grid=(rows // tile,),
        out_shape=jax.ShapeDtypeStruct((len(pairs), rows, 2 * width), F32),
        in_specs=[pl.BlockSpec((tile, width), lambda i: (i, start // width))] * len(pieces),
        out_specs=pl.BlockSpec((len(pairs), tile, 2 * width), lambda i: (0, i, 0)),
        compiler_params=pltpu.CompilerParams(vmem_limit_bytes=24 * 1024 * 1024),
        cost_estimate=pl.CostEstimate(flops=0, bytes_accessed=0, transcendentals=0),
    )(*pieces)


def backward(grad, q, scale, slope, w, saved, beside, idle, waiting, earlier, final):
    s = saved
    length, inner = q.shape
    width = inner // w["heads"]
    states = w["states"]
    n = states // 2
    chunks = length // CHUNK
    factors = jnp.pad(jnp.concatenate([scale, slope], axis=0), ((0, PAD - 2), (0, 0)))
    b_inner, b_states, b_lanes = (rows_of(CHUNK, size) for size in (inner, states, LANES))
    b_heads, b_sp = columns_of(16, CHUNK), rows_of(CHUNK, states + LANES)
    b_block, b_state = rows_of(1, n, inner), all_of(n, inner)
    b_decay = rows_of(1, PAD, inner)
    dy, dgate, u, dgain, adjoint, local = call(
        functools.partial(open_kernel, width),
        chunks,
        [
            ((length, inner), b_inner),
            ((length, inner), b_inner),
            ((length, inner), b_inner),
            ((PAD, inner), all_of(PAD, inner)),
            ((chunks, n, inner), b_block),
            ((n, inner), b_state),
        ],
        [pltpu.VMEM((PAD, inner), F32)],
        2 * 3 * length * n * inner,
        (q, b_inner),
        (s["y"], b_inner),
        (s["gate"], b_inner),
        (w["norm_gain"][None, :], all_of(1, inner)),
        (factors, columns_of(PAD, CHUNK)),
        (s["bc"], b_states),
        (s["cum"], b_lanes),
        (s["chdec"], b_decay),
    )

    def cross(before, done):
        if lax.axis_size("dp") == 2:
            result = pair_products(grad, after(u, before), s["normed"], dgate)
        else:
            result = [
                jnp.concatenate(both, axis=1)
                for both in zip(core_products(grad, u), core_products(s["normed"], dgate))
            ]
        if waiting is not None:
            result = (*result, waiting)
        return beside.advance(*result) if beside is not None else result

    def inside(before, done):
        result = call(
            functools.partial(back_kernel, width),
            chunks,
            [((length, inner), b_inner), ((length, states), b_states)],
            [pltpu.VMEM((CHUNK, CHUNK), F32)],
            2 * 15 * length * CHUNK * inner,
            (after(dy, before), b_inner),
            (s["v"], b_inner),
            (s["bc"], b_states),
            (s["dt"], b_lanes),
            (s["cum"], b_lanes),
            (s["cumt"], b_heads),
            (s["states"], b_block),
        )
        return beside.advance(*result) if beside is not None else result

    def summed(before, done):
        result = [over_cores(*done[0][:2])]
        return beside.advance(*result) if beside is not None else result


    later, (_, (du, dbc), (pair, *_)) = state_before(local, s["decay"], True, [cross, inside, summed])
    pair = over_seq(pair)
    dti, dts, dstep, rows = call(
        functools.partial(close_kernel, width),
        chunks,
        [
            ((length, inner), b_inner),
            ((length, states), b_states),
            ((length, LANES), b_lanes),
            ((3 * PAD, inner), all_of(3 * PAD, inner)),
        ],
        [pltpu.VMEM((n, inner), F32), pltpu.VMEM((PAD, LANES), F32)],
        2 * 6 * length * n * inner,
        (dy, b_inner),
        (s["y"], b_inner),
        (s["v"], b_inner),
        (du, b_inner),
        (s["dsi"], b_inner),
        (adjoint, b_block),
        (s["bc"], b_states),
        (s["dt"], b_lanes),
        (s["cum"], b_lanes),
        (s["sp"], b_sp),
        (w["heads_rows"], all_of(PAD, LANES)),
        (dbc, b_states),
        (s["dss"], b_states),
        (s["chdec"], b_decay),
        (s["final"], b_state),
        (later, b_state),
        backward=True,
        vmem=LARGE,
    )
    if beside is not None:
        dti, dts = beside.advance(dti, dts)
    halo = shifted(jnp.concatenate([dti[:PAD], dts[:PAD]], axis=1), "seq", -1)
    base = matmul(after(dgate, dti), w["gate"], NT)
    halo, base = tied(halo, base)
    def edge(size):
        return pl.BlockSpec((PAD, size), lambda c: (jnp.maximum(c * (CHUNK // PAD) - 1, 0), 0))

    dip, dsp, ri, rs = call(
        filter_back_kernel,
        chunks,
        [
            ((length, inner), b_inner),
            ((length, states), b_states),
            ((5 * PAD, inner), all_of(5 * PAD, inner)),
            ((5 * PAD, states), all_of(5 * PAD, states)),
        ],
        [pltpu.VMEM((CHUNK + PAD, size), F32) for size in (inner, states, inner, states)],
        16 * length * inner,
        (dti, b_inner),
        (halo[:, :inner], all_of(PAD, inner)),
        (dts, b_states),
        (halo[:, inner:], all_of(PAD, states)),
        (s["ip"], b_inner),
        (s["ip"], edge(inner)),
        (s["ib"], all_of(PAD, inner)),
        (s["sp"], b_sp),
        (s["sp"], edge(states + LANES)),
        (s["sb"], all_of(PAD, states)),
        (w["taps_i"], all_of(PAD, inner)),
        (s["taps_s"], all_of(PAD, states)),
        backward=True,
    )
    gains = []

    def product(base, dip, dmaps):
        return base + matmul(dip, w["inner"], NT) + matmul(dmaps, w["maps"])

    def finish(rows_grad, offset):
        def take(array):
            return lax.dynamic_slice_in_dim(array, offset, rows_grad.shape[0], 0)

        x, root = take(s["current"]), take(s["root"])
        scaled = rows_grad * w["pre_gain"][None, :]
        along = jnp.mean(scaled * x, axis=-1, keepdims=True)
        gains.append(jnp.sum(rows_grad * x * root, axis=0))
        return root * scaled - x * (root * root * root * along)

    shared = dsp
    own = states // lax.axis_size("head")
    lefts = [base, dip, jnp.concatenate([dsp, dstep], axis=1)]
    if power_of_two(lax.axis_size("head")):
        way = distances("head")[::-1]
        for number, distance in enumerate(way):
            bit = bit_of("head", distance)
            other = exchanged(half(shared, 1 - bit, 1), "head", distance)
            if number == 0:
                steps = Steps(head_sum(lefts, product, finish))
                (other,) = steps.advance(other)
            shared = half(shared, bit, 1) + other
    else:
        shared = lax.psum_scatter(shared, "head", scatter_dimension=1, tiled=True)
        steps = Steps(head_sum(lefts, product, finish))
        steps.advance()
    over, rest = packed(ri, rs, dgain, rows)
    (dip,) = steps.advance(dip)
    shards = lax.axis_size("seq")
    model = s["normed"].shape[1]
    small = jnp.concatenate([shared, dstep[:, : LANES - own]], axis=1)
    if lax.axis_size("dp") == 2 and model // shards % LANES == 0:
        sent, kept = last_products(s["normed"], dip, small)
        if final:
            kept, pair = tied(kept, pair)
        last = over_cores(sent, kept)
    else:
        last = over_cores(*core_products(s["normed"], dip)).reshape(shards, -1, inner // lax.axis_size("dp"))
        small = matmul(small[:, :SMALL], s["normed"], ((0,), (0,)))
        small = jnp.transpose(small.reshape(SMALL, shards, -1), (1, 0, 2))
        if lax.axis_size("dp") == 2:
            place = lax.axis_index("dp")
            small = over_cores(half(small, 1 - place, 1), half(small, place, 1))
        else:
            small = lax.psum(small, "dp")
        small = jnp.pad(small, ((0, 0), (0, 0), (0, last.shape[2] - small.shape[2])))
        last = jnp.concatenate([last, small], axis=1)
    last = last.reshape(-1, last.shape[2])
    if final:
        (last,) = steps.advance(last)
    else:
        last, pair = steps.advance(last, pair)
    last = over_seq(after(last, pair))
    over_heads = jnp.concatenate([sum(gains).reshape(-1, LANES), over], axis=0)
    small_parts = [*earlier, (over_heads, rest)]
    if not final:
        steps.advance()
        if idle is not None:
            (idle.now,) = steps.advance(idle.now)
        branch = steps.finished()
        return grad + branch, pair, last, small_parts, own
    over_heads = small_sum(jnp.concatenate([part[0] for part in small_parts], axis=0), "head")
    steps.advance()
    flat = jnp.concatenate([over_heads] + [part[1] for part in small_parts], axis=0)
    flat = small_sum(small_sum(flat, "dp"), "seq")
    flat, last = tied(flat, last)
    branch = steps.finished()
    sizes = (small_parts[0][0].size, small_parts[0][1].size)
    return grad + branch, pair, last, (flat, sizes), own


def pack_kernel(ri, rs, dgain, rows, over, rest):
    def line(array, number, k):
        part = array[number * PAD : (number + 1) * PAD, k * LANES : (k + 1) * LANES]
        return jnp.sum(part, axis=0, keepdims=True)

    tiles = ri.shape[1] // LANES
    maps = rs.shape[1] // LANES
    for tap in range(5):
        for k in range(tiles):
            rest[tap * tiles + k : tap * tiles + k + 1, :] = line(ri, tap, k)
        for k in range(maps):
            over[tap * maps + k : tap * maps + k + 1, :] = line(rs, tap, k)
    for k in range(tiles):
        rest[5 * tiles + k : 5 * tiles + k + 1, :] = line(dgain, 0, k)
        rest[6 * tiles + k : 6 * tiles + k + 1, :] = line(rows, 0, k)
    for k in range(2):
        rest[7 * tiles + k : 7 * tiles + k + 1, :] = line(rows, 1 + k, 0)


def packed(ri, rs, dgain, rows):
    counts = (5 * rs.shape[1] // LANES, 7 * ri.shape[1] // LANES + 2)
    return pl.pallas_call(
        pack_kernel,
        out_shape=[jax.ShapeDtypeStruct((count, LANES), F32) for count in counts],
        compiler_params=pltpu.CompilerParams(vmem_limit_bytes=VMEM),
        cost_estimate=pl.CostEstimate(flops=0, bytes_accessed=0, transcendentals=0),
    )(ri, rs, dgain, rows)


def unpack_kernel(width, size, flat, pre, fi, fib, fs, fsb, bias, rate, skip, norm):
    layers, model = pre.shape
    inner = norm.shape[1]
    own = fs.shape[2]
    heads = bias.shape[1]
    place = lax.axis_index("head")
    shares = size // LANES - model // LANES
    shares = shares * LANES // 5 // own
    rest = 7 * inner // LANES + 2

    def row(number):
        return flat[number : number + 1, :]

    for layer in range(layers):
        number = layers - 1 - layer
        base = number * size // LANES
        for k in range(model // LANES):
            pre[layer : layer + 1, k * LANES : (k + 1) * LANES] = row(base + k)
        base += model // LANES
        for tap in range(5):
            chosen = None
            for share in range(shares):
                start = (tap * shares + share) * own
                line, lane = divmod(start, LANES)
                piece = row(base + line)[:, lane : lane + own]
                chosen = piece if share == 0 else jnp.where(place == share, piece, chosen)
            if tap < 4:
                fs[layer, tap : tap + 1, :] = chosen
            else:
                fsb[layer : layer + 1, :] = chosen
        base = layers * size // LANES + number * rest
        sums = []
        for k in range(inner // LANES):
            cols = slice(k * LANES, (k + 1) * LANES)
            for tap in range(4):
                fi[layer, tap : tap + 1, cols] = row(base + tap * (inner // LANES) + k)
            fib[layer : layer + 1, cols] = row(base + 4 * (inner // LANES) + k)
            norm[layer : layer + 1, cols] = row(base + 5 * (inner // LANES) + k)
            sums += head_totals(row(base + 6 * (inner // LANES) + k), width)
        skip[layer : layer + 1, :] = place_heads(sums, (1, LANES))[:, :heads]
        rate[layer : layer + 1, :] = row(base + rest - 2)[:, :heads]
        bias[layer : layer + 1, :] = row(base + rest - 1)[:, :heads]


def unpacked(flat, size, layers, model, inner, own, heads):
    shapes = [
        (layers, model),
        (layers, 4, inner),
        (layers, inner),
        (layers, 4, own),
        (layers, own),
        (layers, heads),
        (layers, heads),
        (layers, heads),
        (layers, inner),
    ]
    return pl.pallas_call(
        functools.partial(unpack_kernel, inner // heads, size),
        out_shape=[jax.ShapeDtypeStruct(shape, F32) for shape in shapes],
        compiler_params=pltpu.CompilerParams(vmem_limit_bytes=VMEM),
        cost_estimate=pl.CostEstimate(flops=0, bytes_accessed=0, transcendentals=0),
    )(flat)


def gathered_columns(value):
    if not power_of_two(lax.axis_size("head")):
        return lax.all_gather(value, "head", axis=1, tiled=True)
    return gather_back(value, "head", distances("head")[::-1], 1)


def body(
    tokens,
    cotangent,
    pre_gain,
    gate_weight,
    inner_weight,
    state_weight,
    step_weight,
    filter_inner,
    filter_inner_bias,
    filter_state,
    filter_state_bias,
    step_bias,
    log_rate,
    skip_gain,
    norm_gain,
    out_weight,
):
    layers = pre_gain.shape[0]
    heads = step_bias.shape[1]
    inner = gate_weight.shape[2]
    taps = jnp.concatenate([filter_state, filter_state_bias[:, None, :]], axis=1)
    taps = jnp.pad(taps, ((0, 0), (0, PAD - taps.shape[1]), (0, 0))).reshape(layers * PAD, -1)
    weights = []
    for layer in range(layers):
        steps = jnp.pad(step_weight[layer], ((0, 0), (0, LANES - heads)))
        weights.append(
            dict(
                layer=layer,
                heads=heads,
                states=state_weight.shape[2] * lax.axis_size("head"),
                pre_gain=pre_gain[layer],
                gate=gate_weight[layer],
                inner=inner_weight[layer],
                state=state_weight[layer],
                step=steps,
                own_step=step_weight[layer],
                out=out_weight[layer],
                norm_gain=norm_gain[layer],
                taps_i=padded_rows([filter_inner[layer], filter_inner_bias[layer][None]], inner),
                heads_rows=padded_rows(
                    [step_bias[layer][None], log_rate[layer][None], skip_gain[layer][None]], LANES
                ),
            )
        )
    maps = jnp.concatenate([state_weight[layer].T for layer in range(layers)], axis=1)
    maps = lax.all_gather(maps, "head", axis=0, tiled=True)
    current = tokens[0]
    grad = cotangent[0]
    kept = []
    extra = None
    for layer in range(layers):
        w = weights[layer]
        gn, squares, saved, taps, maps = forward(current, w, layer == 0, taps, maps)
        if layer == 0:
            for number, other in enumerate(weights):
                size = other["inner"].shape[0]
                cut = maps[:, number * size : (number + 1) * size]
                other["maps"] = jnp.concatenate([cut, after(other["step"], gn).T], axis=0)
        last = layer == layers - 1
        if last:
            both = jnp.concatenate([squares, jnp.sum(extra * gn, axis=1)[None, :]], axis=0)
            both = small_sum(both, "head")
            squares, along = both[0:1], both[1:2]
        else:
            squares = small_sum(squares, "head")
        scale = lax.rsqrt(squares / INNER + epsilon)

        def finish(rows, offset, scale=scale):
            return rows * lax.dynamic_slice_in_dim(scale[0], offset, rows.shape[0], 0)[:, None]

        steps = Steps(head_sum([gn], lambda rows, w=w, p=HIGH if last else HIGHEST: matmul(rows, w["out"], NT, p), finish))
        if layer == 0:
            product = matmul(after(grad, steps.now), weights[layers - 1]["out"])
            if not last:
                steps.advance()
                (product,) = steps.advance(product)
            extra = product
        branch = None if last else steps.finished()
        kept.append((saved, scale, branch))
        if not last:
            current = current + branch
    collected = [None] * layers
    waiting = None
    earlier = []
    for layer in reversed(range(layers)):
        w = weights[layer]
        saved, scale, branch = kept[layer]
        if layer < layers - 1:
            if layer == layers - 2:
                (grad,) = steps.advance(grad)
            q = matmul(grad, w["out"])
            slope = jnp.sum(grad * branch, axis=1)[None, :] * scale * scale / INNER
        else:
            q = extra
            slope = along * scale * scale * scale / INNER
        grad, *collected[layer] = backward(
            grad,
            q,
            scale,
            slope,
            w,
            saved,
            steps if layer == layers - 2 else None,
            steps if layer == layers - 1 else None,
            waiting,
            earlier,
            layer == 0,
        )
        waiting = collected[layer][1]
        earlier = collected[layer][2]
    current = current + steps.finished()
    flat, (size, _) = earlier
    own = collected[0][3]
    stacked = unpacked(flat, size, layers, gate_weight.shape[1], inner, own, heads)
    two = lax.axis_size("dp") == 2

    def with_other(part):
        return part, exchanged(part, "dp", 1) if two else part

    pairs = [[with_other(entry[0]) for entry in collected]]
    half_width = inner // 2 if two else inner
    rows = gate_weight.shape[1] // lax.axis_size("seq")
    large = {
        "out": cores_joined(pairs[0], 0, half_width, rows),
        "gate": cores_joined(pairs[0], half_width, half_width, rows),
    }
    collected[0][1], current, large = tied(collected[0][1], current, large)
    pairs.append([with_other(entry[1]) for entry in collected])
    large["inner"] = cores_joined(pairs[1], 0, half_width, rows)
    small = []
    for mine, other in pairs[1]:
        mine, other = mine[rows:, :rows], other[rows:, :rows]
        if two:
            mine = jnp.concatenate(
                [jnp.where(lax.axis_index("dp") == 0, a, b) for a, b in ((mine, other), (other, mine))],
                axis=0,
            )
        small.append(mine.T)
    small = jnp.stack(small, axis=0)
    return (
        current[None],
        grad[None],
        stacked[0],
        large["gate"],
        large["inner"],
        small[:, :, :own],
        small[:, :, own : own + heads],
        *stacked[1:],
        large["out"],
    )


def solution(mesh):
    placed = (
        P("dp", "seq", None),
        P("dp", "seq", None),
        P(),
        P(None, None, "head"),
        P(None, None, "head"),
        P(None, None, "head"),
        P(None, None, "head"),
        P(None, None, "head"),
        P(None, "head"),
        P(None, None, "head"),
        P(None, "head"),
        P(None, "head"),
        P(None, "head"),
        P(None, "head"),
        P(None, "head"),
        P(None, None, "head"),
    )
    return jax.shard_map(
        body,
        mesh=mesh,
        in_specs=placed,
        out_specs=(
            P("dp", "seq", None),
            P("dp", "seq", None),
            P(),
            P(None, "seq", "head"),
            P(None, "seq", "head"),
            P(None, "seq", "head"),
            P(None, "seq", "head"),
            P(None, None, "head"),
            P(None, "head"),
            P(None, None, "head"),
            P(None, "head"),
            P(None, "head"),
            P(None, "head"),
            P(None, "head"),
            P(None, "head"),
            P(None, "seq", "head"),
        ),
        check_vma=False,
    )
```

```python
import functools

import jax
import jax.numpy as jnp
from jax import lax
from jax.experimental import pallas as pl
from jax.experimental.pallas import tpu as pltpu
from jax.sharding import PartitionSpec as P

INNER = 3072
CHUNK = 128
LANES = 128
PAD = 8
SMALL = 96
COST = 4
VMEM = 20 * 1024 * 1024
LARGE = 56 * 1024 * 1024
epsilon = 1e-05
HIGH = lax.Precision.HIGH
HIGHEST = lax.Precision.HIGHEST
NEG = -1e30
F32 = jnp.float32


def power_of_two(n):
    return n & (n - 1) == 0


def exchanged(value, axis, distance):
    n = lax.axis_size(axis)
    return lax.ppermute(value, axis, [(i, i ^ distance) for i in range(n)])


def shifted(value, axis, step):
    n = lax.axis_size(axis)
    pairs = [(i, i + step) for i in range(n) if 0 <= i + step < n]
    return lax.ppermute(value, axis, pairs)


def distances(axis):
    n = lax.axis_size(axis)
    return [1 << k for k in range(n.bit_length() - 1)]


def bit_of(axis, distance):
    return (lax.axis_index(axis) // distance) % 2


def small_sum(value, axis):
    if not power_of_two(lax.axis_size(axis)):
        return lax.psum(value, axis)
    for distance in distances(axis):
        value = value + exchanged(value, axis, distance)
    return value


def half(value, which, dim=0):
    size = value.shape[dim] // 2
    return lax.dynamic_slice_in_dim(value, which * size, size, dim)


def joined(mine, other, axis, distance, dim=0):
    first = bit_of(axis, distance) == 0
    return jnp.concatenate(
        [jnp.where(first, mine, other), jnp.where(first, other, mine)], axis=dim
    )


def gather_back(value, axis, order, dim=0):
    for distance in order[::-1]:
        value = joined(value, exchanged(value, axis, distance), axis, distance, dim)
    return value


def tied(value, *others):
    return lax.optimization_barrier((value, *others))


def head_sum(lefts, product, finish):
    order = distances("head")
    rows = lefts[0].shape[0] // 2
    ways = (order, order[::-1])

    def chosen(other):
        picked = []
        for array in lefts:
            pieces = []
            for number, way in enumerate(ways):
                bit = bit_of("head", way[0])
                part = array[number * rows : (number + 1) * rows]
                pieces.append(half(part, 1 - bit if other else bit))
            picked.append(jnp.concatenate(pieces, axis=0))
        return product(*picked)

    sent = chosen(True)
    kept = chosen(False)
    sent, kept = yield sent, kept
    size = rows // 2
    got = [
        exchanged(sent[number * size : (number + 1) * size], "head", way[0])
        for number, way in enumerate(ways)
    ]
    kept = [kept[:size], kept[size:]]
    offsets = [bit_of("head", way[0]) * size + number * rows for number, way in enumerate(ways)]
    got, kept = yield got, kept
    for step in range(1, len(order)):
        bits = [bit_of("head", way[step]) for way in ways]
        sends = [half(k, 1 - bit) + half(g, 1 - bit) for k, g, bit in zip(kept, got, bits)]
        arrived = [exchanged(send, "head", way[step]) for send, way in zip(sends, ways)]
        kept = [half(k, bit) + half(g, bit) for k, g, bit in zip(kept, got, bits)]
        offsets = [o + bit * k.shape[0] for o, bit, k in zip(offsets, bits, kept)]
        got, kept = yield arrived, kept
    mine = [finish(k + g, o) for k, g, o in zip(kept, got, offsets)]
    for step in range(len(order) - 1, -1, -1):
        others = [exchanged(m, "head", way[step]) for m, way in zip(mine, ways)]
        others, mine = yield others, mine
        mine = [joined(m, o, "head", way[step]) for m, o, way in zip(mine, others, ways)]
    return jnp.concatenate(mine, axis=0)


class Steps:
    def __init__(self, steps):
        self.steps = steps
        self.now = next(steps)
        self.result = None

    def advance(self, *others):
        if self.result is not None:
            return others
        if len(others) > 0:
            self.now, *others = tied(self.now, *others)
        try:
            self.now = self.steps.send(self.now)
        except StopIteration as end:
            self.result = end.value
        return others

    def finished(self):
        while self.result is None:
            self.advance()
        return self.result


def after(value, *others):
    return tied(value, *others)[0]


def state_before(local, decay, reverse, windows):
    n = lax.axis_size("seq")
    done = []
    arrived = []
    before = local
    for hop in range(n - 1):
        source, target = (n - 1 - hop, n - 2 - hop) if reverse else (hop, hop + 1)
        leaving = local if hop == 0 else decay * before + local
        got = lax.ppermute(leaving, "seq", [(source, target)])
        if hop < len(windows):
            got, *result = tied(got, *windows[hop](before, done))
            done.append(result)
        before = got
        arrived.append(got)
    for window in windows[n - 1 :]:
        done.append(window(before, done))
    return sum(arrived) if len(arrived) > 0 else jnp.zeros_like(local), done


def rows_of(*shape):
    return pl.BlockSpec(shape, lambda c: (c,) + (0,) * (len(shape) - 1))


def columns_of(*shape):
    return pl.BlockSpec(shape, lambda c: (0, c))


def all_of(*shape):
    return pl.BlockSpec(shape, lambda c: (0,) * len(shape))


def reverse(spec, steps):
    index = spec.index_map
    return pl.BlockSpec(spec.block_shape, lambda c: index(steps - 1 - c))


def call(kernel, steps, outs, scratch, flops, *args, backward=False, vmem=VMEM):
    shapes = [jax.ShapeDtypeStruct(shape, F32) for shape, _ in outs]
    size = 4 * sum(a.size for a, _ in args) + 4 * sum(s.size for s in shapes)

    def spec(blocks):
        return reverse(blocks, steps) if backward else blocks

    return pl.pallas_call(
        kernel,
        grid=(steps,),
        out_shape=shapes,
        in_specs=[spec(blocks) for _, blocks in args],
        out_specs=[spec(blocks) for _, blocks in outs],
        scratch_shapes=scratch,
        compiler_params=pltpu.CompilerParams(vmem_limit_bytes=vmem),
        cost_estimate=pl.CostEstimate(flops=flops // COST, bytes_accessed=size // COST, transcendentals=0),
    )(*[a for a, _ in args])


def dot(left, right, dims=((1,), (0,)), precision=HIGH):
    return lax.dot_general(
        left, right, (dims, ((), ())), precision=precision, preferred_element_type=F32
    )


NT = ((1,), (1,))


def sigmoid(value):
    return 1.0 / (1.0 + jnp.exp(-value))


def spread_heads(columns, tile, width):
    each = LANES // width
    lane = lax.broadcasted_iota(jnp.int32, (columns.shape[0], LANES), 1)
    result = columns[:, tile * each : tile * each + 1]
    for k in range(1, each):
        result = jnp.where(lane < k * width, result, columns[:, tile * each + k : tile * each + k + 1])
    return jnp.broadcast_to(result, (columns.shape[0], LANES))


def head_rows(row, width, total):
    tiles = [spread_heads(row, tile, width) for tile in range(total // LANES)]
    return jnp.concatenate(tiles, axis=1)


def filter_tile(scratch, taps, start, rows, cols):
    block = scratch[pl.ds(start, rows + PAD), cols]
    total = taps[4:5, cols] + taps[3:4, cols] * block[PAD:]
    for back in range(1, 4):
        total = total + taps[3 - back : 4 - back, cols] * pltpu.roll(block, back, 0)[PAD:]
    return total


def start_kernel(
    width, ip, ib, sp, sb, ti, ts, hp, v_out, bc_out, dsi, dss, dt_out, cum_out, cumt_out, fresh, local, chdec, passed, padi, pads
):
    inner = ip.shape[1]
    states = ts.shape[1]
    n = states // 2
    c = pl.program_id(0)

    @pl.when(c == 0)
    def _():
        padi[0:PAD, :] = ib[...]
        pads[0:PAD, :] = sb[...]
        passed[...] = jnp.ones_like(passed)
        local[...] = jnp.zeros_like(local)

    @pl.when(c > 0)
    def _():
        padi[0:PAD, :] = padi[CHUNK:, :]
        pads[0:PAD, :] = pads[CHUNK:, :]

    padi[PAD:, :] = ip[...]
    pads[PAD:, :] = sp[:, :states]
    rows = 64

    def filtered(step, _):
        start = pl.multiple_of(step * rows, rows)
        for scratch, taps, out, slope, size in (
            (padi, ti, v_out, dsi, inner),
            (pads, ts, bc_out, dss, states),
        ):
            for tile in range(size // LANES):
                cols = slice(tile * LANES, (tile + 1) * LANES)
                total = filter_tile(scratch, taps, start, rows, cols)
                gate = sigmoid(total)
                value = total * gate
                out[pl.ds(start, rows), cols] = value
                slope[pl.ds(start, rows), cols] = gate + value * (1.0 - gate)
        return 0

    lax.fori_loop(0, CHUNK // rows, filtered, 0)
    raw = sp[:, states:] + hp[0:1, :]
    dt = jnp.maximum(raw, 0.0) + jnp.log1p(jnp.exp(-jnp.abs(raw)))
    dt_out[...] = dt
    rate = -jnp.exp(hp[1:2, :]) * dt
    ones = (
        lax.broadcasted_iota(jnp.int32, (CHUNK, CHUNK), 0)
        >= lax.broadcasted_iota(jnp.int32, (CHUNK, CHUNK), 1)
    ).astype(F32)
    cum = dot(ones, rate, precision=HIGHEST)
    cum_out[...] = cum
    cumt_out[...] = cum.T[: cumt_out.shape[0]]
    last = cum[CHUNK - 1 : CHUNK, :]
    weight = jnp.exp(last - cum) * dt
    maps = bc_out[:, :n].T
    decay = head_rows(jnp.exp(last), width, inner)
    chdec[0] = jnp.broadcast_to(decay, (PAD, inner))
    passed[...] = passed[...] * decay
    for tile in range(inner // LANES):
        cols = slice(tile * LANES, (tile + 1) * LANES)
        weighted = v_out[:, cols] * spread_heads(weight, tile, width)
        part = dot(maps, weighted, precision=HIGHEST)
        fresh[0, :, cols] = part
        local[:, cols] = decay[:, cols] * local[:, cols] + part


def inner_kernel(width, v, bc, dt, cum, cumt, hp, out):
    inner = v.shape[1]
    n = bc.shape[1] // 2
    each = LANES // width
    lane = lax.broadcasted_iota(jnp.int32, (CHUNK, LANES), 1)
    lower = lax.broadcasted_iota(jnp.int32, (CHUNK, CHUNK), 0) >= lax.broadcasted_iota(
        jnp.int32, (CHUNK, CHUNK), 1
    )
    meet = dot(bc[:, n:], bc[:, :n], NT, HIGHEST)
    for tile in range(inner // LANES):
        cols = slice(tile * LANES, (tile + 1) * LANES)
        values = v[:, cols]
        stepped = values * spread_heads(dt[...], tile, width)
        result = None
        for k in range(each):
            head = tile * each + k
            spread = cum[:, head : head + 1] - cumt[head : head + 1, :]
            mixing = jnp.exp(jnp.where(lower, spread, NEG)) * meet
            part = dot(mixing, stepped, precision=HIGHEST)
            result = part if k == 0 else jnp.where(lane < k * width, result, part)
        out[:, cols] = result + spread_heads(hp[2:3, :], tile, width) * values


def gate_kernel(width, yd, bc, cum, fresh, chdec, entering, gate, gain, y_out, gn_out, states, squares, final):
    inner = yd.shape[1]
    n = bc.shape[1] // 2
    ones = jnp.ones((PAD, LANES), F32)
    c = pl.program_id(0)

    @pl.when(c == 0)
    def _():
        final[...] = entering[...]

    carried = jnp.exp(cum[...])
    maps = bc[:, n:]
    total = None
    for tile in range(inner // LANES):
        cols = slice(tile * LANES, (tile + 1) * LANES)
        state = final[:, cols]
        states[0, :, cols] = state
        final[:, cols] = chdec[0, 0:1, cols] * state + fresh[0, :, cols]
        y = yd[:, cols] + spread_heads(carried, tile, width) * dot(maps, state, precision=HIGHEST)
        y_out[:, cols] = y
        g = gate[:, cols]
        gated = y * (g * sigmoid(g))
        gn_out[:, cols] = gated * gain[0:1, cols]
        total = gated * gated if tile == 0 else total + gated * gated
    squares[...] = dot(ones, total, NT, HIGHEST)


def open_kernel(
    width, q, y, gate, gain, factors, bc, cum, chdec, dy_out, dgate, u_out, dgain, adjoint, local, passed
):
    inner = q.shape[1]
    n = bc.shape[1] // 2
    c = pl.program_id(0)

    @pl.when(c == 0)
    def _():
        dgain[...] = jnp.zeros_like(dgain)
        local[...] = jnp.zeros_like(local)
        passed[...] = jnp.ones_like(passed)

    carried = jnp.exp(cum[...])
    maps = bc[:, n:].T
    turned = factors[...].T
    s = turned[:, 0:1]
    t = turned[:, 1:2]
    for tile in range(inner // LANES):
        cols = slice(tile * LANES, (tile + 1) * LANES)
        g = gate[:, cols]
        soft = sigmoid(g)
        silu = g * soft
        out = y[:, cols]
        gated = out * silu
        grad = q[:, cols]
        scaled = gated * s
        u_out[:, cols] = scaled * gain[0:1, cols]
        dgain[:, cols] = dgain[:, cols] + (grad * scaled).reshape(CHUNK // PAD, PAD, LANES).sum(axis=0)
        dgated = s * (grad * gain[0:1, cols]) - t * gated
        dgate[:, cols] = dgated * out * (soft + silu * (1.0 - soft))
        dy = dgated * silu
        dy_out[:, cols] = dy
        part = dot(maps, dy * spread_heads(carried, tile, width))
        adjoint[0, :, cols] = part
        local[:, cols] = local[:, cols] + passed[0:1, cols] * part
    passed[...] = passed[...] * chdec[0]


def back_kernel(width, dy, v, bc, dt, cum, cumt, states, du, dbc, gram):
    inner = v.shape[1]
    n = bc.shape[1] // 2
    each = LANES // width
    lane = lax.broadcasted_iota(jnp.int32, (CHUNK, LANES), 1)
    upper = lax.broadcasted_iota(jnp.int32, (CHUNK, CHUNK), 0) <= lax.broadcasted_iota(
        jnp.int32, (CHUNK, CHUNK), 1
    )
    inputs, outputs = bc[:, :n], bc[:, n:]
    meet = dot(inputs, outputs, NT)
    carried = jnp.exp(cum[...])
    grad_out = None
    for tile in range(inner // LANES):
        cols = slice(tile * LANES, (tile + 1) * LANES)
        grad = dy[:, cols]
        stepped = v[:, cols] * spread_heads(dt[...], tile, width)
        result = None
        for k in range(each):
            head = tile * each + k
            spread = cumt[head : head + 1, :] - cum[:, head : head + 1]
            decay = jnp.exp(jnp.where(upper, spread, NEG))
            part = dot(decay * meet, grad)
            result = part if k == 0 else jnp.where(lane < k * width, result, part)
            own = (lane >= k * width) & (lane < (k + 1) * width)
            cross = decay * dot(jnp.where(own, stepped, 0.0), grad, NT)
            first = tile == 0 and k == 0
            gram[...] = cross if first else gram[...] + cross
        du[:, cols] = result
        part = dot(grad * spread_heads(carried, tile, width), states[0, :, cols], NT)
        grad_out = part if tile == 0 else grad_out + part
    total = gram[...]
    dbc[:, :n] = dot(total, outputs)
    dbc[:, n:] = grad_out + dot(total.T, inputs)


def head_totals(product, width):
    each = LANES // width
    lane = lax.broadcasted_iota(jnp.int32, product.shape, 1)
    result = []
    for k in range(each):
        own = (lane >= k * width) & (lane < (k + 1) * width)
        result.append(jnp.sum(jnp.where(own, product, 0.0), axis=1, keepdims=True))
    return result


def place_heads(columns, shape):
    lane = lax.broadcasted_iota(jnp.int32, shape, 1)
    result = jnp.zeros(shape, F32)
    for head, column in enumerate(columns):
        result = jnp.where(lane == head, column, result)
    return result


def close_kernel(
    width, dy, y, v, du, dsi, adjoint, bc, dt, cum, sp, hp, dbc, dss, chdec, final, later,
    dti, dts, dstep, rows, leaving, running,
):
    inner = v.shape[1]
    n = bc.shape[1] // 2
    heads_rate = -jnp.exp(hp[1:2, :])

    @pl.when(pl.program_id(0) == 0)
    def _():
        crossing = jnp.sum(final[...] * later[...], axis=0, keepdims=True)
        columns = []
        for tile in range(inner // LANES):
            columns += head_totals(crossing[:, tile * LANES : (tile + 1) * LANES], width)
        running[...] = jnp.broadcast_to(place_heads(columns, (1, LANES)), running.shape)
        leaving[...] = later[...]
        rows[...] = jnp.zeros_like(rows)

    ones = (
        lax.broadcasted_iota(jnp.int32, (CHUNK, CHUNK), 0)
        <= lax.broadcasted_iota(jnp.int32, (CHUNK, CHUNK), 1)
    ).astype(F32)
    step = dt[...]
    cums = cum[...]
    fade = jnp.exp(cums[CHUNK - 1 : CHUNK, :] - cums)
    inputs = bc[:, :n]
    grad_in = dbc[:, :n]
    own, direct = [], []
    for tile in range(inner // LANES):
        cols = slice(tile * LANES, (tile + 1) * LANES)
        adj = leaving[:, cols]
        wide_fade = spread_heads(fade, tile, width)
        wide_step = spread_heads(step, tile, width)
        skip = spread_heads(hp[2:3, :], tile, width)
        values = v[:, cols]
        grad = dy[:, cols]
        dstepped = du[:, cols] + wide_fade * dot(inputs, adj)
        grad_in = grad_in + dot(wide_fade * wide_step * values, adj, NT)
        dti[:, cols] = (wide_step * dstepped + skip * grad) * dsi[:, cols]
        own += head_totals(grad * (y[:, cols] - skip * values), width)
        direct += head_totals(values * dstepped, width)
        part = (grad * values).reshape(CHUNK // PAD, PAD, LANES).sum(axis=0)
        rows[0:PAD, cols] = rows[0:PAD, cols] + part
        leaving[:, cols] = adjoint[0, :, cols] + chdec[0, 0:1, cols] * adj
    dts[:, :n] = grad_in * dss[:, :n]
    dts[:, n:] = dbc[:, n:] * dss[:, n:]
    direct = place_heads(direct, (CHUNK, LANES))
    dcum = place_heads(own, (CHUNK, LANES)) - step * direct
    drate = dot(ones, dcum, precision=HIGHEST) + running[0:1, :]
    running[...] = jnp.broadcast_to(drate[0:1, :], running.shape)
    dstep_value = direct + drate * heads_rate
    raw = sp[:, 2 * n :] + hp[0:1, :]
    grad_raw = dstep_value * sigmoid(raw)
    dstep[...] = grad_raw
    lanes = slice(0, LANES)
    rates = drate * heads_rate * step
    rows[PAD : 2 * PAD, lanes] = rows[PAD : 2 * PAD, lanes] + rates.reshape(
        CHUNK // PAD, PAD, LANES
    ).sum(axis=0)
    rows[2 * PAD : 3 * PAD, lanes] = rows[2 * PAD : 3 * PAD, lanes] + grad_raw.reshape(
        CHUNK // PAD, PAD, LANES
    ).sum(axis=0)


def filter_back_kernel(
    dti, hi, dts, hs, ip, pi, ib, sp, ps, sb, ti, ts, dip, dsp, ri, rs, padi, pads, padgi, padgs
):
    inner = ip.shape[1]
    states = dts.shape[1]
    place = pl.program_id(0)

    @pl.when(place == 0)
    def _():
        padgi[CHUNK:, :] = hi[...]
        padgs[CHUNK:, :] = hs[...]
        ri[...] = jnp.zeros_like(ri)
        rs[...] = jnp.zeros_like(rs)

    @pl.when(place > 0)
    def _():
        padgi[CHUNK:, :] = padgi[0:PAD, :]
        padgs[CHUNK:, :] = padgs[0:PAD, :]

    @pl.when(place == pl.num_programs(0) - 1)
    def _():
        padi[0:PAD, :] = ib[...]
        pads[0:PAD, :] = sb[...]

    @pl.when(place < pl.num_programs(0) - 1)
    def _():
        padi[0:PAD, :] = pi[...]
        pads[0:PAD, :] = ps[:, :states]

    padi[PAD:, :] = ip[...]
    pads[PAD:, :] = sp[:, :states]
    padgi[0:CHUNK, :] = dti[...]
    padgs[0:CHUNK, :] = dts[...]
    rows = 64

    def folded(value):
        return value.reshape(rows // PAD, PAD, LANES).sum(axis=0)

    def step(number, _):
        start = pl.multiple_of(number * rows, rows)
        for signal, grads, taps, out, sums, size in (
            (padi, padgi, ti, dip, ri, inner),
            (pads, padgs, ts, dsp, rs, states),
        ):
            for tile in range(size // LANES):
                cols = slice(tile * LANES, (tile + 1) * LANES)
                ahead = grads[pl.ds(start, rows + PAD), cols]
                grad = ahead[:rows]
                before = signal[pl.ds(start, rows + PAD), cols]
                total = taps[3:4, cols] * grad
                sums[3 * PAD : 4 * PAD, cols] = sums[3 * PAD : 4 * PAD, cols] + folded(grad * before[PAD:])
                sums[4 * PAD : 5 * PAD, cols] = sums[4 * PAD : 5 * PAD, cols] + folded(grad)
                for back in range(1, 4):
                    tap = 3 - back
                    total = total + taps[tap : tap + 1, cols] * pltpu.roll(ahead, rows + PAD - back, 0)[:rows]
                    place = slice(tap * PAD, (tap + 1) * PAD)
                    sums[place, cols] = sums[place, cols] + folded(
                        grad * pltpu.roll(before, back, 0)[PAD:]
                    )
                out[pl.ds(start, rows), cols] = total
        return 0

    lax.fori_loop(0, CHUNK // rows, step, 0)


def matmul(left, right, dims=((1,), (0,)), precision=HIGH):
    return lax.dot_general(left, right, (dims, ((), ())), precision=precision)


def padded_rows(rows, lanes):
    rows = jnp.concatenate(rows, axis=0)
    return jnp.pad(rows, ((0, PAD - rows.shape[0]), (0, lanes - rows.shape[1])))


def forward(current, w, first, taps, beside):
    length = current.shape[0]
    inner = w["inner"].shape[1]
    heads = w["heads"]
    width = inner // heads
    states = w["states"]
    n = states // 2
    chunks = length // CHUNK
    root = lax.rsqrt(jnp.mean(current * current, axis=-1, keepdims=True) + epsilon)
    normed = current * root * w["pre_gain"][None, :]
    if first:
        whole = matmul(normed, w["state"], precision=HIGHEST)
        whole = jnp.concatenate([whole, taps], axis=0)
        ip = matmul(after(normed, whole), w["inner"], precision=HIGHEST)
        if power_of_two(lax.axis_size("head")):
            step = None
            for distance in distances("head"):
                other = exchanged(whole, "head", distance)
                if distance == 1:
                    other, ip = tied(other, ip)
                elif step is None:
                    step = matmul(after(normed, whole), w["own_step"], precision=HIGHEST)
                    other, step = tied(other, step)
                whole = joined(whole, other, "head", distance, 1)
        else:
            whole = gathered_columns(whole)
        if not power_of_two(lax.axis_size("head")) or step is None:
            step = matmul(normed, w["own_step"], precision=HIGHEST)
        step = jnp.pad(step, ((0, 0), (0, LANES - heads)))
        taps = whole[length:]
        sp = whole[:length]
    else:
        ip = matmul(normed, w["inner"])
        sp = matmul(normed, w["maps"], NT, HIGHEST)
    border = shifted(
        jnp.concatenate([ip[length - PAD :], sp[length - PAD :, :states]], axis=1), "seq", 1
    )
    if first:
        sp = jnp.concatenate([sp, step], axis=1)
    ib, sb = border[:, :inner], border[:, inner:]
    taps_s = taps[w["layer"] * PAD : (w["layer"] + 1) * PAD]
    b_inner, b_states, b_lanes = (rows_of(CHUNK, size) for size in (inner, states, LANES))
    b_heads, b_sp = columns_of(16, CHUNK), rows_of(CHUNK, states + LANES)
    b_block, b_state = rows_of(1, n, inner), all_of(n, inner)
    b_decay = rows_of(1, PAD, inner)
    v, bc, dsi, dss, dt, cum, cumt, fresh, local, chdec, decay = call(
        functools.partial(start_kernel, width),
        chunks,
        [
            ((length, inner), b_inner),
            ((length, states), b_states),
            ((length, inner), b_inner),
            ((length, states), b_states),
            ((length, LANES), b_lanes),
            ((length, LANES), b_lanes),
            ((16, length), b_heads),
            ((chunks, n, inner), b_block),
            ((n, inner), b_state),
            ((chunks, PAD, inner), b_decay),
            ((PAD, inner), all_of(PAD, inner)),
        ],
        [pltpu.VMEM((CHUNK + PAD, inner), F32), pltpu.VMEM((CHUNK + PAD, states), F32)],
        2 * 3 * length * n * inner,
        (ip, b_inner),
        (ib, all_of(PAD, inner)),
        (sp, b_sp),
        (sb, all_of(PAD, states)),
        (w["taps_i"], all_of(PAD, inner)),
        (taps_s, all_of(PAD, states)),
        (w["heads_rows"], all_of(PAD, LANES)),
        vmem=LARGE,
    )
    decay = decay[0:1]

    def inside(before, done):
        return call(
            functools.partial(inner_kernel, width),
            chunks,
            [((length, inner), b_inner)],
            [],
            2 * 6 * length * CHUNK * inner,
            (v, b_inner),
            (bc, b_states),
            (dt, b_lanes),
            (cum, b_lanes),
            (cumt, b_heads),
            (w["heads_rows"], all_of(PAD, LANES)),
            vmem=LARGE,
        )

    def aside(before, done):
        gate = matmul(after(normed, before), w["gate"], precision=HIGHEST if first else HIGH)
        return [gate, beside]

    entering, ((yd,), (gate, beside)) = state_before(local, decay, False, [inside, aside])
    y, gn, carried, squares, final = call(
        functools.partial(gate_kernel, width),
        chunks,
        [
            ((length, inner), b_inner),
            ((length, inner), b_inner),
            ((chunks, n, inner), b_block),
            ((PAD, length), columns_of(PAD, CHUNK)),
            ((n, inner), b_state),
        ],
        [],
        2 * 3 * length * n * inner,
        (yd, b_inner),
        (bc, b_states),
        (cum, b_lanes),
        (fresh, b_block),
        (chdec, b_decay),
        (entering, b_state),
        (gate, b_inner),
        (w["norm_gain"][None, :], all_of(1, inner)),
    )
    saved = dict(
        current=current, root=root, normed=normed, ip=ip, sp=sp, ib=ib, sb=sb, gate=gate, v=v, bc=bc,
        dsi=dsi, dss=dss, dt=dt, cum=cum, cumt=cumt, fresh=fresh, chdec=chdec, decay=decay, y=y,
        gn=gn, states=carried, taps_s=taps_s, final=final,
    )
    return gn, squares[0:1], saved, taps, beside


def core_products(left, right):
    place = lax.axis_index("dp")
    if lax.axis_size("dp") != 2:
        total = matmul(left, right, ((0,), (0,)))
        return total, total
    return (
        matmul(left, half(right, 1 - place, 1), ((0,), (0,))),
        matmul(left, half(right, place, 1), ((0,), (0,))),
    )


def over_cores(sent, kept):
    if lax.axis_size("dp") != 2:
        return lax.psum(kept, "dp")
    return kept + exchanged(sent, "dp", 1)


def pair_kernel(one, a, two, b, sent, kept):
    width = a.shape[1] // 2
    first = lax.axis_index("dp") == 0
    for number, (left, right) in enumerate(((one, a), (two, b))):
        product = dot(left[...].T, right[...])
        cols = slice(number * width, (number + 1) * width)
        sent[:, cols] = jnp.where(first, product[:, width:], product[:, :width])
        kept[:, cols] = jnp.where(first, product[:, :width], product[:, width:])


def pair_products(one, a, two, b):
    length, model = one.shape
    inner = a.shape[1]
    tile = 256
    out = ((model, inner), rows_of(tile, inner))
    return call(
        pair_kernel,
        model // tile,
        [out, out],
        [],
        4 * length * model * inner,
        (one, columns_of(length, tile)),
        (a, all_of(length, inner)),
        (two, columns_of(length, tile)),
        (b, all_of(length, inner)),
    )


def last_kernel(left, right, small, sent, kept):
    width = right.shape[1] // 2
    rows = left.shape[1]
    first = lax.axis_index("dp") == 0
    turned = left[...].T
    product = dot(turned, right[...])
    sent[0, :rows, :] = jnp.where(first, product[:, width:], product[:, :width])
    kept[0, :rows, :] = jnp.where(first, product[:, :width], product[:, width:])
    below = dot(small[...].T, left[...])
    size = SMALL // 2
    sent[0, rows:, :] = jnp.where(first, below[size : 2 * size], below[:size])
    kept[0, rows:, :] = jnp.where(first, below[:size], below[size : 2 * size])


def last_products(left, right, small):
    length, model = left.shape
    inner = right.shape[1]
    shards = lax.axis_size("seq")
    rows = model // shards
    out = ((shards, rows + SMALL // 2, inner // 2), rows_of(1, rows + SMALL // 2, inner // 2))
    return call(
        last_kernel,
        shards,
        [out, out],
        [],
        2 * length * model * (inner + LANES),
        (left, columns_of(length, rows)),
        (right, all_of(length, inner)),
        (small, all_of(length, LANES)),
    )


def over_seq(total):
    return lax.psum_scatter(total, "seq", scatter_dimension=0, tiled=True)


def place_kernel(*refs):
    *parts, out = refs
    first = lax.axis_index("dp") == 0
    width = out.shape[2] // 2
    for layer in range(len(parts) // 2):
        mine, other = parts[2 * layer], parts[2 * layer + 1]

        @pl.when(first)
        def _():
            out[layer, :, :width] = mine[...]
            out[layer, :, width:] = other[...]

        @pl.when(jnp.logical_not(first))
        def _():
            out[layer, :, :width] = other[...]
            out[layer, :, width:] = mine[...]


def cores_joined(pairs, start, width, rows):
    if lax.axis_size("dp") != 2:
        return jnp.stack([mine[:rows, start : start + width] for mine, _ in pairs], axis=0)
    pieces = [piece for pair in pairs for piece in pair]
    tile = 96 if rows % 96 == 0 else rows
    return pl.pallas_call(
        place_kernel,
        grid=(rows // tile,),
        out_shape=jax.ShapeDtypeStruct((len(pairs), rows, 2 * width), F32),
        in_specs=[pl.BlockSpec((tile, width), lambda i: (i, start // width))] * len(pieces),
        out_specs=pl.BlockSpec((len(pairs), tile, 2 * width), lambda i: (0, i, 0)),
        compiler_params=pltpu.CompilerParams(vmem_limit_bytes=24 * 1024 * 1024),
        cost_estimate=pl.CostEstimate(flops=0, bytes_accessed=0, transcendentals=0),
    )(*pieces)


def backward(grad, q, scale, slope, w, saved, beside, idle, waiting, earlier, final):
    s = saved
    length, inner = q.shape
    width = inner // w["heads"]
    states = w["states"]
    n = states // 2
    chunks = length // CHUNK
    factors = jnp.pad(jnp.concatenate([scale, slope], axis=0), ((0, PAD - 2), (0, 0)))
    b_inner, b_states, b_lanes = (rows_of(CHUNK, size) for size in (inner, states, LANES))
    b_heads, b_sp = columns_of(16, CHUNK), rows_of(CHUNK, states + LANES)
    b_block, b_state = rows_of(1, n, inner), all_of(n, inner)
    b_decay = rows_of(1, PAD, inner)
    dy, dgate, u, dgain, adjoint, local = call(
        functools.partial(open_kernel, width),
        chunks,
        [
            ((length, inner), b_inner),
            ((length, inner), b_inner),
            ((length, inner), b_inner),
            ((PAD, inner), all_of(PAD, inner)),
            ((chunks, n, inner), b_block),
            ((n, inner), b_state),
        ],
        [pltpu.VMEM((PAD, inner), F32)],
        2 * 3 * length * n * inner,
        (q, b_inner),
        (s["y"], b_inner),
        (s["gate"], b_inner),
        (w["norm_gain"][None, :], all_of(1, inner)),
        (factors, columns_of(PAD, CHUNK)),
        (s["bc"], b_states),
        (s["cum"], b_lanes),
        (s["chdec"], b_decay),
    )

    def cross(before, done):
        if lax.axis_size("dp") == 2:
            result = pair_products(grad, after(u, before), s["normed"], dgate)
        else:
            result = [
                jnp.concatenate(both, axis=1)
                for both in zip(core_products(grad, u), core_products(s["normed"], dgate))
            ]
        if waiting is not None:
            result = (*result, waiting)
        return beside.advance(*result) if beside is not None else result

    def inside(before, done):
        result = call(
            functools.partial(back_kernel, width),
            chunks,
            [((length, inner), b_inner), ((length, states), b_states)],
            [pltpu.VMEM((CHUNK, CHUNK), F32)],
            2 * 15 * length * CHUNK * inner,
            (after(dy, before), b_inner),
            (s["v"], b_inner),
            (s["bc"], b_states),
            (s["dt"], b_lanes),
            (s["cum"], b_lanes),
            (s["cumt"], b_heads),
            (s["states"], b_block),
        )
        return beside.advance(*result) if beside is not None else result

    def summed(before, done):
        result = [over_cores(*done[0][:2])]
        return beside.advance(*result) if beside is not None else result


    later, (_, (du, dbc), (pair, *_)) = state_before(local, s["decay"], True, [cross, inside, summed])
    pair = over_seq(pair)
    dti, dts, dstep, rows = call(
        functools.partial(close_kernel, width),
        chunks,
        [
            ((length, inner), b_inner),
            ((length, states), b_states),
            ((length, LANES), b_lanes),
            ((3 * PAD, inner), all_of(3 * PAD, inner)),
        ],
        [pltpu.VMEM((n, inner), F32), pltpu.VMEM((PAD, LANES), F32)],
        2 * 6 * length * n * inner,
        (dy, b_inner),
        (s["y"], b_inner),
        (s["v"], b_inner),
        (du, b_inner),
        (s["dsi"], b_inner),
        (adjoint, b_block),
        (s["bc"], b_states),
        (s["dt"], b_lanes),
        (s["cum"], b_lanes),
        (s["sp"], b_sp),
        (w["heads_rows"], all_of(PAD, LANES)),
        (dbc, b_states),
        (s["dss"], b_states),
        (s["chdec"], b_decay),
        (s["final"], b_state),
        (later, b_state),
        backward=True,
        vmem=LARGE,
    )
    if beside is not None:
        dti, dts = beside.advance(dti, dts)
    halo = shifted(jnp.concatenate([dti[:PAD], dts[:PAD]], axis=1), "seq", -1)
    base = matmul(after(dgate, dti), w["gate"], NT)
    halo, base = tied(halo, base)
    def edge(size):
        return pl.BlockSpec((PAD, size), lambda c: (jnp.maximum(c * (CHUNK // PAD) - 1, 0), 0))

    dip, dsp, ri, rs = call(
        filter_back_kernel,
        chunks,
        [
            ((length, inner), b_inner),
            ((length, states), b_states),
            ((5 * PAD, inner), all_of(5 * PAD, inner)),
            ((5 * PAD, states), all_of(5 * PAD, states)),
        ],
        [pltpu.VMEM((CHUNK + PAD, size), F32) for size in (inner, states, inner, states)],
        16 * length * inner,
        (dti, b_inner),
        (halo[:, :inner], all_of(PAD, inner)),
        (dts, b_states),
        (halo[:, inner:], all_of(PAD, states)),
        (s["ip"], b_inner),
        (s["ip"], edge(inner)),
        (s["ib"], all_of(PAD, inner)),
        (s["sp"], b_sp),
        (s["sp"], edge(states + LANES)),
        (s["sb"], all_of(PAD, states)),
        (w["taps_i"], all_of(PAD, inner)),
        (s["taps_s"], all_of(PAD, states)),
        backward=True,
    )
    gains = []

    def product(base, dip, dmaps):
        return base + matmul(dip, w["inner"], NT) + matmul(dmaps, w["maps"])

    def finish(rows_grad, offset):
        def take(array):
            return lax.dynamic_slice_in_dim(array, offset, rows_grad.shape[0], 0)

        x, root = take(s["current"]), take(s["root"])
        scaled = rows_grad * w["pre_gain"][None, :]
        along = jnp.mean(scaled * x, axis=-1, keepdims=True)
        gains.append(jnp.sum(rows_grad * x * root, axis=0))
        return root * scaled - x * (root * root * root * along)

    shared = dsp
    own = states // lax.axis_size("head")
    lefts = [base, dip, jnp.concatenate([dsp, dstep], axis=1)]
    if power_of_two(lax.axis_size("head")):
        way = distances("head")[::-1]
        for number, distance in enumerate(way):
            bit = bit_of("head", distance)
            other = exchanged(half(shared, 1 - bit, 1), "head", distance)
            if number == 0:
                steps = Steps(head_sum(lefts, product, finish))
                (other,) = steps.advance(other)
            shared = half(shared, bit, 1) + other
    else:
        shared = lax.psum_scatter(shared, "head", scatter_dimension=1, tiled=True)
        steps = Steps(head_sum(lefts, product, finish))
        steps.advance()
    over, rest = packed(ri, rs, dgain, rows)
    (dip,) = steps.advance(dip)
    shards = lax.axis_size("seq")
    model = s["normed"].shape[1]
    small = jnp.concatenate([shared, dstep[:, : LANES - own]], axis=1)
    if lax.axis_size("dp") == 2 and model // shards % LANES == 0:
        sent, kept = last_products(s["normed"], dip, small)
        if final:
            kept, pair = tied(kept, pair)
        last = over_cores(sent, kept)
    else:
        last = over_cores(*core_products(s["normed"], dip)).reshape(shards, -1, inner // lax.axis_size("dp"))
        small = matmul(small[:, :SMALL], s["normed"], ((0,), (0,)))
        small = jnp.transpose(small.reshape(SMALL, shards, -1), (1, 0, 2))
        if lax.axis_size("dp") == 2:
            place = lax.axis_index("dp")
            small = over_cores(half(small, 1 - place, 1), half(small, place, 1))
        else:
            small = lax.psum(small, "dp")
        small = jnp.pad(small, ((0, 0), (0, 0), (0, last.shape[2] - small.shape[2])))
        last = jnp.concatenate([last, small], axis=1)
    last = last.reshape(-1, last.shape[2])
    if final:
        steps.advance()
    else:
        last, pair = steps.advance(last, pair)
    last = over_seq(after(last, pair))
    over_heads = jnp.concatenate([sum(gains).reshape(-1, LANES), over], axis=0)
    small_parts = [*earlier, (over_heads, rest)]
    if not final:
        steps.advance()
        if idle is not None:
            (idle.now,) = steps.advance(idle.now)
        branch = steps.finished()
        return grad + branch, pair, last, small_parts, own
    over_heads = small_sum(jnp.concatenate([part[0] for part in small_parts], axis=0), "head")
    steps.advance()
    flat = jnp.concatenate([over_heads] + [part[1] for part in small_parts], axis=0)
    flat = small_sum(small_sum(flat, "dp"), "seq")
    flat, last = tied(flat, last)
    branch = steps.finished()
    sizes = (small_parts[0][0].size, small_parts[0][1].size)
    return grad + branch, pair, last, (flat, sizes), own


def pack_kernel(ri, rs, dgain, rows, over, rest):
    def line(array, number, k):
        part = array[number * PAD : (number + 1) * PAD, k * LANES : (k + 1) * LANES]
        return jnp.sum(part, axis=0, keepdims=True)

    tiles = ri.shape[1] // LANES
    maps = rs.shape[1] // LANES
    for tap in range(5):
        for k in range(tiles):
            rest[tap * tiles + k : tap * tiles + k + 1, :] = line(ri, tap, k)
        for k in range(maps):
            over[tap * maps + k : tap * maps + k + 1, :] = line(rs, tap, k)
    for k in range(tiles):
        rest[5 * tiles + k : 5 * tiles + k + 1, :] = line(dgain, 0, k)
        rest[6 * tiles + k : 6 * tiles + k + 1, :] = line(rows, 0, k)
    for k in range(2):
        rest[7 * tiles + k : 7 * tiles + k + 1, :] = line(rows, 1 + k, 0)


def packed(ri, rs, dgain, rows):
    counts = (5 * rs.shape[1] // LANES, 7 * ri.shape[1] // LANES + 2)
    return pl.pallas_call(
        pack_kernel,
        out_shape=[jax.ShapeDtypeStruct((count, LANES), F32) for count in counts],
        compiler_params=pltpu.CompilerParams(vmem_limit_bytes=VMEM),
        cost_estimate=pl.CostEstimate(flops=0, bytes_accessed=0, transcendentals=0),
    )(ri, rs, dgain, rows)


def unpack_kernel(width, size, flat, pre, fi, fib, fs, fsb, bias, rate, skip, norm):
    layers, model = pre.shape
    inner = norm.shape[1]
    own = fs.shape[2]
    heads = bias.shape[1]
    place = lax.axis_index("head")
    shares = size // LANES - model // LANES
    shares = shares * LANES // 5 // own
    rest = 7 * inner // LANES + 2

    def row(number):
        return flat[number : number + 1, :]

    for layer in range(layers):
        number = layers - 1 - layer
        base = number * size // LANES
        for k in range(model // LANES):
            pre[layer : layer + 1, k * LANES : (k + 1) * LANES] = row(base + k)
        base += model // LANES
        for tap in range(5):
            chosen = None
            for share in range(shares):
                start = (tap * shares + share) * own
                line, lane = divmod(start, LANES)
                piece = row(base + line)[:, lane : lane + own]
                chosen = piece if share == 0 else jnp.where(place == share, piece, chosen)
            if tap < 4:
                fs[layer, tap : tap + 1, :] = chosen
            else:
                fsb[layer : layer + 1, :] = chosen
        base = layers * size // LANES + number * rest
        sums = []
        for k in range(inner // LANES):
            cols = slice(k * LANES, (k + 1) * LANES)
            for tap in range(4):
                fi[layer, tap : tap + 1, cols] = row(base + tap * (inner // LANES) + k)
            fib[layer : layer + 1, cols] = row(base + 4 * (inner // LANES) + k)
            norm[layer : layer + 1, cols] = row(base + 5 * (inner // LANES) + k)
            sums += head_totals(row(base + 6 * (inner // LANES) + k), width)
        skip[layer : layer + 1, :] = place_heads(sums, (1, LANES))[:, :heads]
        rate[layer : layer + 1, :] = row(base + rest - 2)[:, :heads]
        bias[layer : layer + 1, :] = row(base + rest - 1)[:, :heads]


def unpacked(flat, size, layers, model, inner, own, heads):
    shapes = [
        (layers, model),
        (layers, 4, inner),
        (layers, inner),
        (layers, 4, own),
        (layers, own),
        (layers, heads),
        (layers, heads),
        (layers, heads),
        (layers, inner),
    ]
    return pl.pallas_call(
        functools.partial(unpack_kernel, inner // heads, size),
        out_shape=[jax.ShapeDtypeStruct(shape, F32) for shape in shapes],
        compiler_params=pltpu.CompilerParams(vmem_limit_bytes=VMEM),
        cost_estimate=pl.CostEstimate(flops=0, bytes_accessed=0, transcendentals=0),
    )(flat)


def gathered_columns(value):
    if not power_of_two(lax.axis_size("head")):
        return lax.all_gather(value, "head", axis=1, tiled=True)
    return gather_back(value, "head", distances("head")[::-1], 1)


def body(
    tokens,
    cotangent,
    pre_gain,
    gate_weight,
    inner_weight,
    state_weight,
    step_weight,
    filter_inner,
    filter_inner_bias,
    filter_state,
    filter_state_bias,
    step_bias,
    log_rate,
    skip_gain,
    norm_gain,
    out_weight,
):
    layers = pre_gain.shape[0]
    heads = step_bias.shape[1]
    inner = gate_weight.shape[2]
    taps = jnp.concatenate([filter_state, filter_state_bias[:, None, :]], axis=1)
    taps = jnp.pad(taps, ((0, 0), (0, PAD - taps.shape[1]), (0, 0))).reshape(layers * PAD, -1)
    weights = []
    for layer in range(layers):
        steps = jnp.pad(step_weight[layer], ((0, 0), (0, LANES - heads)))
        weights.append(
            dict(
                layer=layer,
                heads=heads,
                states=state_weight.shape[2] * lax.axis_size("head"),
                pre_gain=pre_gain[layer],
                gate=gate_weight[layer],
                inner=inner_weight[layer],
                state=state_weight[layer],
                step=steps,
                own_step=step_weight[layer],
                out=out_weight[layer],
                norm_gain=norm_gain[layer],
                taps_i=padded_rows([filter_inner[layer], filter_inner_bias[layer][None]], inner),
                heads_rows=padded_rows(
                    [step_bias[layer][None], log_rate[layer][None], skip_gain[layer][None]], LANES
                ),
            )
        )
    maps = jnp.concatenate([state_weight[layer].T for layer in range(layers)], axis=1)
    maps = lax.all_gather(maps, "head", axis=0, tiled=True)
    current = tokens[0]
    grad = cotangent[0]
    kept = []
    extra = None
    for layer in range(layers):
        w = weights[layer]
        gn, squares, saved, taps, maps = forward(current, w, layer == 0, taps, maps)
        if layer == 0:
            for number, other in enumerate(weights):
                size = other["inner"].shape[0]
                cut = maps[:, number * size : (number + 1) * size]
                other["maps"] = jnp.concatenate([cut, after(other["step"], gn).T], axis=0)
        last = layer == layers - 1
        if last:
            both = jnp.concatenate([squares, jnp.sum(extra * gn, axis=1)[None, :]], axis=0)
            both = small_sum(both, "head")
            squares, along = both[0:1], both[1:2]
        else:
            squares = small_sum(squares, "head")
        scale = lax.rsqrt(squares / INNER + epsilon)

        def finish(rows, offset, scale=scale):
            return rows * lax.dynamic_slice_in_dim(scale[0], offset, rows.shape[0], 0)[:, None]

        steps = Steps(head_sum([gn], lambda rows, w=w, p=HIGH if last else HIGHEST: matmul(rows, w["out"], NT, p), finish))
        if layer == 0:
            product = matmul(after(grad, steps.now), weights[layers - 1]["out"])
            if not last:
                steps.advance()
                (product,) = steps.advance(product)
            extra = product
        branch = None if last else steps.finished()
        kept.append((saved, scale, branch))
        if not last:
            current = current + branch
    collected = [None] * layers
    waiting = None
    earlier = []
    for layer in reversed(range(layers)):
        w = weights[layer]
        saved, scale, branch = kept[layer]
        if layer < layers - 1:
            if layer == layers - 2:
                (grad,) = steps.advance(grad)
            q = matmul(grad, w["out"])
            slope = jnp.sum(grad * branch, axis=1)[None, :] * scale * scale / INNER
        else:
            q = extra
            slope = along * scale * scale * scale / INNER
        grad, *collected[layer] = backward(
            grad,
            q,
            scale,
            slope,
            w,
            saved,
            steps if layer == layers - 2 else None,
            steps if layer == layers - 1 else None,
            waiting,
            earlier,
            layer == 0,
        )
        waiting = collected[layer][1]
        earlier = collected[layer][2]
    current = current + steps.finished()
    flat, (size, _) = earlier
    own = collected[0][3]
    stacked = unpacked(flat, size, layers, gate_weight.shape[1], inner, own, heads)
    two = lax.axis_size("dp") == 2

    def with_other(part):
        return part, exchanged(part, "dp", 1) if two else part

    pairs = [[with_other(entry[0]) for entry in collected]]
    half_width = inner // 2 if two else inner
    rows = gate_weight.shape[1] // lax.axis_size("seq")
    large = {
        "out": cores_joined(pairs[0], 0, half_width, rows),
        "gate": cores_joined(pairs[0], half_width, half_width, rows),
    }
    collected[0][1], current, large = tied(collected[0][1], current, large)
    pairs.append([with_other(entry[1]) for entry in collected])
    large["inner"] = cores_joined(pairs[1], 0, half_width, rows)
    small = []
    for mine, other in pairs[1]:
        mine, other = mine[rows:, :rows], other[rows:, :rows]
        if two:
            mine = jnp.concatenate(
                [jnp.where(lax.axis_index("dp") == 0, a, b) for a, b in ((mine, other), (other, mine))],
                axis=0,
            )
        small.append(mine.T)
    small = jnp.stack(small, axis=0)
    return (
        current[None],
        grad[None],
        stacked[0],
        large["gate"],
        large["inner"],
        small[:, :, :own],
        small[:, :, own : own + heads],
        *stacked[1:],
        large["out"],
    )


def solution(mesh):
    placed = (
        P("dp", "seq", None),
        P("dp", "seq", None),
        P(),
        P(None, None, "head"),
        P(None, None, "head"),
        P(None, None, "head"),
        P(None, None, "head"),
        P(None, None, "head"),
        P(None, "head"),
        P(None, None, "head"),
        P(None, "head"),
        P(None, "head"),
        P(None, "head"),
        P(None, "head"),
        P(None, "head"),
        P(None, None, "head"),
    )
    return jax.shard_map(
        body,
        mesh=mesh,
        in_specs=placed,
        out_specs=(
            P("dp", "seq", None),
            P("dp", "seq", None),
            P(),
            P(None, "seq", "head"),
            P(None, "seq", "head"),
            P(None, "seq", "head"),
            P(None, "seq", "head"),
            P(None, None, "head"),
            P(None, "head"),
            P(None, None, "head"),
            P(None, "head"),
            P(None, "head"),
            P(None, "head"),
            P(None, "head"),
            P(None, "head"),
            P(None, "seq", "head"),
        ),
        check_vma=False,
    )
```
